32 devices in a mesh: dp: 2 (over x), blk: 16 (over z, y, core).
Axes of the slice: x: 2, y: 2, z: 4, core: 2. Of those that a mesh axis runs over, the one named last changes fastest.
Arguments:
- dec_in: bfloat16 [2, 2048, 1024], P('dp', 'blk'), may hold values from -6 to 6
- enc_out: bfloat16 [2, 2048, 1024], P('dp', 'blk'), may hold values from -6 to 6
- cotangent: bfloat16 [2, 2048, 1024], P('dp', 'blk'), may hold values from -6 to 6
- dec_seg: int32 [2, 2048], P('dp', 'blk'), may hold values from 0 to 2, as said below
- dec_valid: int32 [2, 2048], P('dp', 'blk'), may hold values from 0 to 1, as said below
- enc_seg: int32 [2, 2048], P('dp', 'blk'), may hold values from 0 to 2, as said below
- enc_valid: int32 [2, 2048], P('dp', 'blk'), may hold values from 0 to 1, as said below
- self_gain: bfloat16 [1024], P('blk'), may hold values from 0.5 to 1.5
- self_query: bfloat16 [1024, 1024], P('blk'), may hold values from -0.1875 to 0.1875
- self_key: bfloat16 [1024, 1024], P('blk'), may hold values from -0.1875 to 0.1875
- self_value: bfloat16 [1024, 1024], P('blk'), may hold values from -0.1875 to 0.1875
- self_out: bfloat16 [1024, 1024], P('blk'), may hold values from -0.75 to 0.75
- cross_gain: bfloat16 [1024], P('blk'), may hold values from 0.5 to 1.5
- cross_query: bfloat16 [1024, 1024], P('blk'), may hold values from -0.1875 to 0.1875
- cross_key: bfloat16 [1024, 1024], P('blk'), may hold values from -0.1875 to 0.1875
- cross_value: bfloat16 [1024, 1024], P('blk'), may hold values from -0.1875 to 0.1875
- cross_out: bfloat16 [1024, 1024], P('blk'), may hold values from -1 to 1
- feed_gain: bfloat16 [1024], P('blk'), may hold values from 0.5 to 1.5
- feed_gate: bfloat16 [1024, 2816], P('blk'), may hold values from -0.1875 to 0.1875
- feed_up: bfloat16 [1024, 2816], P('blk'), may hold values from -0.1875 to 0.1875
- feed_down: bfloat16 [2816, 1024], P('blk'), may hold values from -0.109375 to 0.109375
Outputs:
- mixed: bfloat16 [2, 2048, 1024], P('dp', 'blk')
- dec_grad: float32 [2, 2048, 1024], P('dp', 'blk')
- enc_grad: float32 [2, 2048, 1024], P('dp', 'blk')
- self_gain_grad: float32 [1024], P('blk')
- self_query_grad: float32 [1024, 1024], P('blk')
- self_key_grad: float32 [1024, 1024], P('blk')
- self_value_grad: float32 [1024, 1024], P('blk')
- self_out_grad: float32 [1024, 1024], P('blk')
- cross_gain_grad: float32 [1024], P('blk')
- cross_query_grad: float32 [1024, 1024], P('blk')
- cross_key_grad: float32 [1024, 1024], P('blk')
- cross_value_grad: float32 [1024, 1024], P('blk')
- cross_out_grad: float32 [1024, 1024], P('blk')
- feed_gain_grad: float32 [1024], P('blk')
- feed_gate_grad: float32 [1024, 2816], P('blk')
- feed_up_grad: float32 [1024, 2816], P('blk')
- feed_down_grad: float32 [2816, 1024], P('blk')
The draws below stay inside these ranges and needn't reach their ends.
Inputs may be any that keep to these rules, and one draw needn't show every extreme that they name: `dec_seg`: in each row the ids are 0, 1 and 2, never falling, each present; id 1 begins within the first 128 positions and id 2 begins within the last 128 positions. `dec_valid`: in each row a leading run of 1 and then 0 (at least one 0); every position of ids 0 and 1 and the first position of id 2 hold 1. `enc_seg`: in each row the ids are 0, 1 and 2, never falling, each present; id 1 begins within the first 128 positions and id 2 begins within the last 128 positions. `enc_valid`: in each row a leading run of 1 and then 0 (at least one 0); every position of ids 0 and 1 and the first position of id 2 hold 1.
All inputs are finite; a program needn't handle non-finite values.
Results may differ from the reference program's by a relative error of at most 0.03.
Values may be sent and summed in bfloat16 or wider, within the bound.
A program may use at most 256 MiB of HBM per device.

```python
import jax
import jax.numpy as jnp
from jax import lax

D = 1024
HEADS = 16
HEAD_DIM = 64
FF = 2816
TOK_BLK = 128
SEQ = 2048
ROWS = 2


def layout(key, salt):
    key = jax.random.fold_in(key, salt)
    first_key, second_key, third_key = jax.random.split(key, 3)
    first = jax.random.randint(first_key, (ROWS, 1), 1, TOK_BLK)
    second = jax.random.randint(second_key, (ROWS, 1), SEQ - TOK_BLK + 1, SEQ - 1)
    spare = jax.random.randint(third_key, (ROWS, 1), 0, 1 << 20)
    ending = second + 1 + spare % (SEQ - 1 - second)
    places = jnp.arange(SEQ, dtype=jnp.int32)[None, :]
    segment = (places >= first).astype(jnp.int32) + (places >= second).astype(jnp.int32)
    valid = (places < ending).astype(jnp.int32)
    return (segment, valid)


def draw_dec_seg(key, part):
    segment, valid = layout(key, 17)
    return segment


def draw_dec_valid(key, part):
    segment, valid = layout(key, 17)
    return valid


def draw_enc_seg(key, part):
    segment, valid = layout(key, 29)
    return segment


def draw_enc_valid(key, part):
    segment, valid = layout(key, 29)
    return valid


def level_of(stream_key, dims, pieces, least, top_value):
    factor_of, own = 1.0, jax.random.fold_in(stream_key, 6)
    for dim, parts in pieces:
        draws = jnp.exp(jax.random.uniform(jax.random.fold_in(own, dim), (parts,), jnp.float32, least / len(pieces), top_value / len(pieces)))
        factor_of = factor_of * jnp.repeat(draws, dims[dim] // parts).reshape([-1 if axis == dim else 1 for axis in range(len(dims))])
    return factor_of


def gaussian(own_key, dims, width, bound, pieces=(), kind=jnp.bfloat16):
    values = jax.random.normal(own_key, dims, jnp.float32) * width
    if len(pieces) > 0:
        values = level_of(own_key, dims, pieces, -0.22, 0.18) * values
    return jnp.clip(values, min=-bound, max=bound).astype(kind)


def setup_inputs(seed: int = 0) -> dict:
    arg_keys = jax.random.split(jax.random.key(seed), 22)
    dec_in = gaussian(arg_keys[0], (ROWS, SEQ, D), 1.0, 6.0, ((0, 2), (1, 16)))
    enc_out = gaussian(arg_keys[1], (ROWS, SEQ, D), 1.0, 6.0, ((0, 2), (1, 16)))
    cotangent = gaussian(arg_keys[2], (ROWS, SEQ, D), 1.0, 6.0, ((0, 2), (1, 16)))
    dec_seg = draw_dec_seg(jax.random.fold_in(arg_keys[21], 71), 0)
    dec_valid = draw_dec_valid(jax.random.fold_in(arg_keys[21], 71), 0)
    enc_seg = draw_enc_seg(jax.random.fold_in(arg_keys[21], 71), 0)
    enc_valid = draw_enc_valid(jax.random.fold_in(arg_keys[21], 71), 0)
    self_gain = jnp.clip(1.0 + 0.1 * jax.random.normal(arg_keys[7], (D,), jnp.float32), 0.5, 1.5).astype(jnp.bfloat16)
    self_query = gaussian(arg_keys[8], (D, D), D ** -0.5, 0.1875, ((0, 16),))
    self_key = gaussian(arg_keys[9], (D, D), D ** -0.5, 0.1875, ((0, 16),))
    self_value = gaussian(arg_keys[10], (D, D), D ** -0.5, 0.1875, ((0, 16),))
    self_out = gaussian(arg_keys[11], (D, D), (max(D // 16, 1)) ** -0.5, 0.75, ((0, 16),))
    cross_gain = jnp.clip(1.0 + 0.1 * jax.random.normal(arg_keys[12], (D,), jnp.float32), 0.5, 1.5).astype(jnp.bfloat16)
    cross_query = gaussian(arg_keys[13], (D, D), D ** -0.5, 0.1875, ((0, 16),))
    cross_key = gaussian(arg_keys[14], (D, D), D ** -0.5, 0.1875, ((0, 16),))
    cross_value = gaussian(arg_keys[15], (D, D), D ** -0.5, 0.1875, ((0, 16),))
    cross_out = gaussian(arg_keys[16], (D, D), (max(D // 32, 1)) ** -0.5, 1.0, ((0, 16),))
    feed_gain = jnp.clip(1.0 + 0.1 * jax.random.normal(arg_keys[17], (D,), jnp.float32), 0.5, 1.5).astype(jnp.bfloat16)
    feed_gate = gaussian(arg_keys[18], (D, FF), D ** -0.5, 0.1875, ((0, 16),))
    feed_up = gaussian(arg_keys[19], (D, FF), D ** -0.5, 0.1875, ((0, 16),))
    feed_down = gaussian(arg_keys[20], (FF, D), FF ** -0.5, 0.109375, ((0, 16),))
    return dict(dec_in=dec_in, enc_out=enc_out, cotangent=cotangent, dec_seg=dec_seg, dec_valid=dec_valid, enc_seg=enc_seg, enc_valid=enc_valid, self_gain=self_gain, self_query=self_query, self_key=self_key, self_value=self_value, self_out=self_out, cross_gain=cross_gain, cross_query=cross_query, cross_key=cross_key, cross_value=cross_value, cross_out=cross_out, feed_gain=feed_gain, feed_gate=feed_gate, feed_up=feed_up, feed_down=feed_down)


@jax.custom_vjp
def low(v):
    return lax.optimization_barrier(v.astype(jnp.bfloat16)).astype(jnp.float32)

@jax.custom_vjp
def low_back(v):
    return v

def low_keep(v):
    return (low(v), None)

def low_pass(kept, grad):
    return (grad,)

def back_keep(v):
    return (v, None)

def back_low(kept, grad):
    return (low(grad),)
low.defvjp(low_keep, low_pass)
low_back.defvjp(back_keep, back_low)

def rms_norm(values, gain):
    return values * lax.rsqrt(lax.optimization_barrier(jnp.mean(values * values, axis=-1, keepdims=True)) + 1e-06) * gain

def matmul(left, right):
    return jnp.dot(left, right, precision=lax.Precision.HIGHEST)

def attention(queries, keys, values, query_seg, key_seg, causal):
    length = queries.shape[0]
    size = min(512, length)
    blocks = length // size
    query_heads = queries.reshape(blocks, size, HEADS, HEAD_DIM)
    query_segs = query_seg.reshape(blocks, size)
    places = jnp.arange(length, dtype=jnp.int32).reshape(blocks, size)
    key_heads = keys.reshape(keys.shape[0], HEADS, HEAD_DIM)
    value_heads = values.reshape(values.shape[0], HEADS, HEAD_DIM)
    key_pos = jnp.arange(keys.shape[0], dtype=jnp.int32)

    def one_block(item):
        block, segment, place = item
        scores = jnp.einsum('qhe,khe->hqk', block, key_heads, precision=lax.Precision.HIGHEST) * HEAD_DIM ** (-0.5)
        scores = low_back(scores)
        keep = segment[:, None] == key_seg[None, :]
        if causal:
            keep = keep & (key_pos[None, :] <= place[:, None])
        scores = jnp.where(keep[None], scores, -1e+30)
        top = lax.optimization_barrier(jnp.max(scores, axis=-1, keepdims=True))
        weights = jnp.exp(scores - top)
        probs = low(weights / lax.optimization_barrier(jnp.sum(weights, axis=-1, keepdims=True)))
        return jnp.einsum('hqk,khe->qhe', probs, value_heads, precision=lax.Precision.HIGHEST)
    output = lax.map(jax.checkpoint(one_block), (query_heads, query_segs, places))
    return output.reshape(length, HEADS * HEAD_DIM)

def layer_row(params, tokens, encoded, seg_dec, valid_dec, seg_enc, valid_enc):
    self_gain, self_query, self_key, self_value, self_out, cross_gain, cross_query, cross_key, cross_value, cross_out, feed_gain, feed_gate, feed_up, feed_down = params
    self_keys = jnp.where(valid_dec == 1, seg_dec, -1)
    cross_keys = jnp.where(valid_enc == 1, seg_enc, -1)
    normed_one = low(rms_norm(tokens, self_gain))
    query_one = low(low_back(matmul(normed_one, self_query)))
    key_one = low(low_back(matmul(normed_one, self_key)))
    value_one = low(low_back(matmul(normed_one, self_value)))
    attn_one = low(low_back(attention(query_one, key_one, value_one, seg_dec, self_keys, True)))
    resid_one = tokens + low_back(matmul(attn_one, self_out))
    normed_two = low(rms_norm(resid_one, cross_gain))
    query_two = low(low_back(matmul(normed_two, cross_query)))
    key_two = low(low_back(matmul(encoded, cross_key)))
    value_two = low(low_back(matmul(encoded, cross_value)))
    attn_two = low(low_back(attention(query_two, key_two, value_two, seg_dec, cross_keys, False)))
    resid_two = resid_one + low_back(matmul(attn_two, cross_out))
    normed_three = low(rms_norm(resid_two, feed_gain))
    gate = low_back(matmul(normed_three, feed_gate))
    upward = low_back(matmul(normed_three, feed_up))
    hidden = low(jax.nn.gelu(gate, approximate=True) * upward)
    return resid_two + low_back(matmul(hidden, feed_down))

def reference(dec_in, enc_out, cotangent, dec_seg, dec_valid, enc_seg, enc_valid, self_gain, self_query, self_key, self_value, self_out, cross_gain, cross_query, cross_key, cross_value, cross_out, feed_gain, feed_gate, feed_up, feed_down):
    weights = tuple((item.astype(jnp.float32) for item in (self_gain, self_query, self_key, self_value, self_out, cross_gain, cross_query, cross_key, cross_value, cross_out, feed_gain, feed_gate, feed_up, feed_down)))

    def one_row(summed, row):
        tokens, encoded, upstream, seg_dec, valid_dec, seg_enc, valid_enc = row

        def forward(params, inputs, context):
            return layer_row(params, inputs, context, seg_dec, valid_dec, seg_enc, valid_enc)
        output, pull = jax.vjp(forward, weights, tokens.astype(jnp.float32), encoded.astype(jnp.float32))
        grad_params, grad_tokens, grad_encoded = pull(upstream.astype(jnp.float32) * valid_dec[:, None].astype(jnp.float32))
        summed = jax.tree.map(lambda left, right: left + right, summed, grad_params)
        return (summed, (output.astype(jnp.bfloat16), grad_tokens, grad_encoded))
    start = jax.tree.map(jnp.zeros_like, weights)
    totals, outputs = lax.scan(one_row, start, (dec_in, enc_out, cotangent, dec_seg, dec_valid, enc_seg, enc_valid))
    mixed, dec_grad, enc_grad = outputs
    return (mixed, dec_grad, enc_grad, totals[0], totals[1], totals[2], totals[3], totals[4], totals[5], totals[6], totals[7], totals[8], totals[9], totals[10], totals[11], totals[12], totals[13])
```

```python
import functools

import jax
import jax.numpy as jnp
from jax import lax
from jax.experimental import pallas as pl
from jax.experimental.pallas import tpu as pltpu
from jax.sharding import PartitionSpec as P

HEADS = 16
HEAD_DIM = 64
epsilon = 1e-06
negative = -1e30
MESH = pl.DeviceIdType.MESH
VMEM_LIMIT = 56 * 1024 * 1024
bf16 = jnp.bfloat16
f32 = jnp.float32


def place(n):
    chips = n // 2
    dp, me = lax.axis_index("dp"), lax.axis_index("blk")
    core = lax.rem(me, 2)
    chip = me // 2
    y, z = lax.rem(chip, 2), chip // 2
    pos = z + y * (chips - 1 - 2 * z)

    def chip_at(position):
        position = lax.rem(position + 2 * chips, chips)
        side = position // (chips // 2)
        return 2 * (position + side * (chips - 1 - 2 * position)) + side

    return dp, me, core, pos, chip_at


def ring_partners(n):
    dp, me, core, pos, chip_at = place(n)
    right = (dp, 2 * chip_at(pos + 1) + core)
    left = (dp, 2 * chip_at(pos - 1) + core)
    sibling = (dp, me + 1 - 2 * core)
    return right, left, sibling


def greet(partners):
    barrier = pltpu.get_barrier_semaphore()
    for partner in partners:
        pl.semaphore_signal(barrier, inc=1, device_id=partner, device_id_type=MESH)
    pl.semaphore_wait(barrier, len(partners))


def remote(src, dst, send, recv, device):
    return pltpu.make_async_remote_copy(
        src_ref=src, dst_ref=dst, send_sem=send, recv_sem=recv, device_id=device, device_id_type=MESH
    )


def gather_kernel(n, x_ref, out_ref, own_sem, ring_send, ring_recv, sib_send, sib_recv):
    chips = n // 2
    half = chips // 2
    rows = out_ref.shape[1]
    part = rows // 2
    dp, me, core, pos, chip_at = place(n)
    right, left, sibling = ring_partners(n)
    own = pltpu.make_async_copy(x_ref, out_ref.at[me], own_sem)
    own.start()
    greet((right, left, sibling))
    own.wait()

    def piece(position, k):
        return out_ref.at[2 * chip_at(position) + core, pl.ds(k * part, part)]

    def ring(way, step, k):
        ref = piece(pos - step if way == 0 else pos + step, k)
        return remote(ref, ref, ring_send.at[way, step, k], ring_recv.at[way, step, k], right if way == 0 else left)

    def across(way, step, k):
        ref = piece(pos - step if way == 0 else pos + step, k)
        return remote(ref, ref, sib_send.at[way, step, k], sib_recv.at[way, step, k], sibling)

    def pieces(way, step):
        return (0, 1) if step < half - 1 else (way,)

    started = []
    for k in (0, 1):
        for way in (0, 1):
            if k in pieces(way, 0):
                copy = ring(way, 0, k)
                copy.start()
                started.append(copy)
    for k in (0, 1):
        copy = across(0, 0, k)
        copy.start()
        started.append(copy)
    siblings = [(0, 0, 0), (0, 0, 1)]
    for step in range(half):
        for k in (0, 1):
            for way in (0, 1):
                if k not in pieces(way, step):
                    continue
                ring(way, step, k).wait_recv()
                if step + 1 < half and k in pieces(way, step + 1):
                    copy = ring(way, step + 1, k)
                    copy.start()
                    started.append(copy)
                copy = across(way, step + 1, k)
                copy.start()
                started.append(copy)
                siblings.append((way, step + 1, k))
    for key in siblings:
        across(*key).wait_recv()
    for copy in started:
        copy.wait_send()


def ring_gather(x, n, collective_id):
    rows, columns = x.shape
    half = n // 4
    return pl.pallas_call(
        functools.partial(gather_kernel, n),
        out_shape=jax.ShapeDtypeStruct((n, rows, columns), x.dtype),
        in_specs=[pl.BlockSpec(memory_space=pl.ANY)],
        out_specs=pl.BlockSpec(memory_space=pl.ANY),
        scratch_shapes=[
            pltpu.SemaphoreType.DMA,
            pltpu.SemaphoreType.DMA((2, half, 2)),
            pltpu.SemaphoreType.DMA((2, half, 2)),
            pltpu.SemaphoreType.DMA((2, half + 1, 2)),
            pltpu.SemaphoreType.DMA((2, half + 1, 2)),
        ],
        compiler_params=pltpu.CompilerParams(
            collective_id=collective_id, has_side_effects=True, vmem_limit_bytes=VMEM_LIMIT
        ),
        name="ring_gather",
    )(x)


def scatter_kernel(
    n, x_ref, out_ref, sib_ref, held, landed, ring_send, ring_recv, sib_send, sib_recv
):
    chips = n // 2
    half = chips // 2
    rows = out_ref.shape[0]
    part = rows // 2
    dp, me, core, pos, chip_at = place(n)
    right, left, sibling = ring_partners(n)
    greet((right, left, sibling))

    order = [half]
    for t in range(half - 1, 0, -1):
        order += [t, -t]
    order.append(0)

    def across(offset):
        chip = chip_at(pos + offset)
        index = offset + half
        return remote(
            x_ref.at[2 * chip + 1 - core], sib_ref.at[chip], sib_send.at[index], sib_recv.at[index], sibling
        )

    started = []
    for offset in order:
        copy = across(offset)
        copy.start()
        started.append(copy)

    def mine(offset, k):
        chip = chip_at(pos + offset)
        window = pl.ds(k * part, part)
        return x_ref[2 * chip + core, window, :].astype(f32) + sib_ref[chip, window, :].astype(f32)

    def ring(way, t, k):
        return remote(
            held.at[way, t, k], landed.at[way, t, k], ring_send.at[way, t, k], ring_recv.at[way, t, k],
            right if way == 0 else left,
        )

    for t in range(half):
        for way in (0, 1):
            offset = half - t if way == 0 else t - half
            if t == 0:
                offset = half
            if not (t == 0 and way == 1):
                across(offset).wait_recv()
            for k in (way, 1 - way):
                if t == 0 and k != way:
                    continue
                value = mine(offset, k)
                if t >= 2 or (t == 1 and k == way):
                    ring(way, t - 1, k).wait_recv()
                    value = value + landed[way, t - 1, k].astype(f32)
                held[way, t, k] = value.astype(held.dtype)
                copy = ring(way, t, k)
                copy.start()
                started.append(copy)
    across(0).wait_recv()
    for k in (0, 1):
        value = mine(0, k)
        for way in (0, 1):
            ring(way, half - 1, k).wait_recv()
            value = value + landed[way, half - 1, k].astype(f32)
        out_ref[pl.ds(k * part, part), :] = value
    for copy in started:
        copy.wait_send()


def ring_scatter(x, n, collective_id):
    _, rows, columns = x.shape
    half = n // 4
    return pl.pallas_call(
        functools.partial(scatter_kernel, n),
        out_shape=jax.ShapeDtypeStruct((rows, columns), f32),
        in_specs=[pl.BlockSpec(memory_space=pltpu.VMEM)],
        out_specs=pl.BlockSpec(memory_space=pltpu.VMEM),
        scratch_shapes=[
            pltpu.VMEM((n // 2, rows, columns), x.dtype),
            pltpu.VMEM((2, half, 2, rows // 2, columns), x.dtype),
            pltpu.VMEM((2, half, 2, rows // 2, columns), x.dtype),
            pltpu.SemaphoreType.DMA((2, half, 2)),
            pltpu.SemaphoreType.DMA((2, half, 2)),
            pltpu.SemaphoreType.DMA((2 * half + 1,)),
            pltpu.SemaphoreType.DMA((2 * half + 1,)),
        ],
        compiler_params=pltpu.CompilerParams(
            collective_id=collective_id, has_side_effects=True, vmem_limit_bytes=VMEM_LIMIT
        ),
        name="ring_scatter",
    )(x)


def exchange_kernel(n, x_ref, out_ref, own_sem, send, recv):
    dp, me = lax.axis_index("dp"), lax.axis_index("blk")
    own = pltpu.make_async_copy(x_ref.at[me], out_ref.at[me], own_sem)
    own.start()
    others = [lax.rem(me + k, n) for k in range(1, n)]
    greet([(dp, other) for other in others])
    copies = []
    for k, other in enumerate(others):
        copy = remote(x_ref.at[other], out_ref.at[me], send.at[k], recv.at[k], (dp, other))
        copy.start()
        copies.append(copy)
    own.wait()
    for copy in copies:
        copy.wait()


def exchange(x, n, collective_id):
    return pl.pallas_call(
        functools.partial(exchange_kernel, n),
        out_shape=jax.ShapeDtypeStruct(x.shape, x.dtype),
        in_specs=[pl.BlockSpec(memory_space=pl.ANY)],
        out_specs=pl.BlockSpec(memory_space=pl.ANY),
        scratch_shapes=[
            pltpu.SemaphoreType.DMA,
            pltpu.SemaphoreType.DMA((n - 1,)),
            pltpu.SemaphoreType.DMA((n - 1,)),
        ],
        compiler_params=pltpu.CompilerParams(
            collective_id=collective_id, has_side_effects=True, vmem_limit_bytes=VMEM_LIMIT
        ),
        name="exchange",
    )(x)


def settle_kernel(n, ndp, x_ref, local_ref, out_ref, both_ref, own_sems, send, recv, dp_send, dp_recv, loc_send, loc_recv):
    dp, me = lax.axis_index("dp"), lax.axis_index("blk")
    others = [lax.rem(me + k, n) for k in range(1, n)]
    peers = [lax.rem(dp + r, ndp) for r in range(1, ndp)]
    own = pltpu.make_async_copy(x_ref.at[me], out_ref.at[dp, me], own_sems.at[0])
    own.start()
    own_local = pltpu.make_async_copy(local_ref, both_ref.at[dp], own_sems.at[1])
    own_local.start()
    greet([(dp, other) for other in others] + [(peer, me) for peer in peers])
    copies = []
    for k, other in enumerate(others):
        copy = remote(x_ref.at[other], out_ref.at[dp, me], send.at[k], recv.at[k], (dp, other))
        copy.start()
        copies.append(copy)
    later = []
    for r, peer in enumerate(peers):
        copy = remote(local_ref, both_ref.at[dp], loc_send.at[r], loc_recv.at[r], (peer, me))
        copy.start()
        later.append(copy)
        copy = remote(x_ref.at[me], out_ref.at[dp, me], dp_send.at[r, 0], dp_recv.at[r, 0], (peer, me))
        copy.start()
        later.append(copy)
    for k, copy in enumerate(copies):
        copy.wait_recv()
        source = lax.rem(me + n - 1 - k, n)
        for r, peer in enumerate(peers):
            onward = remote(
                out_ref.at[dp, source], out_ref.at[dp, source], dp_send.at[r, k + 1], dp_recv.at[r, k + 1], (peer, me)
            )
            onward.start()
            later.append(onward)
    own.wait()
    own_local.wait()
    for copy in copies:
        copy.wait_send()
    for copy in later:
        copy.wait()


def settle(x, local, n, ndp, collective_id):
    return pl.pallas_call(
        functools.partial(settle_kernel, n, ndp),
        out_shape=(
            jax.ShapeDtypeStruct((ndp,) + x.shape, x.dtype),
            jax.ShapeDtypeStruct((ndp,) + local.shape, local.dtype),
        ),
        in_specs=[pl.BlockSpec(memory_space=pl.ANY)] * 2,
        out_specs=(pl.BlockSpec(memory_space=pl.ANY),) * 2,
        scratch_shapes=[
            pltpu.SemaphoreType.DMA((2,)),
            pltpu.SemaphoreType.DMA((n - 1,)),
            pltpu.SemaphoreType.DMA((n - 1,)),
            pltpu.SemaphoreType.DMA((ndp - 1, n)),
            pltpu.SemaphoreType.DMA((ndp - 1, n)),
            pltpu.SemaphoreType.DMA((ndp - 1,)),
            pltpu.SemaphoreType.DMA((ndp - 1,)),
        ],
        compiler_params=pltpu.CompilerParams(
            collective_id=collective_id, has_side_effects=True, vmem_limit_bytes=VMEM_LIMIT
        ),
        name="settle",
    )(x, local)


def contract(left, right, dims):
    return lax.dot_general(left, right, ((dims[:1], dims[1:]), ((), ())), preferred_element_type=f32)


def forward_kernel(causal, tile, q_ref, k_ref, v_ref, qs_ref, ks_ref, o_ref, l_ref):
    length = q_ref.shape[0]

    def one(start, reach):
        rows = pl.ds(start, tile)
        scores = contract(q_ref[rows, :], k_ref[:reach, :], (1, 1))
        keep = qs_ref[rows, :] == ks_ref[:, :reach]
        if causal:
            keep = keep & (
                lax.broadcasted_iota(jnp.int32, (tile, reach), 1)
                <= lax.broadcasted_iota(jnp.int32, (tile, reach), 0) + start
            )
        scores = jnp.where(keep, scores, negative)
        top = jnp.max(scores, axis=1, keepdims=True)
        weights = jnp.exp(scores - top)
        total = jnp.sum(weights, axis=1, keepdims=True)
        o_ref[rows, :] = contract(weights.astype(bf16), v_ref[:reach, :], (1, 0)) / total
        l_ref[rows, :] = top + jnp.log(total)

    if causal:
        for i in range(length // tile):
            one(i * tile, (i + 1) * tile)
    else:

        @pl.loop(0, length // tile)
        def _(i):
            one(pl.multiple_of(i * tile, tile), length)


def attend_forward(queries, keys, values, query_seg, key_seg, causal):
    length, width = queries.shape
    return pl.pallas_call(
        functools.partial(forward_kernel, causal, 256),
        out_shape=(jax.ShapeDtypeStruct((length, width), f32), jax.ShapeDtypeStruct((length, 1), f32)),
        compiler_params=pltpu.CompilerParams(vmem_limit_bytes=VMEM_LIMIT),
        name="attend_forward",
    )(queries, keys, values, query_seg[:, None], key_seg[None, :])


def backward_kernel(
    causal, tile, q_ref, k_ref, v_ref, g_ref, qs_ref, ks_ref, l_ref, s_ref, dq_ref, dk_ref, dv_ref, dk_sum, dv_sum
):
    length = q_ref.shape[0]
    dk_sum[...] = jnp.zeros_like(dk_sum)
    dv_sum[...] = jnp.zeros_like(dv_sum)

    def one(start, reach):
        rows = pl.ds(start, tile)
        queries, grads, keys = q_ref[rows, :], g_ref[rows, :], k_ref[:reach, :]
        scores = contract(keys, queries, (1, 1))
        keep = ks_ref[:reach, :] == qs_ref[:, rows]
        if causal:
            keep = keep & (
                lax.broadcasted_iota(jnp.int32, (reach, tile), 0)
                <= lax.broadcasted_iota(jnp.int32, (reach, tile), 1) + start
            )
        probs = jnp.where(keep, jnp.exp(scores - l_ref[:, rows]), 0.0)
        dprobs = contract(v_ref[:reach, :], grads, (1, 1))
        dscores = (probs * (dprobs - s_ref[:, rows])).astype(bf16)
        dk_sum[:reach, :] += contract(dscores, queries, (1, 0))
        dv_sum[:reach, :] += contract(probs.astype(bf16), grads, (1, 0))
        dq_ref[rows, :] = (contract(dscores, keys, (0, 0)) * HEAD_DIM ** (-0.5)).astype(bf16)

    if causal:
        for i in range(length // tile):
            one(i * tile, (i + 1) * tile)
    else:

        @pl.loop(0, length // tile)
        def _(i):
            one(pl.multiple_of(i * tile, tile), length)

    dk_ref[...] = dk_sum[...].astype(bf16)
    dv_ref[...] = dv_sum[...].astype(bf16)


def attend_backward(queries, keys, values, grads, query_seg, key_seg, log_total, spread, causal):
    length, width = queries.shape
    return pl.pallas_call(
        functools.partial(backward_kernel, causal, 256),
        out_shape=(jax.ShapeDtypeStruct((length, width), bf16),) * 3,
        scratch_shapes=[pltpu.VMEM((length, width), f32)] * 2,
        compiler_params=pltpu.CompilerParams(vmem_limit_bytes=VMEM_LIMIT),
        name="attend_backward",
    )(queries, keys, values, grads, query_seg[None, :], key_seg[:, None], log_total, spread)


def rms_norm(values, gain):
    return values * lax.rsqrt(jnp.mean(values * values, axis=-1, keepdims=True) + epsilon) * gain


def mm(left, right):
    return jnp.dot(left, right, preferred_element_type=f32)


def mm_nt(left, right):
    return contract(left, right, (1, 1))


def mm_tn(left, right):
    return contract(left, right, (0, 0))


def gated(gate, upward):
    return jax.nn.gelu(gate, approximate=True) * upward


def local(
    n,
    ndp,
    dec_in,
    enc_out,
    cotangent,
    dec_seg,
    dec_valid,
    enc_seg,
    enc_valid,
    self_gain,
    self_query,
    self_key,
    self_value,
    self_out,
    cross_gain,
    cross_query,
    cross_key,
    cross_value,
    cross_out,
    feed_gain,
    feed_gate,
    feed_up,
    feed_down,
):
    count, width = dec_in.shape[1:]
    units = feed_gate.shape[1]
    depth = self_query.shape[0]
    span = width // n
    share = HEAD_DIM // span
    slim = units // n
    length = n * count
    me = lax.axis_index("blk")

    shards = (self_query, self_key, self_value, cross_query, cross_key, cross_value, feed_gate, feed_up)
    widths = [span] * 6 + [slim] * 2
    total = sum(widths)
    padded = -(-max(total, 3 * count) // 128) * 128

    def by_target(shard, columns):
        return jnp.swapaxes(shard.reshape(depth, n, columns), 0, 1)

    pieces = jnp.concatenate([by_target(s, c) for s, c in zip(shards, widths)], axis=2)
    pieces = jnp.pad(pieces, ((0, 0), (0, 0), (0, padded - total)))
    self_keys = jnp.where(dec_valid == 1, dec_seg, -1)
    cross_keys = jnp.where(enc_valid == 1, enc_seg, -1)
    gains = jnp.concatenate([self_gain, cross_gain, feed_gain])
    marks = jnp.concatenate([dec_seg[0], self_keys[0], cross_keys[0]]).astype(bf16)
    extra = jnp.stack(
        [jnp.pad(gains, (0, padded - gains.shape[0])), jnp.pad(marks, (0, padded - marks.shape[0]))]
    )
    extra = jnp.pad(extra, ((0, 14), (0, 0)))
    pieces = jnp.concatenate([pieces, jnp.broadcast_to(extra[None], (n,) + extra.shape)], axis=1)
    got = exchange(pieces, n, 0)
    slices = got[:, :depth, :].reshape(n * depth, padded)
    w_self = slices[:, : 3 * span]
    w_cq = slices[:, 3 * span : 4 * span]
    w_ckv = slices[:, 4 * span : 6 * span]
    w_feed = slices[:, 6 * span : total]
    gains = got[:, depth, : 3 * depth].reshape(n, 3, depth)
    gain_self, gain_cross, gain_feed = (gains[:, i].reshape(width).astype(f32) for i in range(3))
    marks = got[:, depth + 1, : 3 * count].reshape(n, 3, count)
    seg_row, self_row, cross_row = (marks[:, i].reshape(length).astype(jnp.int32) for i in range(3))

    def spread_rows(x, collective_id):
        return ring_gather(x, n, collective_id).reshape(length, width)

    def sum_rows(x, collective_id):
        return ring_scatter(x.astype(bf16).reshape(n, count, width), n, collective_id)

    groups = [[h * share + i for i in range(share)] for h in range(n // share)]

    def whole_head(x):
        if share == 1:
            return x
        return lax.all_gather(x, "blk", axis=1, tiled=True, axis_index_groups=groups)

    def own_part(x):
        if share == 1:
            return x
        return lax.dynamic_slice_in_dim(x, lax.rem(me, share) * span, span, axis=1)

    tokens = dec_in[0].astype(f32)
    grad_out = cotangent[0].astype(f32) * dec_valid[0][:, None].astype(f32)

    normed_one = spread_rows(rms_norm(tokens, gain_self).astype(bf16), 1)
    encoded = spread_rows(enc_out[0], 1)
    grad_low = spread_rows(grad_out.astype(bf16), 1)
    scale = jnp.asarray(HEAD_DIM ** (-0.5), bf16)

    qkv = mm(normed_one, w_self).astype(bf16)
    query_one = whole_head(qkv[:, :span] * scale)
    key_one = whole_head(qkv[:, span : 2 * span])
    value_one = whole_head(qkv[:, 2 * span :])
    wide_one, log_one = attend_forward(query_one, key_one, value_one, seg_row, self_row, True)
    attn_one = own_part(wide_one).astype(bf16)
    resid_one = tokens + sum_rows(mm(attn_one, self_out), 2)

    normed_two = spread_rows(rms_norm(resid_one, gain_cross).astype(bf16), 1)
    query_two = whole_head(mm(normed_two, w_cq).astype(bf16) * scale)
    kv = mm(encoded, w_ckv).astype(bf16)
    key_two, value_two = whole_head(kv[:, :span]), whole_head(kv[:, span:])
    wide_two, log_two = attend_forward(query_two, key_two, value_two, seg_row, cross_row, False)
    attn_two = own_part(wide_two).astype(bf16)
    resid_two = resid_one + sum_rows(mm(attn_two, cross_out), 2)

    normed_three = spread_rows(rms_norm(resid_two, gain_feed).astype(bf16), 1)
    both = mm(normed_three, w_feed)
    gate, upward = both[:, :slim], both[:, slim:]
    hidden = gated(gate, upward).astype(bf16)
    mixed = (resid_two + sum_rows(mm(hidden, feed_down), 2)).astype(bf16)

    down_grad = mm_tn(hidden, grad_low)
    _, pull = jax.vjp(gated, gate, upward)
    grad_both = jnp.concatenate(pull(mm_nt(grad_low, feed_down)), axis=1).astype(bf16)
    feed_grads = mm_tn(normed_three, grad_both)
    grad_three = sum_rows(mm_nt(grad_both, w_feed), 2)
    _, pull = jax.vjp(rms_norm, resid_two, gain_feed)
    grad_resid, gain_three = pull(grad_three)
    grad_two = grad_out + grad_resid

    grad_two_low = spread_rows(grad_two.astype(bf16), 1)
    out_two = mm_tn(attn_two, grad_two_low)
    grad_attn = whole_head(mm_nt(grad_two_low, cross_out).astype(bf16))
    spread = jnp.sum(grad_attn.astype(f32) * wide_two, axis=1)[None, :]
    cross_dq, cross_dk, cross_dv = (
        own_part(x)
        for x in attend_backward(
            query_two, key_two, value_two, grad_attn, seg_row, cross_row, log_two.reshape(1, length), spread, False
        )
    )
    cross_kv = jnp.concatenate([cross_dk, cross_dv], axis=1)
    cross_grads = (mm_tn(normed_two, cross_dq), mm_tn(encoded, cross_kv))
    grad_normed = sum_rows(mm_nt(cross_dq, w_cq), 2)
    enc_grad = sum_rows(mm_nt(cross_kv, w_ckv), 2)
    _, pull = jax.vjp(rms_norm, resid_one, gain_cross)
    grad_resid, gain_two = pull(grad_normed)
    grad_one = grad_two + grad_resid

    grad_one_low = spread_rows(grad_one.astype(bf16), 1)
    out_one = mm_tn(attn_one, grad_one_low)
    grad_attn = whole_head(mm_nt(grad_one_low, self_out).astype(bf16))
    spread = jnp.sum(grad_attn.astype(f32) * wide_one, axis=1)[None, :]
    self_grad = jnp.concatenate(
        [
            own_part(x)
            for x in attend_backward(
                query_one, key_one, value_one, grad_attn, seg_row, self_row, log_one.reshape(1, length), spread, True
            )
        ],
        axis=1,
    )
    self_grads = mm_tn(normed_one, self_grad)
    _, pull = jax.vjp(rms_norm, tokens, gain_self)
    grad_resid, gain_one = pull(sum_rows(mm_nt(self_grad, w_self), 2))
    dec_grad = grad_one + grad_resid

    columns = jnp.concatenate((self_grads,) + cross_grads + (feed_grads,), axis=1).astype(bf16)
    columns = jnp.pad(columns, ((0, 0), (0, padded - total))).reshape(n, depth, padded)
    gains = jnp.stack([gain_one, gain_two, gain_three]).reshape(3, n, depth)
    gains = jnp.pad(jnp.swapaxes(gains, 0, 1).reshape(n, 1, 3 * depth), ((0, 0), (0, 15), (0, padded - 3 * depth)))
    columns = jnp.concatenate([columns, gains.astype(bf16)], axis=1)
    rows = jnp.concatenate([out_one, out_two, down_grad], axis=0).astype(bf16)
    columns, rows = settle(columns, rows, n, ndp, 3)
    columns = jnp.sum(columns.astype(f32), axis=0)
    rows = jnp.sum(rows.astype(f32), axis=0)
    out_one, out_two, down_grad = rows[:depth], rows[depth : 2 * depth], rows[2 * depth :]
    gains = jnp.sum(columns[:, depth, : 3 * depth], axis=0)
    pieces, at = [], 0
    for c in widths:
        pieces.append(jnp.swapaxes(columns[:, :depth, at : at + c], 0, 1).reshape(depth, n * c))
        at += c
    return (
        mixed[None],
        dec_grad[None],
        enc_grad[None],
        gains[:depth],
        pieces[0],
        pieces[1],
        pieces[2],
        out_one,
        gains[depth : 2 * depth],
        pieces[3],
        pieces[4],
        pieces[5],
        out_two,
        gains[2 * depth :],
        pieces[6],
        pieces[7],
        down_grad,
    )


def solution(mesh):
    row, token = P("dp", "blk"), P("dp", "blk", None)
    gain, weight = P("blk"), P("blk", None)
    return jax.shard_map(
        functools.partial(local, mesh.shape["blk"], mesh.shape["dp"]),
        mesh=mesh,
        in_specs=(token,) * 3 + (row,) * 4 + ((gain,) + (weight,) * 4) * 2 + (gain,) + (weight,) * 3,
        out_specs=(token,) * 3 + ((gain,) + (weight,) * 4) * 2 + (gain,) + (weight,) * 3,
        check_vma=False,
    )
```

```python
import functools
import types

import jax
import jax.numpy as jnp
from jax import lax
from jax.experimental import pallas as pl
from jax.experimental.pallas import tpu as pltpu
from jax.sharding import PartitionSpec as P

HEADS = 16
HEAD_DIM = 64
LANES = 128
PIECES = 2
epsilon = 1e-06
negative = -1e30
MESH = pl.DeviceIdType.MESH
bf16 = jnp.bfloat16
f32 = jnp.float32
VMEM = pltpu.VMEM
DMA = pltpu.SemaphoreType.DMA


def contract(left, right, dims):
    return lax.dot_general(left, right, ((dims[:1], dims[1:]), ((), ())), preferred_element_type=f32)


def mm(left, right):
    return contract(left, right, (1, 0))


def mm_nt(left, right):
    return contract(left, right, (1, 1))


def mm_tn(left, right):
    return contract(left, right, (0, 0))


class Place:
    def __init__(self, n):
        self.n, self.chips = n, n // 2
        self.half = self.chips // 2
        self.dp, self.me = lax.axis_index("dp"), lax.axis_index("blk")
        self.core = lax.rem(self.me, 2)
        chip = self.me // 2
        y, z = lax.rem(chip, 2), chip // 2
        self.pos = z + y * (self.chips - 1 - 2 * z)
        self.sibling = (self.dp, self.me + 1 - 2 * self.core)
        self.half_row = lax.rem(self.dp, 2)
        self.twin = (self.dp + 1 - 2 * self.half_row, self.me)
        self.sides = tuple((self.dp, 2 * self.chip(step) + self.core) for step in (1, -1))

    def chip(self, offset):
        position = lax.rem(self.pos + offset + 2 * self.chips, self.chips)
        side = position // (self.chips // 2)
        return 2 * (position + side * (self.chips - 1 - 2 * position)) + side

    def others(self):
        return [(self.dp, lax.rem(self.me + k, self.n)) for k in range(1, self.n)]

    def around(self):
        return [self.sibling, *self.sides]


def greet(partners):
    barrier = pltpu.get_barrier_semaphore()
    for partner in partners:
        pl.semaphore_signal(barrier, inc=1, device_id=partner, device_id_type=MESH)
    pl.semaphore_wait(barrier, len(partners))


def remote(src, dst, send, recv, device):
    return pltpu.make_async_remote_copy(
        src_ref=src, dst_ref=dst, send_sem=send, recv_sem=recv, device_id=device, device_id_type=MESH
    )


def pieces_of(half, way, step):
    if step < half - 1:
        return tuple(range(PIECES))
    return tuple(range(PIECES // 2)) if way == 0 else tuple(range(PIECES // 2, PIECES))


def drain(task):
    for _ in task:
        pass


def beside(main, task, waits=1, steps=1):
    for count, _ in enumerate(main):
        if (count + 1) % steps == 0:
            for _ in range(waits):
                next(task, None)


def in_turn(*tasks):
    tasks = list(tasks)
    while tasks:
        for task in list(tasks):
            if next(task, "done") == "done":
                tasks.remove(task)
            else:
                yield


def one_by_one(*tasks):
    for task in tasks:
        yield from task


def gather_scratch(n):
    half = n // 4
    return [DMA((2, half, PIECES))] * 2 + [DMA((2, half + 1, PIECES))] * 2


def gather(place, buf, sems, use=None):
    ring_send, ring_recv, sib_send, sib_recv = sems
    half, part = place.half, buf.shape[1] // PIECES
    started = []

    def start(copy):
        copy.start()
        started.append(copy)

    def piece(way, step, k):
        offset = -step if way == 0 else step
        return buf.at[2 * place.chip(offset) + place.core, pl.ds(k * part, part)]

    def ring(way, step, k):
        ref = piece(way, step, k)
        return remote(ref, ref, ring_send.at[way, step, k], ring_recv.at[way, step, k], place.sides[way])

    def across(way, step, k):
        ref = piece(way, step, k)
        return remote(ref, ref, sib_send.at[way, step, k], sib_recv.at[way, step, k], place.sibling)

    def ready(way, step):
        for k in range(PIECES) if step == 0 else pieces_of(half, way, step - 1):
            across(way, step, k).wait_recv()

    for i in range(PIECES):
        for way in (0, 1):
            k = i if way == 0 else PIECES - 1 - i
            if k in pieces_of(half, way, 0):
                start(ring(way, 0, k))
    for k in range(PIECES):
        start(across(0, 0, k))
    for step in range(half):
        for i in range(PIECES):
            for way in (0, 1):
                k = i if way == 0 else PIECES - 1 - i
                if k not in pieces_of(half, way, step):
                    continue
                yield
                ring(way, step, k).wait_recv()
                if step + 1 < half and k in pieces_of(half, way, step + 1):
                    start(ring(way, step + 1, k))
                start(across(way, step + 1, k))
        for way in (0, 1) if step else (0,):
            ready(way, step)
            if use is not None:
                use(place.chip(-step if way == 0 else step))
    yield
    for way in (0, 1):
        ready(way, half)
    if use is not None:
        use(place.chip(half))
    for copy in started:
        copy.wait_send()


def scatter_scratch(n, rows, columns):
    half = n // 4
    return [
        VMEM((n, rows, columns), bf16),
        VMEM((n // 2, rows, columns), bf16),
        VMEM((2, half, PIECES, rows // PIECES, columns), bf16),
        VMEM((2, half, PIECES, rows // PIECES, columns), bf16),
        DMA((2, half, PIECES)),
        DMA((2, half, PIECES)),
        DMA((2 * half + 1,)),
        DMA((2 * half + 1,)),
    ]


def scatter(place, scratch, produce, finish):
    blocks, theirs, held, landed, ring_send, ring_recv, sib_send, sib_recv = scratch
    half, rows = place.half, blocks.shape[1]
    part = rows // PIECES
    started = []

    def start(copy):
        copy.start()
        started.append(copy)

    def across(offset):
        chip, index = place.chip(offset), offset + half
        return remote(
            blocks.at[2 * chip + 1 - place.core], theirs.at[chip], sib_send.at[index], sib_recv.at[index], place.sibling
        )

    def make(offset):
        chip = place.chip(offset)
        value = produce(chip).astype(bf16)
        blocks[2 * chip] = value[:rows]
        blocks[2 * chip + 1] = value[rows:]
        start(across(offset))

    def ring(way, step, k):
        return remote(
            held.at[way, step, k], landed.at[way, step, k], ring_send.at[way, step, k], ring_recv.at[way, step, k],
            place.sides[way],
        )

    def mine(offset, k):
        chip, window = place.chip(offset), pl.ds(k * part, part)
        return blocks[2 * chip + place.core, window, :].astype(f32) + theirs[chip, window, :].astype(f32)

    first = [pieces_of(half, way, half - 1) for way in (0, 1)]
    make(half)
    for step in range(half):
        left = half - 1 - step
        for offset in (left, -left) if left else (0,):
            make(offset)
        if step == 0:
            yield
            across(half).wait_recv()
        else:
            yield
            across(half - step).wait_recv()
            across(step - half).wait_recv()
        for i in range(PIECES):
            for way in (0, 1):
                k = i if way == 0 else PIECES - 1 - i
                if step == 0 and k not in first[way]:
                    continue
                offset = half if step == 0 else half - step if way == 0 else step - half
                value = mine(offset, k)
                if step >= 2 or (step == 1 and k in first[way]):
                    yield
                    ring(way, step - 1, k).wait_recv()
                    value = value + landed[way, step - 1, k].astype(f32)
                held[way, step, k] = value.astype(bf16)
                start(ring(way, step, k))
    yield
    across(0).wait_recv()
    for k in range(PIECES):
        value = mine(0, k)
        for way in (0, 1):
            yield
            ring(way, half - 1, k).wait_recv()
            value = value + landed[way, half - 1, k].astype(f32)
        finish(k, value)
    for copy in started:
        copy.wait_send()


def mark_row(marks, which):
    return jnp.concatenate([marks[i, which : which + 1, :] for i in range(marks.shape[0])], axis=1).astype(f32)


def mark_columns(marks, which):
    n = marks.shape[0]
    rows = jnp.concatenate([marks[i, which : which + 1, :].astype(f32) for i in range(n)], axis=0)
    rows = jnp.concatenate([rows, jnp.zeros((LANES - n, LANES), f32)], axis=0)
    return rows.T


def column_of(columns, first, count):
    blocks = count // LANES
    return jnp.concatenate([columns[:, first // LANES + i : first // LANES + i + 1] for i in range(blocks)], axis=0)


def gain_row(marks, which, depth):
    return jnp.concatenate(
        [marks[i, which : which + 1, :].astype(f32)[:, :depth] for i in range(marks.shape[0])], axis=1
    )


def normalise(values, gain):
    return values * lax.rsqrt(jnp.mean(values * values, axis=-1, keepdims=True) + epsilon) * gain


def tile_of(length):
    return 256 if length <= 2048 else 128


def attend_forward(causal, q_ref, k_ref, v_ref, query_column, key_row, o_ref, l_ref):
    length = q_ref.shape[0]
    tile = tile_of(length)
    for start in range(0, length, tile):
        reach = start + tile if causal else length
        scores = mm_nt(q_ref[start : start + tile, :], k_ref[:reach, :])
        keep = column_of(query_column, start, tile) == key_row[:, :reach]
        if causal:
            keep = keep & (
                lax.broadcasted_iota(jnp.int32, (tile, reach), 1)
                <= lax.broadcasted_iota(jnp.int32, (tile, reach), 0) + start
            )
        scores = jnp.where(keep, scores, negative)
        top = jnp.max(scores, axis=1, keepdims=True)
        weights = jnp.exp(scores - top)
        total = jnp.sum(weights, axis=1, keepdims=True)
        o_ref[start : start + tile, :] = mm(weights.astype(bf16), v_ref[:reach, :]) / total
        l_ref[:, start : start + tile] = jnp.broadcast_to(top + jnp.log(total), (tile, LANES)).T[:1, :]
        yield


def attend_backward(
    causal, q_ref, k_ref, v_ref, g_ref, o_ref, l_ref, query_row, key_column, dq_ref, dk_sum, dv_sum
):
    length = q_ref.shape[0]
    tile = tile_of(length)
    dk_sum[...] = jnp.zeros_like(dk_sum)
    dv_sum[...] = jnp.zeros_like(dv_sum)
    for start in range(0, length, tile):
        reach = start + tile if causal else length
        rows = slice(start, start + tile)
        queries, grads = q_ref[rows, :], g_ref[rows, :]
        spread = jnp.sum(grads.astype(f32) * o_ref[rows, :], axis=1, keepdims=True)
        spread = jnp.broadcast_to(spread, (tile, LANES)).T[:1, :]
        dq = 0.0
        for begin in range(0, reach, 2048):
            part = slice(begin, min(reach, begin + 2048))
            keys = k_ref[part, :]
            count = keys.shape[0]
            scores = mm_nt(keys, queries)
            keep = column_of(key_column, begin, count) == query_row[:, rows]
            if causal:
                keep = keep & (
                    lax.broadcasted_iota(jnp.int32, (count, tile), 0) + begin
                    <= lax.broadcasted_iota(jnp.int32, (count, tile), 1) + start
                )
            probs = jnp.where(keep, jnp.exp(scores - l_ref[:, rows]), 0.0)
            dprobs = mm_nt(v_ref[part, :], grads)
            dscores = (probs * (dprobs - spread)).astype(bf16)
            dk_sum[part, :] += mm(dscores, queries)
            dv_sum[part, :] += mm(probs.astype(bf16), grads)
            dq = dq + mm_tn(dscores, keys)
        dq_ref[rows, :] = (dq * HEAD_DIM ** (-0.5)).astype(bf16)
        yield


class Stage:
    def __init__(self, body, inputs, outputs, scratch):
        self.body, self.inputs, self.outputs, self.scratch = body, inputs, outputs, scratch


def fused(name, collective_id, n, ndp, stages, arrays, wanted):
    outputs, scratch = {}, {}
    for stage in stages:
        outputs.update(stage.outputs)
        scratch.update(stage.scratch)
    inputs = [x for stage in stages for x in stage.inputs if x not in outputs]
    inputs = list(dict.fromkeys(inputs))
    for key in list(outputs):
        if key not in wanted:
            scratch[key] = VMEM(outputs[key].shape, outputs.pop(key).dtype)

    def specs(names):
        return tuple(pl.BlockSpec(memory_space=pl.ANY if x.startswith("_") else VMEM) for x in names)

    flat, slots = [], {}
    for key, value in scratch.items():
        many = isinstance(value, list)
        items = value if many else [value]
        slots[key] = (len(flat), len(items), many)
        flat += items

    def kernel(*refs):
        table = dict(zip(inputs + list(outputs), refs))
        rest = refs[len(inputs) + len(outputs) :]
        for key, (at, length, many) in slots.items():
            table[key] = rest[at : at + length] if many else rest[at]
        table["saves"] = []
        place = Place(n)
        view = types.SimpleNamespace(**table)
        behind = iter(())
        for number, stage in enumerate(stages):
            behind = stage.body(place, view, behind, number == 0)
        drain(behind)
        for copy in view.saves:
            copy.wait()

    results = pl.pallas_call(
        kernel,
        out_shape=tuple(outputs.values()),
        in_specs=specs(inputs),
        out_specs=specs(outputs),
        scratch_shapes=flat,
        compiler_params=pltpu.CompilerParams(
            collective_id=collective_id, has_side_effects=True, vmem_limit_bytes=(58 if n <= 16 else 62) * 1024 * 1024
        ),
        name=name,
    )(*[arrays[x] for x in inputs])
    arrays.update(zip(outputs, results))


def shape(*dims, kind=bf16):
    return jax.ShapeDtypeStruct(dims, kind)


def settle_columns(place, ndp, span, mine, wide, landed, sems):
    mate_send, mate_recv, own_sem, send, recv, dp_send, dp_recv = sems
    matrices, mates, width, _ = mine.shape
    groups = place.n // mates
    depth = landed.shape[2]
    group, lane = place.me // mates, lax.rem(place.me, mates)
    started = []

    def start(copy):
        copy.start()
        started.append(copy)

    def swap(r):
        mate = group * mates + lax.rem(lane + r, mates)
        ref = mine.at[:, lane]
        return remote(ref, ref, mate_send.at[r - 1], mate_recv.at[r - 1], (place.dp, mate))

    def rows(device):
        return wide.at[:, pl.ds(pl.multiple_of(device * depth, depth), depth), :]

    def lanes(origin):
        return landed.at[place.dp, :, :, pl.ds(pl.multiple_of(origin * LANES, LANES), LANES)]

    def move(step):
        target = lax.rem(group + step, groups) * mates + lane
        return remote(rows(target), lanes(group), send.at[step - 1], recv.at[step - 1], (place.dp, target))

    def pass_on(step, r, ref, origin):
        peer = lax.rem(place.dp + r, ndp)
        return remote(ref, lanes(origin), dp_send.at[step, r - 1], dp_recv.at[step, r - 1], (peer, place.me))

    for r in range(1, mates):
        start(swap(r))
    yield
    for r in range(1, mates):
        swap(r).wait_recv()
    for m in range(matrices):
        wide[m] = jnp.concatenate([mine[m, i] for i in range(mates)], axis=1)
    for step in range(1, groups):
        start(move(step))
    own = pltpu.make_async_copy(rows(place.me), lanes(group), own_sem)
    own.start()
    for r in range(1, ndp):
        start(pass_on(0, r, rows(place.me), group))
    for step in range(1, groups):
        yield
        move(step).wait_recv()
        origin = lax.rem(group + groups - step, groups)
        for r in range(1, ndp):
            start(pass_on(step, r, lanes(origin), origin))
    yield
    own.wait()
    for step in range(groups):
        for r in range(1, ndp):
            pass_on(step, r, lanes(group), group).wait_recv()
    for copy in started:
        copy.wait_send()


def settle_columns_scratch(n, ndp, span, depth, width, matrices):
    mates = LANES // span
    groups = n // mates
    return [
        VMEM((matrices, mates, width, span), bf16),
        VMEM((matrices, width, LANES), bf16),
        VMEM((ndp, matrices, depth, width), bf16),
        DMA((mates - 1,)),
        DMA((mates - 1,)),
        DMA,
        DMA((groups - 1,)),
        DMA((groups - 1,)),
        DMA((groups, ndp - 1)),
        DMA((groups, ndp - 1)),
    ]


def settle_blocks(place, ndp, source, landed, sems):
    own_sem, send, recv, dp_send, dp_recv = sems
    n = place.n
    here = place.dp if ndp > 1 else 0
    started = []

    def start(copy):
        copy.start()
        started.append(copy)

    def move(k):
        target = lax.rem(place.me + k, n)
        return remote(
            source(target), landed.at[here, place.me], send.at[k - 1], recv.at[k - 1], (place.dp, target)
        )

    def pass_on(k, r, ref, origin):
        peer = lax.rem(place.dp + r, ndp)
        return remote(ref, landed.at[here, origin], dp_send.at[k, r - 1], dp_recv.at[k, r - 1], (peer, place.me))

    for k in range(1, n):
        start(move(k))
    own = pltpu.make_async_copy(source(place.me), landed.at[here, place.me], own_sem)
    own.start()
    for r in range(1, ndp):
        start(pass_on(0, r, source(place.me), place.me))
    for k in range(1, n):
        yield
        move(k).wait_recv()
        origin = lax.rem(place.me + n - k, n)
        for r in range(1, ndp):
            start(pass_on(k, r, landed.at[here, origin], origin))
    yield
    own.wait()
    for k in range(n):
        for r in range(1, ndp):
            pass_on(k, r, landed.at[here, place.me], place.me).wait_recv()
    for copy in started:
        copy.wait_send()


def settle_blocks_scratch(n, ndp, shape, kind):
    return [
        VMEM((ndp, n) + shape, kind),
        DMA,
        DMA((n - 1,)),
        DMA((n - 1,)),
        DMA((n, max(1, ndp - 1))),
        DMA((n, max(1, ndp - 1))),
    ]


def settle_rows(place, ndp, parts, landed, sems):
    send, recv = sems
    copies, at = [], 0
    for i, part in enumerate(parts):
        window = pl.ds(at, part.shape[0])
        at += part.shape[0]
        for r in range(1, ndp):
            peer = lax.rem(place.dp + r, ndp)
            copy = remote(
                part, landed.at[place.dp, window], send.at[i, r - 1], recv.at[i, r - 1], (peer, place.me)
            )
            copy.start()
            copies.append(copy)
        landed[place.dp, window] = part[...]
    yield
    for copy in copies:
        copy.wait()


def settle_rows_scratch(ndp, rows, width, parts):
    return [VMEM((ndp, rows, width), bf16), DMA((parts, ndp - 1)), DMA((parts, ndp - 1))]


def peers(place, ndp):
    return [(lax.rem(place.dp + r, ndp), place.me) for r in range(1, ndp)]


def own_part(place, values, span):
    share = HEAD_DIM // span
    part = values[:, :span]
    for i in range(1, share):
        part = jnp.where(lax.rem(place.me, share) == i, values[:, i * span : (i + 1) * span], part)
    return part


def rows_of(chip, count):
    return pl.ds(pl.multiple_of(chip * 2 * count, 2 * count), 2 * count)


def chip_rows(blocks, chip):
    _, count, width = blocks.shape
    return blocks[pl.ds(2 * chip, 2)].reshape(2 * count, width)


def piece_rows(k, count):
    part = count // PIECES
    return slice(k * part, (k + 1) * part)


def columns_task(place, span, stack, buf, first, last, sems):
    own_sem, send, recv, twin_send, twin_recv, pass_send, pass_recv = sems
    mates = LANES // span
    groups = place.n // mates
    depth = stack.shape[1]
    part = depth // 2
    group, lane = place.me // mates, lax.rem(place.me, mates)
    which = pl.ds(first, last - first)
    started = []

    def start(copy):
        copy.start()
        started.append(copy)

    def lanes(target):
        return pl.ds(pl.multiple_of(target * LANES, LANES), LANES)

    def rows(device, begin, count):
        return buf.at[which, pl.ds(pl.multiple_of(device * depth + begin, part), count), :]

    def half(device, other):
        return rows(device, (1 - place.half_row if other else place.half_row) * part, part)

    def hand(step, other, r, source, target):
        mate = group * mates + lax.rem(lane + r, mates)
        return remote(
            source, target, pass_send.at[step, other, r - 1], pass_recv.at[step, other, r - 1], (place.dp, mate)
        )

    def arrival(step):
        target = lax.rem(group + step, groups)
        source = stack.at[which, pl.ds(pl.multiple_of(place.half_row * part, part), part), lanes(target)]
        return remote(
            source, half(place.me, 0), send.at[step - 1], recv.at[step - 1], (place.dp, target * mates + lane)
        )

    def origin(step):
        return lax.rem(group + groups - step, groups) * mates + lane

    def twin(step):
        ref = half(origin(step), 0)
        return remote(ref, ref, twin_send.at[step - 1], twin_recv.at[step - 1], place.twin)

    def pass_on(step, other):
        for r in range(1, mates):
            ref = half(origin(step), other)
            start(hand(step, other, r, ref, ref))

    for step in range(1, groups):
        start(arrival(step))
    mine = stack.at[which, :, lanes(group)]
    own = pltpu.make_async_copy(mine, rows(place.me, 0, depth), own_sem)
    own.start()
    for r in range(1, mates):
        start(hand(0, 0, r, mine, rows(place.me, 0, depth)))
    for step in range(1, groups + 1):
        yield
        if step < groups:
            arrival(step).wait_recv()
            start(twin(step))
            pass_on(step, 0)
        if step > 1:
            twin(step - 1).wait_recv()
            pass_on(step - 1, 1)
    yield
    own.wait()
    for r in range(1, mates):
        hand(0, 0, r, mine, rows(place.me, 0, depth)).wait_recv()
        for step in range(1, groups):
            for other in (0, 1):
                ref = half(place.me, other)
                hand(step, other, r, ref, ref).wait_recv()
    for copy in started:
        copy.wait_send()


def columns_scratch(n, span):
    mates = LANES // span
    groups = n // mates
    return [DMA] + [DMA((groups - 1,))] * 4 + [DMA((groups, 2, mates - 1))] * 2


def share_blocks(place, blocks, landed, sems, window=4):
    own_sem, send, recv, twin_send, twin_recv = sems
    n, part = place.n, blocks.shape[1] // 2
    rows = pl.ds(pl.multiple_of(place.half_row * part, part), part)
    started = []

    def start(copy):
        copy.start()
        started.append(copy)

    def move(k):
        target = lax.rem(place.me + k, n)
        return remote(
            blocks.at[target, rows], landed.at[place.me, rows], send.at[k - 1], recv.at[k - 1], (place.dp, target)
        )

    def twin(k):
        ref = landed.at[lax.rem(place.me + n - k, n), rows]
        return remote(ref, ref, twin_send.at[k - 1], twin_recv.at[k - 1], place.twin)

    own = pltpu.make_async_copy(blocks.at[place.me], landed.at[place.me], own_sem)
    own.start()
    for k in range(1, min(window, n)):
        start(move(k))
    for k in range(1, n + 1):
        yield
        if k + window - 1 < n:
            start(move(k + window - 1))
        if k < n:
            move(k).wait_recv()
            start(twin(k))
        if k > 1:
            twin(k - 1).wait_recv()
    yield
    own.wait()
    for copy in started:
        copy.wait_send()


def share_scratch(n):
    return [DMA] + [DMA((n - 1,))] * 4


def open_stage(n, ndp, span, depth, count, width, slim):
    length = n * count
    mates = LANES // span

    def body(place, v, behind, first):
        v.x_all[place.me] = v.x[...]
        v.encoded[place.me] = v.enc[...]
        for i, ref in enumerate((v.wq, v.wk, v.wv, v.wcq, v.wck, v.wcv)):
            v.stack[i] = ref[...]
        segment = v.dec_seg[...].astype(f32)
        rows = [segment, jnp.where(v.dec_valid[...] == 1, segment, -1.0)]
        rows.append(jnp.where(v.enc_valid[...] == 1, v.enc_seg[...].astype(f32), -1.0))
        for ref in (v.gain_self, v.gain_cross, v.gain_feed):
            rows.append(jnp.concatenate([ref[...].astype(f32), jnp.zeros((1, LANES - depth), f32)], axis=1))
        rows.append(jnp.zeros((10, LANES), f32))
        v.mark[...] = jnp.concatenate(rows, axis=0).astype(bf16)
        v.marks_in[place.me] = v.mark[...]
        if first:
            greet(place.others() + peers(place, ndp))
        copies = []
        for k, other in enumerate(place.others()):
            copy = remote(v.mark, v.marks_in.at[place.me], v.mark_send.at[k], v.mark_recv.at[k], other)
            copy.start()
            copies.append(copy)
        side = lax.rem(place.me, mates) // (HEAD_DIM // span)

        def head(index):
            pair = v.buf[index]
            return jnp.where(side == 0, pair[:, :HEAD_DIM], pair[:, HEAD_DIM:])

        scale = HEAD_DIM ** (-0.5)
        gain, ready, waiting = [], [], []

        def begin(chip):
            if not ready:
                waiting.append(chip)
                return
            for b in (0, 1):
                v.normed_a[2 * chip + b] = normalise(v.x_all[2 * chip + b].astype(f32), gain[0]).astype(bf16)
            rows = rows_of(chip, count)
            qkv = mm(chip_rows(v.normed_a, chip), v.w_self[...])
            v.q1[rows, :] = (qkv[:, :HEAD_DIM].astype(bf16).astype(f32) * scale).astype(bf16)
            v.k1[rows, :] = qkv[:, HEAD_DIM : 2 * HEAD_DIM].astype(bf16)
            v.v1[rows, :] = qkv[:, 2 * HEAD_DIM :].astype(bf16)

        def cross(chip):
            if len(ready) < 2:
                waiting.append(chip)
                return
            rows = rows_of(chip, count)
            kv = mm(chip_rows(v.encoded, chip), v.w_ckv[...])
            v.k2[rows, :] = kv[:, :HEAD_DIM].astype(bf16)
            v.v2[rows, :] = kv[:, HEAD_DIM:].astype(bf16)

        def background():
            weights = columns_task(place, span, v.stack, v.buf, 4, 6, v.late)
            next(weights)
            for _ in gather(place, v.encoded, v.ring_enc, cross):
                yield
                if len(ready) < 2 and next(weights, "done") == "done":
                    v.w_ckv[...] = jnp.concatenate([head(4), head(5)], axis=1)
                    v.w_ckv_own[...] = jnp.concatenate([own_part(place, head(i), span) for i in (4, 5)], axis=1)
                    ready.append(True)
                    for chip in waiting:
                        cross(chip)
            v.saves.append(pltpu.make_async_copy(v.encoded, v._encoded, v.open_out.at[1]))
            v.saves[-1].start()

        weights = columns_task(place, span, v.stack, v.buf, 0, 4, v.early)
        next(weights)
        ring = gather(place, v.x_all, v.ring_x, begin)
        behind = one_by_one(behind, background())
        for number, _ in enumerate(ring):
            if not ready and next(weights, "done") == "done":
                for copy in copies:
                    copy.wait()
                v.marks[...] = v.marks_in[...]
                gain.append(gain_row(v.marks, 3, depth))
                v.w_self[...] = jnp.concatenate([head(0), head(1), head(2)], axis=1)
                v.w_self_own[...] = jnp.concatenate([own_part(place, head(i), span) for i in range(3)], axis=1)
                v.w_cq[...] = head(3)
                ready.append(True)
                for chip in waiting:
                    begin(chip)
                waiting.clear()
            elif ready and number % 2:
                next(behind, None)
        v.saves.append(pltpu.make_async_copy(v.normed_a, v._normed_one, v.open_out.at[0]))
        v.saves[-1].start()
        column, row = mark_columns(v.marks, 0), mark_row(v.marks, 1)
        beside(attend_forward(True, v.q1, v.k1, v.v1, column, row, v.o1, v.l1), behind)
        return behind

    head = shape(length, HEAD_DIM)
    gathered = shape(n, count, width)
    return Stage(
        body,
        ["x", "enc", "wq", "wk", "wv", "wcq", "wck", "wcv", "dec_seg", "dec_valid", "enc_seg", "enc_valid"]
        + ["gain_self", "gain_cross", "gain_feed"],
        dict(
            _normed_one=gathered, _encoded=gathered, q1=head, k1=head, v1=head, o1=shape(length, HEAD_DIM, kind=f32),
            l1=shape(1, length, kind=f32), k2=head, v2=head, w_self_own=shape(width, 3 * span),
            w_cq=shape(width, HEAD_DIM), w_ckv_own=shape(width, 2 * span), marks=shape(n, 16, LANES),
        ),
        dict(
            x_all=VMEM((n, count, width), bf16), normed_a=VMEM((n, count, width), bf16),
            encoded=VMEM((n, count, width), bf16), stack=VMEM((6, depth, width), bf16), buf=VMEM((6, width, LANES), bf16),
            w_self=VMEM((width, 3 * HEAD_DIM), bf16), w_ckv=VMEM((width, 2 * HEAD_DIM), bf16), mark=VMEM((16, LANES), bf16),
            marks_in=VMEM((n, 16, LANES), bf16), mark_send=DMA((n - 1,)), mark_recv=DMA((n - 1,)), open_out=DMA((2,)),
            ring_x=gather_scratch(n), ring_enc=gather_scratch(n), early=columns_scratch(n, span),
            late=columns_scratch(n, span),
        ),
    )


def cross_stage(n, ndp, span, depth, count, width, slim):
    length = n * count

    def body(place, v, behind, first):
        kept = jnp.broadcast_to(v.dec_valid[...].astype(f32), (LANES, LANES)).T[:, :1]
        v.low_a[place.me] = (v.cotangent[...].astype(f32) * kept).astype(bf16)
        gain = gain_row(v.marks, 4, depth)
        if first:
            greet(place.others() + peers(place, ndp))

        def produce(chip):
            return mm(own_part(place, v.o1[rows_of(chip, count), :], span).astype(bf16), v.out_self[...])

        def finish(k, value):
            rows = piece_rows(k, count)
            value = value + v.x[rows, :].astype(f32)
            v.resid_one[rows, :] = value
            v.normed_b[place.me, rows, :] = normalise(value, gain).astype(bf16)

        def query(chip):
            value = mm(chip_rows(v.normed_b, chip), v.w_cq[...]).astype(bf16)
            v.q2[rows_of(chip, count), :] = (value.astype(f32) * HEAD_DIM ** (-0.5)).astype(bf16)

        def weights():
            for device in range(n):
                columns = slice(device * slim, (device + 1) * slim)
                both = [ref[:, columns].astype(f32) for ref in (v.gate, v.up)]
                v.targets[device] = jnp.concatenate(both, axis=1).astype(bf16)
            yield
            yield from share_blocks(place, v.targets, v.w_feed_in, v.feed_in)
            v.saves.append(pltpu.make_async_copy(v.w_feed_in, v._w_feed, v.cross_out.at[2]))
            v.saves[-1].start()

        def lows():
            yield from gather(place, v.low_a, v.ring_low)
            v.saves.append(pltpu.make_async_copy(v.low_a, v._low_all, v.cross_out.at[1]))
            v.saves[-1].start()

        behind = in_turn(behind, weights(), lows())
        beside(scatter(place, v.sums_a, produce, finish), behind, 1, 2)
        beside(gather(place, v.normed_b, v.ring_b, query), behind, 1, 2)
        v.saves.append(pltpu.make_async_copy(v.normed_b, v._normed_two, v.cross_out.at[0]))
        v.saves[-1].start()
        column, row = mark_columns(v.marks, 0), mark_row(v.marks, 2)
        if first:
            beside(attend_forward(False, v.q2, v.k2, v.v2, column, row, v.o2, v.l2), behind, 2)
        else:
            drain(behind)
            drain(attend_forward(False, v.q2, v.k2, v.v2, column, row, v.o2, v.l2))
        return behind

    gathered = shape(n, count, width)
    return Stage(
        body,
        ["o1", "out_self", "x", "marks", "w_cq", "k2", "v2", "cotangent", "dec_valid", "gate", "up"],
        dict(
            resid_one=shape(count, width, kind=f32), _normed_two=gathered, _low_all=gathered, q2=shape(length, HEAD_DIM),
            o2=shape(length, HEAD_DIM, kind=f32), l2=shape(1, length, kind=f32), _w_feed=shape(n, depth, 2 * slim),
        ),
        dict(
            normed_b=VMEM((n, count, width), bf16), low_a=VMEM((n, count, width), bf16),
            targets=VMEM((n, depth, 2 * slim), bf16), w_feed_in=VMEM((n, depth, 2 * slim), bf16), cross_out=DMA((3,)),
            ring_b=gather_scratch(n), ring_low=gather_scratch(n), sums_a=scatter_scratch(n, count, width),
            feed_in=share_scratch(n),
        ),
    )


def norm_back(values, gain, grad):
    r = lax.rsqrt(jnp.mean(values * values, axis=-1, keepdims=True) + epsilon)
    scaled = grad * gain
    inner = jnp.mean(values * scaled, axis=-1, keepdims=True)
    return r * scaled - values * (r * r * r * inner), grad * values * r


def gelu_pair(v):
    c = 0.7978845608028654
    square = v * v
    t = jnp.tanh(c * v * (1.0 + 0.044715 * square))
    value = 0.5 * v * (1.0 + t)
    slope = 0.5 * (1.0 + t) + 0.5 * c * v * (1.0 - t * t) * (1.0 + 3.0 * 0.044715 * square)
    return value, slope


def feed_stage(n, ndp, span, depth, count, width, slim):
    length = n * count

    def body(place, v, behind, first):
        loads = [
            pltpu.make_async_copy(v._low_all, v.low_b, v.feed_load.at[0]),
            pltpu.make_async_copy(v._w_feed, v.w_feed, v.feed_load.at[1]),
        ]
        for load in loads:
            load.start()
        gain = gain_row(v.marks, 5, depth)
        if first:
            greet(place.others() + peers(place, ndp))

        def produce(chip):
            return mm(own_part(place, v.o2[rows_of(chip, count), :], span).astype(bf16), v.out_cross[...])

        def finish(k, value):
            rows = piece_rows(k, count)
            value = value + v.resid_one[rows, :]
            v.resid_two[rows, :] = value
            v.normed_c[place.me, rows, :] = normalise(value, gain).astype(bf16)

        def feed(chip):
            rows = rows_of(chip, count)
            both = mm(chip_rows(v.normed_c, chip), v.w_feed[...].reshape(width, 2 * slim))
            gate, upward = both[:, :slim], both[:, slim:]
            value, slope = gelu_pair(gate)
            grad = mm_nt(chip_rows(v.low_b, chip), v.down[...])
            v.hidden[rows, :] = (value * upward).astype(bf16)
            v.d_both[rows, :] = jnp.concatenate([grad * upward * slope, grad * value], axis=1).astype(bf16)

        def produce_back(chip):
            return mm_nt(v.d_both[rows_of(chip, count), :], v.w_feed[...].reshape(width, 2 * slim))

        def finish_back(k, value):
            rows = piece_rows(k, count)
            grad, part = norm_back(v.resid_two[rows, :], gain, value)
            v.grad_two[rows, :] = v.low_b[place.me, rows, :].astype(f32) + grad
            part = jnp.sum(part, axis=0, keepdims=True)
            v.tip_three[...] = part if k == 0 else v.tip_three[...] + part

        def weight_grads():
            step = 256
            for start in range(0, width, step):
                columns = slice(start, start + step)
                left = v.normed_c[:, :, columns].reshape(length, step)
                v.feed_grad[columns, :] = mm_tn(left, v.d_both[...]).astype(bf16)
                yield
                left = v.low_b[:, :, columns].reshape(length, step)
                v.down_grad[:, columns] = mm_tn(v.hidden[...], left).astype(bf16)
                yield

        beside(scatter(place, v.sums_c, produce, finish), behind)
        for load in loads:
            load.wait()
        beside(gather(place, v.normed_c, v.ring_c, feed), behind)
        grads = weight_grads()
        beside(scatter(place, v.sums_c, produce_back, finish_back), in_turn(behind, grads))
        drain(grads)
        return behind

    return Stage(
        body,
        ["o2", "out_cross", "resid_one", "marks", "_w_feed", "down", "_low_all"],
        dict(
            resid_two=shape(count, width, kind=f32), grad_two=shape(count, width, kind=f32),
            tip_three=shape(1, width, kind=f32), hidden=shape(length, slim), feed_grad=shape(width, 2 * slim),
            down_grad=shape(slim, width),
        ),
        dict(
            normed_c=VMEM((n, count, width), bf16), low_b=VMEM((n, count, width), bf16),
            w_feed=VMEM((n, depth, 2 * slim), bf16), d_both=VMEM((length, 2 * slim), bf16), feed_load=DMA((2,)),
            ring_c=gather_scratch(n), sums_c=scatter_scratch(n, count, width),
        ),
    )


def own_grads(place, span, sources, target):
    step = 256
    for start in range(0, target.shape[0], step):
        rows = slice(start, start + step)
        parts = [own_part(place, source[rows, :].astype(bf16), span) for source in sources]
        target[rows, :] = jnp.concatenate(parts, axis=1)


def cross_back_stage(n, ndp, span, depth, count, width, slim):
    length = n * count

    def body(place, v, behind, first):
        v.low_c[place.me] = v.grad_two[...].astype(bf16)
        v.out_sum_c[...] = jnp.zeros_like(v.out_sum_c)
        if first:
            greet(place.others() + peers(place, ndp))

        def into(chip):
            block, rows = chip_rows(v.low_c, chip), rows_of(chip, count)
            v.d_attn_c[rows, :] = mm_nt(block, v.out_cross_head[...]).astype(bf16)
            v.out_sum_c[...] += mm_tn(own_part(place, v.o2[rows, :], span).astype(bf16), block)

        def produce(chip):
            return mm(v.hidden[rows_of(chip, count), :], v.down[...])

        def finish(k, value):
            rows = piece_rows(k, count)
            v.mixed[rows, :] = (v.resid_two[rows, :] + value).astype(bf16)

        def feed_rows(device):
            return v.feed_grad.at[pl.ds(pl.multiple_of(device * depth, depth), depth), :]

        feeds, *feed_sems = v.feed_back
        downs, *down_sems = v.down_back
        behind = in_turn(
            behind,
            scatter(place, v.sums_d, produce, finish),
            settle_blocks(place, ndp, feed_rows, feeds, feed_sems),
            settle_rows(place, ndp, (v.down_grad,), downs, down_sems),
        )
        beside(gather(place, v.low_c, v.ring_d, into), behind)
        row, column = mark_row(v.marks, 0), mark_columns(v.marks, 2)
        attention = attend_backward(
            False, v.q2, v.k2, v.v2, v.d_attn_c, v.o2, v.l2, row, column, v.d_attn_c, v.dk_c, v.dv_c
        )
        beside(attention, behind, 3)
        drain(behind)
        v.saves.append(pltpu.make_async_copy(feeds, v._feeds, v.back_out.at[0]))
        v.saves.append(pltpu.make_async_copy(downs, v._downs, v.back_out.at[1]))
        for copy in v.saves[-2:]:
            copy.start()
        own_grads(place, span, (v.d_attn_c,), v.dq2)
        own_grads(place, span, (v.dk_c, v.dv_c), v.dkv2)
        v.out_two[...] = v.out_sum_c[...].astype(bf16)
        return iter(())

    return Stage(
        body,
        ["grad_two", "out_cross_head", "o2", "l2", "q2", "k2", "v2", "marks", "hidden", "down", "resid_two", "feed_grad"]
        + ["down_grad"],
        dict(
            dq2=shape(length, span), dkv2=shape(length, 2 * span), out_two=shape(span, width), mixed=shape(count, width),
            _feeds=shape(ndp, n, depth, 2 * slim), _downs=shape(ndp, slim, width),
        ),
        dict(
            low_c=VMEM((n, count, width), bf16), d_attn_c=VMEM((length, HEAD_DIM), bf16),
            dk_c=VMEM((length, HEAD_DIM), f32), dv_c=VMEM((length, HEAD_DIM), f32),
            out_sum_c=VMEM((span, width), f32), back_out=DMA((2,)), ring_d=gather_scratch(n),
            sums_d=scatter_scratch(n, count, width), feed_back=settle_blocks_scratch(n, ndp, (depth, 2 * slim), bf16),
            down_back=settle_rows_scratch(ndp, slim, width, 1),
        ),
    )


def self_back_stage(n, ndp, span, depth, count, width, slim):
    length = n * count
    roomy = n <= 16

    def body(place, v, behind, first):
        lane = lax.rem(place.me, LANES // span)
        mine, wide, landed, *column_sems = v.columns_e
        outs, *out_sems = v.outs_e
        loads = [
            pltpu.make_async_copy(ref, v.saved, v.self_load.at[i]) for i, ref in enumerate((v._normed_two, v._encoded))
        ]
        loads[0].start()
        gain = gain_row(v.marks, 4, depth)
        v.out_sum_e[...] = jnp.zeros_like(v.out_sum_e)
        v.w_cq_own[...] = own_part(place, v.w_cq[...], span)
        if first:
            greet(place.others() + peers(place, ndp))

        def produce(chip):
            return mm_nt(v.dq2[rows_of(chip, count), :], v.w_cq_own[...])

        def finish(k, value):
            rows = piece_rows(k, count)
            grad, part = norm_back(v.resid_one[rows, :], gain, value)
            grad = v.grad_two[rows, :] + grad
            v.grad_one[rows, :] = grad
            v.low_e[place.me, rows, :] = grad.astype(bf16)
            part = jnp.sum(part, axis=0, keepdims=True)
            v.tip_two[...] = part if k == 0 else v.tip_two[...] + part

        def weight_grads():
            step = 256
            loads[0].wait()
            for start in range(0, width, step):
                columns = slice(start, start + step)
                left = v.saved[:, :, columns].reshape(length, step)
                mine[0, lane, columns, :] = mm_tn(left, v.dq2[...]).astype(bf16)
                yield
            loads[1].start()
            yield
            loads[1].wait()
            for start in range(0, width, step):
                columns = slice(start, start + step)
                left = v.saved[:, :, columns].reshape(length, step)
                value = mm_tn(left, v.dkv2[...]).astype(bf16)
                mine[1, lane, columns, :] = value[:, :span]
                mine[2, lane, columns, :] = value[:, span:]
                yield

        def into(chip):
            block, rows = chip_rows(v.low_e, chip), rows_of(chip, count)
            v.d_attn_e[rows, :] = mm_nt(block, v.out_self_head[...]).astype(bf16)
            v.out_sum_e[...] += mm_tn(own_part(place, v.o1[rows, :], span).astype(bf16), block)

        def produce_enc(chip):
            return mm_nt(v.dkv2[rows_of(chip, count), :], v.w_ckv_own[...])

        def finish_enc(k, value):
            v.enc_grad[piece_rows(k, count), :] = value

        def columns():
            yield from settle_columns(place, ndp, span, mine, wide, landed, column_sems)
            v.saves.append(pltpu.make_async_copy(landed, v._columns_two, v.self_load.at[2]))
            v.saves[-1].start()

        def rests():
            yield from settle_rows(place, ndp, (v.out_two,), outs, out_sems)
            v.saves.append(pltpu.make_async_copy(outs, v._outs_two, v.self_load.at[3]))
            v.saves[-1].start()

        grads = weight_grads()
        beside(scatter(place, v.sums_e, produce, finish), in_turn(behind, grads))
        drain(grads)
        encs = scatter(place, v.sums_f if roomy else v.sums_e, produce_enc, finish_enc)
        behind = in_turn(behind, columns(), rests(), *([encs] if roomy else []))
        beside(gather(place, v.low_e, v.ring_e, into), behind)
        if not roomy:
            behind = in_turn(behind, encs)
        row, column = mark_row(v.marks, 0), mark_columns(v.marks, 1)
        attention = attend_backward(
            True, v.q1, v.k1, v.v1, v.d_attn_e, v.o1, v.l1, row, column, v.d_attn_e, v.dk_e, v.dv_e
        )
        beside(attention, behind, 2)
        own_grads(place, span, (v.d_attn_e, v.dk_e, v.dv_e), v.grads_one)
        v.out_one[...] = v.out_sum_e[...].astype(bf16)
        return behind

    rows = shape(count, width, kind=f32)
    return Stage(
        body,
        ["dq2", "dkv2", "w_cq", "w_ckv_own", "resid_one", "grad_two", "marks", "out_self_head", "o1", "l1", "q1", "k1", "v1"]
        + ["out_two", "_normed_two", "_encoded"],
        dict(
            grads_one=shape(length, 3 * span), out_one=shape(span, width), grad_one=rows, enc_grad=rows,
            tip_two=shape(1, width, kind=f32), _columns_two=shape(ndp, 3, depth, width), _outs_two=shape(ndp, span, width),
        ),
        dict(
            saved=VMEM((n, count, width), bf16), low_e=VMEM((n, count, width), bf16),
            d_attn_e=VMEM((length, HEAD_DIM), bf16),
            dk_e=VMEM((length, HEAD_DIM), f32), dv_e=VMEM((length, HEAD_DIM), f32), out_sum_e=VMEM((span, width), f32),
            w_cq_own=VMEM((width, span), bf16), self_load=DMA((4,)), ring_e=gather_scratch(n),
            sums_e=scatter_scratch(n, count, width),
            columns_e=settle_columns_scratch(n, ndp, span, depth, width, 3), outs_e=settle_rows_scratch(ndp, span, width, 1),
            **(dict(sums_f=scatter_scratch(n, count, width)) if roomy else {}),
        ),
    )


def close_stage(n, ndp, span, depth, count, width, slim):
    length = n * count
    mates = LANES // span

    def body(place, v, behind, first):
        lane = lax.rem(place.me, mates)
        mine, wide, landed, *column_sems = v.columns_g
        outs, *out_sems = v.outs_g
        tips, *tip_sems = v.tips_g
        load = pltpu.make_async_copy(v._normed_one, v.saved, v.close_load.at[0])
        load.start()
        gain = gain_row(v.marks, 3, depth)
        v.tip_all[...] = jnp.zeros_like(v.tip_all)
        v.tip_all[1:2, :] = v.tip_two[...]
        v.tip_all[2:3, :] = v.tip_three[...]
        if first:
            greet(place.others() + peers(place, ndp))

        def produce(chip):
            return mm_nt(v.grads_one[rows_of(chip, count), :], v.w_self_own[...])

        def finish(k, value):
            rows = piece_rows(k, count)
            grad, part = norm_back(v.x[rows, :].astype(f32), gain, value)
            v.dec_grad[rows, :] = v.grad_one[rows, :] + grad
            v.tip_all[0:1, :] += jnp.sum(part, axis=0, keepdims=True)

        def columns():
            load.wait()
            step = 256
            for start in range(0, width, step):
                columns = slice(start, start + step)
                value = mm_tn(v.saved[:, :, columns].reshape(length, step), v.grads_one[...]).astype(bf16)
                for i in range(3):
                    mine[i, lane, columns, :] = value[:, i * span : (i + 1) * span]
                yield
            yield from settle_columns(place, ndp, span, mine, wide, landed, column_sems)

        def tip(device):
            return v.tip_all.at[:, pl.ds(pl.multiple_of(device // mates * LANES, LANES), LANES)]

        behind = in_turn(columns(), settle_rows(place, ndp, (v.out_one,), outs, out_sems), behind)
        beside(scatter(place, v.sums_e, produce, finish), behind)
        drain(in_turn(settle_blocks(place, ndp, tip, tips, tip_sems), behind))
        for i, (source, target) in enumerate(((landed, v._columns_one), (outs, v._outs_one), (tips, v._tips))):
            v.saves.append(pltpu.make_async_copy(source, target, v.close_load.at[i + 1]))
            v.saves[-1].start()
        return iter(())

    return Stage(
        body,
        ["grads_one", "w_self_own", "x", "grad_one", "marks", "out_one", "tip_two", "tip_three", "_normed_one"],
        dict(
            dec_grad=shape(count, width, kind=f32), _columns_one=shape(ndp, 3, depth, width),
            _outs_one=shape(ndp, span, width), _tips=shape(ndp, n, 8, LANES, kind=f32),
        ),
        dict(
            saved=VMEM((n, count, width), bf16), tip_all=VMEM((8, width), f32), close_load=DMA((4,)),
            sums_e=scatter_scratch(n, count, width), columns_g=settle_columns_scratch(n, ndp, span, depth, width, 3),
            outs_g=settle_rows_scratch(ndp, span, width, 1), tips_g=settle_blocks_scratch(n, ndp, (8, LANES), f32),
        ),
    )


def over_dp(landed, *index):
    return sum(landed[(d, *index)].astype(f32) for d in range(landed.shape[0]))


def total_kernel(
    n, span,
    columns_one, columns_two, outs_one, outs_two, feeds, downs, tips,
    gains_out, q_out, k_out, v_out, out_one, cq_out, ck_out, cv_out, out_two, gate_out, up_out, down_out,
):
    for i, ref in enumerate((q_out, k_out, v_out)):
        ref[...] = over_dp(columns_one, i)
    for i, ref in enumerate((cq_out, ck_out, cv_out)):
        ref[...] = over_dp(columns_two, i)
    out_one[...] = over_dp(outs_one)
    out_two[...] = over_dp(outs_two)
    down_out[...] = over_dp(downs)
    slim = gate_out.shape[1] // n
    for i in range(n):
        piece = over_dp(feeds, i)
        gate_out[:, i * slim : (i + 1) * slim] = piece[:, :slim]
        up_out[:, i * slim : (i + 1) * slim] = piece[:, slim:]
    total = sum(over_dp(tips, i) for i in range(n))
    mates = LANES // span
    lane = lax.rem(lax.axis_index("blk"), mates)
    part = total[:, :span]
    for i in range(1, mates):
        part = jnp.where(lane == i, total[:, i * span : (i + 1) * span], part)
    gains_out[...] = part


def total_grads(n, span, columns_one, columns_two, outs_one, outs_two, feeds, downs, tips):
    depth, width = columns_one.shape[2:]
    slim = downs.shape[1]

    square, out = shape(depth, width, kind=f32), shape(span, width, kind=f32)
    return pl.pallas_call(
        functools.partial(total_kernel, n, span),
        out_shape=(
            shape(8, span, kind=f32), square, square, square, out, square, square, square, out,
            shape(depth, n * slim, kind=f32), shape(depth, n * slim, kind=f32), shape(slim, width, kind=f32),
        ),
        compiler_params=pltpu.CompilerParams(vmem_limit_bytes=40 * 1024 * 1024),
        name="total_grads",
    )(columns_one, columns_two, outs_one, outs_two, feeds, downs, tips)


def local(
    n,
    ndp,
    dec_in,
    enc_out,
    cotangent,
    dec_seg,
    dec_valid,
    enc_seg,
    enc_valid,
    self_gain,
    self_query,
    self_key,
    self_value,
    self_out,
    cross_gain,
    cross_query,
    cross_key,
    cross_value,
    cross_out,
    feed_gain,
    feed_gate,
    feed_up,
    feed_down,
):
    width = dec_in.shape[2]
    depth = self_query.shape[0]
    span = width // n
    share = HEAD_DIM // span

    def whole_head(weight):
        if share == 1:
            return weight
        groups = [[h * share + i for i in range(share)] for h in range(n // share)]
        return lax.all_gather(weight, "blk", axis=0, tiled=True, axis_index_groups=groups)

    count, slim = dec_in.shape[1], feed_gate.shape[1] // n
    arrays = dict(
        x=dec_in[0], enc=enc_out[0], cotangent=cotangent[0],
        dec_seg=dec_seg, dec_valid=dec_valid, enc_seg=enc_seg, enc_valid=enc_valid,
        gain_self=self_gain[None], gain_cross=cross_gain[None], gain_feed=feed_gain[None],
        wq=self_query, wk=self_key, wv=self_value, wcq=cross_query, wck=cross_key, wcv=cross_value,
        out_self=self_out, out_cross=cross_out, gate=feed_gate, up=feed_up, down=feed_down,
        out_self_head=whole_head(self_out), out_cross_head=whole_head(cross_out),
    )
    stages = [
        (name, make(n, ndp, span, depth, count, width, slim))
        for name, make in (
            ("open", open_stage), ("cross", cross_stage), ("feed", feed_stage),
            ("cross_back", cross_back_stage), ("self_back", self_back_stage), ("close", close_stage),
        )
    ]
    size = 2 if n <= 16 else 1
    results = {"mixed", "dec_grad", "enc_grad", "_columns_one", "_columns_two", "_outs_one", "_outs_two"}
    results |= {"_feeds", "_downs", "_tips"}
    for at in range(0, len(stages), size):
        later = {key for _, stage in stages[at + size :] for key in stage.inputs}
        group = stages[at : at + size]
        name = "_and_".join(key for key, _ in group)
        fused(name, at, n, ndp, [stage for _, stage in group], arrays, later | results)
    gains, q, k, v, o, cq, ck, cv, co, gate, up, down = total_grads(
        n, span, *(arrays[key] for key in ("_columns_one", "_columns_two", "_outs_one", "_outs_two", "_feeds", "_downs", "_tips"))
    )
    return (
        arrays["mixed"][None], arrays["dec_grad"][None], arrays["enc_grad"][None],
        gains[0], q, k, v, o,
        gains[1], cq, ck, cv, co,
        gains[2], gate, up, down,
    )


def solution(mesh):
    row, token = P("dp", "blk"), P("dp", "blk", None)
    gain, weight = P("blk"), P("blk", None)
    return jax.shard_map(
        functools.partial(local, mesh.shape["blk"], mesh.shape["dp"]),
        mesh=mesh,
        in_specs=(token,) * 3 + (row,) * 4 + ((gain,) + (weight,) * 4) * 2 + (gain,) + (weight,) * 3,
        out_specs=(token,) * 3 + ((gain,) + (weight,) * 4) * 2 + (gain,) + (weight,) * 3,
        check_vma=False,
    )
```

```python
import functools
import types

import jax
import jax.numpy as jnp
from jax import lax
from jax.experimental import pallas as pl
from jax.experimental.pallas import tpu as pltpu
from jax.sharding import PartitionSpec as P

HEADS = 16
HEAD_DIM = 64
LANES = 128
PIECES = 2
epsilon = 1e-06
negative = -1e30
MESH = pl.DeviceIdType.MESH
bf16 = jnp.bfloat16
f32 = jnp.float32
VMEM = pltpu.VMEM
DMA = pltpu.SemaphoreType.DMA


def contract(left, right, dims):
    return lax.dot_general(left, right, ((dims[:1], dims[1:]), ((), ())), preferred_element_type=f32)


def mm(left, right):
    return contract(left, right, (1, 0))


def mm_nt(left, right):
    return contract(left, right, (1, 1))


def mm_tn(left, right):
    return contract(left, right, (0, 0))


class Place:
    def __init__(self, n):
        self.n, self.chips = n, n // 2
        self.half = self.chips // 2
        self.dp, self.me = lax.axis_index("dp"), lax.axis_index("blk")
        self.core = lax.rem(self.me, 2)
        chip = self.me // 2
        y, z = lax.rem(chip, 2), chip // 2
        self.pos = z + y * (self.chips - 1 - 2 * z)
        self.sibling = (self.dp, self.me + 1 - 2 * self.core)
        self.half_row = lax.rem(self.dp, 2)
        self.twin = (self.dp + 1 - 2 * self.half_row, self.me)
        self.sides = tuple((self.dp, 2 * self.chip(step) + self.core) for step in (1, -1))

    def chip(self, offset):
        position = lax.rem(self.pos + offset + 2 * self.chips, self.chips)
        side = position // (self.chips // 2)
        return 2 * (position + side * (self.chips - 1 - 2 * position)) + side

    def others(self):
        return [(self.dp, lax.rem(self.me + k, self.n)) for k in range(1, self.n)]

    def around(self):
        return [self.sibling, *self.sides]


def greet(partners):
    barrier = pltpu.get_barrier_semaphore()
    for partner in partners:
        pl.semaphore_signal(barrier, inc=1, device_id=partner, device_id_type=MESH)
    pl.semaphore_wait(barrier, len(partners))


def remote(src, dst, send, recv, device):
    return pltpu.make_async_remote_copy(
        src_ref=src, dst_ref=dst, send_sem=send, recv_sem=recv, device_id=device, device_id_type=MESH
    )


def wait_sent(ref, sem, device):
    remote(ref, ref, sem, sem, device).wait_send()


def wait_landed(ref, sem, device):
    remote(ref, ref, sem, sem, device).wait_recv()


def pieces_of(half, way, step):
    if step < half - 1:
        return tuple(range(PIECES))
    return tuple(range(PIECES // 2)) if way == 0 else tuple(range(PIECES // 2, PIECES))


def drain(task):
    for _ in task:
        pass


def beside(main, task, waits=1, steps=1):
    for count, _ in enumerate(main):
        if (count + 1) % steps == 0:
            for _ in range(waits):
                next(task, None)


def in_turn(*tasks):
    tasks = list(tasks)
    while tasks:
        for task in list(tasks):
            if next(task, "done") == "done":
                tasks.remove(task)
            else:
                yield


def one_by_one(*tasks):
    for task in tasks:
        yield from task


def gather_scratch(n):
    half = n // 4
    return [DMA, DMA((2, half, PIECES)), DMA, DMA((n // 2,))]


def gather(place, buf, sems, use=None):
    ring_send, ring_recv, sib_send, sib_recv = sems
    half, part = place.half, buf.shape[1] // PIECES

    def ring(way, step, k):
        ref = buf.at[2 * place.chip(-step if way == 0 else step) + place.core, pl.ds(k * part, part)]
        return remote(ref, ref, ring_send, ring_recv.at[way, step, k], place.sides[way])

    def across(offset):
        ref = buf.at[2 * place.chip(offset) + place.core]
        return remote(ref, ref, sib_send, sib_recv.at[offset + half - 1], place.sibling)

    def ready(offset):
        across(offset).wait_recv()
        if use is not None:
            use(place.chip(offset))

    for i in range(PIECES):
        for way in (0, 1):
            k = i if way == 0 else PIECES - 1 - i
            if k in pieces_of(half, way, 0):
                ring(way, 0, k).start()
    across(0).start()
    for step in range(half):
        for i in range(PIECES):
            for way in (0, 1):
                k = i if way == 0 else PIECES - 1 - i
                if k not in pieces_of(half, way, step):
                    continue
                yield
                ring(way, step, k).wait_recv()
                if step + 1 < half and k in pieces_of(half, way, step + 1):
                    ring(way, step + 1, k).start()
                if step + 1 < half and i == PIECES - 1:
                    across(-1 - step if way == 0 else step + 1).start()
        if step + 1 == half:
            across(half).start()
        for way in (0, 1) if step else (0,):
            ready(-step if way == 0 else step)
    yield
    ready(half)
    wait_sent(buf.at[pl.ds(0, place.chips - 1)], ring_send, place.sides[0])
    wait_sent(buf.at[pl.ds(0, place.chips)], sib_send, place.sibling)


def scatter_scratch(n, rows, columns):
    half = n // 4
    return [
        VMEM((n, rows, columns), bf16),
        VMEM((n // 2, rows, columns), bf16),
        VMEM((2, half, PIECES, rows // PIECES, columns), bf16),
        VMEM((2, half, PIECES, rows // PIECES, columns), bf16),
        DMA,
        DMA((2, half, PIECES)),
        DMA,
        DMA((n // 2,)),
    ]


def scatter(place, scratch, produce, finish):
    blocks, theirs, held, landed, ring_send, ring_recv, sib_send, sib_recv = scratch
    half, rows = place.half, blocks.shape[1]
    part = rows // PIECES

    def across(offset):
        chip = place.chip(offset)
        return remote(
            blocks.at[2 * chip + 1 - place.core], theirs.at[chip], sib_send, sib_recv.at[offset + half - 1], place.sibling
        )

    def make(offset):
        chip = place.chip(offset)
        value = produce(chip).astype(bf16)
        blocks[2 * chip] = value[:rows]
        blocks[2 * chip + 1] = value[rows:]
        across(offset).start()

    def ring(way, step, k):
        return remote(
            held.at[way, step, k], landed.at[way, step, k], ring_send, ring_recv.at[way, step, k], place.sides[way]
        )

    def mine(offset, k):
        chip, window = place.chip(offset), pl.ds(k * part, part)
        return blocks[2 * chip + place.core, window, :].astype(f32) + theirs[chip, window, :].astype(f32)

    first = [pieces_of(half, way, half - 1) for way in (0, 1)]
    make(half)
    for step in range(half):
        left = half - 1 - step
        for offset in (left, -left) if left else (0,):
            make(offset)
        yield
        across(half - step).wait_recv()
        if step:
            across(step - half).wait_recv()
        for i in range(PIECES):
            for way in (0, 1):
                k = i if way == 0 else PIECES - 1 - i
                if step == 0 and k not in first[way]:
                    continue
                offset = half if step == 0 else half - step if way == 0 else step - half
                value = mine(offset, k)
                if step >= 2 or (step == 1 and k in first[way]):
                    yield
                    ring(way, step - 1, k).wait_recv()
                    value = value + landed[way, step - 1, k].astype(f32)
                held[way, step, k] = value.astype(bf16)
                ring(way, step, k).start()
    yield
    across(0).wait_recv()
    for k in range(PIECES):
        value = mine(0, k)
        for way in (0, 1):
            yield
            ring(way, half - 1, k).wait_recv()
            value = value + landed[way, half - 1, k].astype(f32)
        finish(k, value)
    wait_sent(theirs.at[pl.ds(0, place.chips - 1)], ring_send, place.sides[0])
    wait_sent(theirs, sib_send, place.sibling)


def mark_row(marks, which):
    return jnp.concatenate([marks[i, which : which + 1, :] for i in range(marks.shape[0])], axis=1).astype(f32)


def mark_columns(marks, which):
    n = marks.shape[0]
    rows = jnp.concatenate([marks[i, which : which + 1, :].astype(f32) for i in range(n)], axis=0)
    rows = jnp.concatenate([rows, jnp.zeros((LANES - n, LANES), f32)], axis=0)
    return rows.T


def column_of(columns, first, count):
    blocks = count // LANES
    return jnp.concatenate([columns[:, first // LANES + i : first // LANES + i + 1] for i in range(blocks)], axis=0)


def gain_row(marks, which, depth):
    return jnp.concatenate(
        [marks[i, which : which + 1, :].astype(f32)[:, :depth] for i in range(marks.shape[0])], axis=1
    )


def normalise(values, gain):
    return values * lax.rsqrt(jnp.mean(values * values, axis=-1, keepdims=True) + epsilon) * gain


def tile_of(length):
    return 256 if length <= 2048 else 128


def attend_forward(causal, q_ref, k_ref, v_ref, query_column, key_row, o_ref, l_ref):
    length = q_ref.shape[0]
    tile = tile_of(length)

    def one(start, reach, column):
        rows = pl.ds(start, tile)
        scores = mm_nt(q_ref[rows, :], k_ref[:reach, :])
        keep = column == key_row[:, :reach]
        if causal:
            keep = keep & (
                lax.broadcasted_iota(jnp.int32, (tile, reach), 1)
                <= lax.broadcasted_iota(jnp.int32, (tile, reach), 0) + start
            )
        scores = jnp.where(keep, scores, negative)
        top = jnp.max(scores, axis=1, keepdims=True)
        weights = jnp.exp(scores - top)
        total = jnp.sum(weights, axis=1, keepdims=True)
        o_ref[rows, :] = mm(weights.astype(bf16), v_ref[:reach, :]) / total
        l_ref[:, rows] = jnp.broadcast_to(top + jnp.log(total), (tile, LANES)).T[:1, :]

    if tile == LANES and not causal:

        @pl.loop(0, length // tile)
        def _(i):
            lanes = lax.broadcasted_iota(jnp.int32, query_column.shape, 1)
            column = jnp.sum(jnp.where(lanes == i, query_column, 0.0), axis=1, keepdims=True)
            one(pl.multiple_of(i * tile, tile), length, column)

        return
    for start in range(0, length, tile):
        one(start, start + tile if causal else length, column_of(query_column, start, tile))
        yield


def attend_backward(
    causal, q_ref, k_ref, v_ref, g_ref, o_ref, l_ref, query_row, key_column, dq_ref, dk_sum, dv_sum
):
    length = q_ref.shape[0]
    tile = tile_of(length)
    dk_sum[...] = jnp.zeros_like(dk_sum)
    dv_sum[...] = jnp.zeros_like(dv_sum)
    for start in range(0, length, tile):
        reach = start + tile if causal else length
        rows = slice(start, start + tile)
        queries, grads = q_ref[rows, :], g_ref[rows, :]
        spread = jnp.sum(grads.astype(f32) * o_ref[rows, :], axis=1, keepdims=True)
        spread = jnp.broadcast_to(spread, (tile, LANES)).T[:1, :]
        dq = 0.0
        for begin in range(0, reach, 2048):
            part = slice(begin, min(reach, begin + 2048))
            keys = k_ref[part, :]
            count = keys.shape[0]
            scores = mm_nt(keys, queries)
            keep = column_of(key_column, begin, count) == query_row[:, rows]
            if causal:
                keep = keep & (
                    lax.broadcasted_iota(jnp.int32, (count, tile), 0) + begin
                    <= lax.broadcasted_iota(jnp.int32, (count, tile), 1) + start
                )
            probs = jnp.where(keep, jnp.exp(scores - l_ref[:, rows]), 0.0)
            dprobs = mm_nt(v_ref[part, :], grads)
            dscores = (probs * (dprobs - spread)).astype(bf16)
            dk_sum[part, :] += mm(dscores, queries)
            dv_sum[part, :] += mm(probs.astype(bf16), grads)
            dq = dq + mm_tn(dscores, keys)
        dq_ref[rows, :] = (dq * HEAD_DIM ** (-0.5)).astype(bf16)
        yield


class Stage:
    def __init__(self, body, inputs, outputs, scratch):
        self.body, self.inputs, self.outputs, self.scratch = body, inputs, outputs, scratch


def fused(name, collective_id, n, ndp, stages, arrays, wanted):
    outputs, scratch = {}, {}
    for stage in stages:
        outputs.update(stage.outputs)
        scratch.update(stage.scratch)
    inputs = [x for stage in stages for x in stage.inputs if x not in outputs]
    inputs = list(dict.fromkeys(inputs))
    for key in list(outputs):
        if key not in wanted:
            scratch[key] = VMEM(outputs[key].shape, outputs.pop(key).dtype)

    def specs(names):
        return tuple(pl.BlockSpec(memory_space=pl.ANY if x.startswith("_") else VMEM) for x in names)

    flat, slots = [], {}
    for key, value in scratch.items():
        many = isinstance(value, list)
        items = value if many else [value]
        slots[key] = (len(flat), len(items), many)
        flat += items

    def kernel(*refs):
        table = dict(zip(inputs + list(outputs), refs))
        rest = refs[len(inputs) + len(outputs) :]
        for key, (at, length, many) in slots.items():
            table[key] = rest[at : at + length] if many else rest[at]
        table["saves"] = []
        place = Place(n)
        view = types.SimpleNamespace(**table)
        behind = iter(())
        for number, stage in enumerate(stages):
            behind = stage.body(place, view, behind, number == 0)
        drain(behind)
        for copy in view.saves:
            copy.wait()

    results = pl.pallas_call(
        kernel,
        out_shape=tuple(outputs.values()),
        in_specs=specs(inputs),
        out_specs=specs(outputs),
        scratch_shapes=flat,
        compiler_params=pltpu.CompilerParams(
            collective_id=collective_id, has_side_effects=True, vmem_limit_bytes=(58 if n <= 16 else 62) * 1024 * 1024
        ),
        name=name,
    )(*[arrays[x] for x in inputs])
    arrays.update(zip(outputs, results))


def shape(*dims, kind=bf16):
    return jax.ShapeDtypeStruct(dims, kind)


def settle_columns(place, ndp, span, mine, wide, landed, sems):
    mate_send, mate_recv, own_sem, send, recv, dp_send, dp_recv = sems
    matrices, mates, width, _ = mine.shape
    groups = place.n // mates
    depth = landed.shape[2]
    group, lane = place.me // mates, lax.rem(place.me, mates)

    def swap(r):
        mate = group * mates + lax.rem(lane + r, mates)
        ref = mine.at[:, lane]
        return remote(ref, ref, mate_send.at[r - 1], mate_recv.at[r - 1], (place.dp, mate))

    def rows(device):
        return wide.at[:, pl.ds(pl.multiple_of(device * depth, depth), depth), :]

    def lanes(origin):
        return landed.at[place.dp, :, :, pl.ds(pl.multiple_of(origin * LANES, LANES), LANES)]

    def move(step):
        target = lax.rem(group + step, groups) * mates + lane
        return remote(rows(target), lanes(group), send, recv.at[step - 1], (place.dp, target))

    def peer(r):
        return (lax.rem(place.dp + r, ndp), place.me)

    def pass_on(ref, origin):
        for r in range(1, ndp):
            remote(ref, lanes(origin), dp_send.at[r - 1], dp_recv.at[r - 1], peer(r)).start()

    for r in range(1, mates):
        swap(r).start()
    yield
    for r in range(1, mates):
        swap(r).wait_recv()
    for m in range(matrices):
        wide[m] = jnp.concatenate([mine[m, i] for i in range(mates)], axis=1)
    for step in range(1, groups):
        move(step).start()
    own = pltpu.make_async_copy(rows(place.me), lanes(group), own_sem)
    own.start()
    pass_on(rows(place.me), group)
    for step in range(1, groups):
        yield
        move(step).wait_recv()
        origin = lax.rem(group + groups - step, groups)
        pass_on(lanes(origin), origin)
    yield
    own.wait()
    for r in range(1, mates):
        swap(r).wait_send()
    wait_sent(wide.at[:, pl.ds(0, (groups - 1) * depth), :], send, place.sibling)
    for r in range(1, ndp):
        wait_sent(landed.at[0], dp_send.at[r - 1], peer(r))
        wait_landed(landed.at[0], dp_recv.at[r - 1], peer(r))


def settle_columns_scratch(n, ndp, span, depth, width, matrices):
    mates = LANES // span
    groups = n // mates
    return [
        VMEM((matrices, mates, width, span), bf16),
        VMEM((matrices, width, LANES), bf16),
        VMEM((ndp, matrices, depth, width), bf16),
        DMA((mates - 1,)),
        DMA((mates - 1,)),
        DMA,
        DMA,
        DMA((groups - 1,)),
        DMA((ndp - 1,)),
        DMA((ndp - 1,)),
    ]


def settle_blocks(place, ndp, source, landed, sems):
    own_sem, send, recv, dp_send, dp_recv = sems
    n = place.n

    def move(k):
        target = lax.rem(place.me + k, n)
        return remote(source(target), landed.at[place.dp, place.me], send, recv.at[k - 1], (place.dp, target))

    def peer(r):
        return (lax.rem(place.dp + r, ndp), place.me)

    def pass_on(ref, origin):
        for r in range(1, ndp):
            remote(ref, landed.at[place.dp, origin], dp_send.at[r - 1], dp_recv.at[r - 1], peer(r)).start()

    window = 4
    for k in range(1, window):
        move(k).start()
    own = pltpu.make_async_copy(source(place.me), landed.at[place.dp, place.me], own_sem)
    own.start()
    pass_on(source(place.me), place.me)
    for k in range(1, n):
        yield
        if k + window - 1 < n:
            move(k + window - 1).start()
        move(k).wait_recv()
        origin = lax.rem(place.me + n - k, n)
        pass_on(landed.at[place.dp, origin], origin)
    yield
    own.wait()
    wait_sent(landed.at[0, pl.ds(0, n - 1)], send, place.sibling)
    for r in range(1, ndp):
        wait_sent(landed.at[0], dp_send.at[r - 1], peer(r))
        wait_landed(landed.at[0], dp_recv.at[r - 1], peer(r))


def settle_blocks_scratch(n, ndp, block, kind):
    return [VMEM((ndp, n) + block, kind), DMA, DMA, DMA((n - 1,)), DMA((ndp - 1,)), DMA((ndp - 1,))]


def settle_tips(place, ndp, source, landed, sems):
    own_sem, send, recv = sems
    n = place.n
    here = place.dp * n + place.me
    for r in range(ndp):
        for k in range(n):
            if r or k:
                target = (lax.rem(place.dp + r, ndp), lax.rem(place.me + k, n))
                remote(source(target[1]), landed.at[here], send, recv, target).start()
    own = pltpu.make_async_copy(source(place.me), landed.at[here], own_sem)
    own.start()
    yield
    own.wait()
    wait_landed(landed.at[pl.ds(0, ndp * n - 1)], recv, place.sibling)
    wait_sent(landed.at[pl.ds(0, ndp * n - 1)], send, place.sibling)


def settle_rows(place, ndp, parts, landed, sems):
    send, recv = sems
    copies, at = [], 0
    for i, part in enumerate(parts):
        window = pl.ds(at, part.shape[0])
        at += part.shape[0]
        for r in range(1, ndp):
            peer = lax.rem(place.dp + r, ndp)
            copy = remote(
                part, landed.at[place.dp, window], send.at[i, r - 1], recv.at[i, r - 1], (peer, place.me)
            )
            copy.start()
            copies.append(copy)
        landed[place.dp, window] = part[...]
    yield
    for copy in copies:
        copy.wait()


def settle_tips_scratch(n, ndp):
    return [VMEM((ndp * n, 8, LANES), f32), DMA, DMA, DMA]


def settle_rows_scratch(ndp, rows, width, parts):
    return [VMEM((ndp, rows, width), bf16), DMA((parts, ndp - 1)), DMA((parts, ndp - 1))]


def peers(place, ndp):
    return [(lax.rem(place.dp + r, ndp), place.me) for r in range(1, ndp)]


def own_part(place, values, span):
    share = HEAD_DIM // span
    part = values[:, :span]
    for i in range(1, share):
        part = jnp.where(lax.rem(place.me, share) == i, values[:, i * span : (i + 1) * span], part)
    return part


def rows_of(chip, count):
    return pl.ds(pl.multiple_of(chip * 2 * count, 2 * count), 2 * count)


def chip_rows(blocks, chip):
    _, count, width = blocks.shape
    return blocks[pl.ds(2 * chip, 2)].reshape(2 * count, width)


def piece_rows(k, count):
    part = count // PIECES
    return slice(k * part, (k + 1) * part)


def columns_task(place, span, stack, buf, first, last, sems):
    own_sem, send, recv, twin_send, twin_recv, pass_send, pass_recv = sems
    mates = LANES // span
    groups = place.n // mates
    depth = stack.shape[1]
    part = depth // 2
    group, lane = place.me // mates, lax.rem(place.me, mates)
    which = pl.ds(first, last - first)

    def lanes(target):
        return pl.ds(pl.multiple_of(target * LANES, LANES), LANES)

    def rows(device, begin, count):
        return buf.at[which, pl.ds(pl.multiple_of(device * depth + begin, part), count), :]

    def half(device, other):
        return rows(device, (1 - place.half_row if other else place.half_row) * part, part)

    def mate(r):
        return (place.dp, group * mates + lax.rem(lane + r, mates))

    def hand(source, target):
        for r in range(1, mates):
            remote(source, target, pass_send.at[r - 1], pass_recv.at[r - 1], mate(r)).start()

    def arrival(step):
        target = lax.rem(group + step, groups)
        source = stack.at[which, pl.ds(pl.multiple_of(place.half_row * part, part), part), lanes(target)]
        return remote(source, half(place.me, 0), send, recv.at[step - 1], (place.dp, target * mates + lane))

    def origin(step):
        return lax.rem(group + groups - step, groups) * mates + lane

    def twin(step):
        ref = half(origin(step), 0)
        return remote(ref, ref, twin_send, twin_recv.at[step - 1], place.twin)

    for step in range(1, groups):
        arrival(step).start()
    mine = stack.at[which, :, lanes(group)]
    own = pltpu.make_async_copy(mine, rows(place.me, 0, depth), own_sem)
    own.start()
    hand(mine, rows(place.me, 0, depth))
    for step in range(1, groups + 1):
        yield
        if step < groups:
            arrival(step).wait_recv()
            twin(step).start()
            ref = half(origin(step), 0)
            hand(ref, ref)
        if step > 1:
            twin(step - 1).wait_recv()
            ref = half(origin(step - 1), 1)
            hand(ref, ref)
    yield
    own.wait()
    sent = buf.at[which, pl.ds(0, (groups - 1) * part), :]
    wait_sent(sent, send, place.sibling)
    wait_sent(sent, twin_send, place.twin)
    for r in range(1, mates):
        passed = buf.at[which, pl.ds(0, groups * depth), :]
        wait_landed(passed, pass_recv.at[r - 1], mate(r))
        wait_sent(passed, pass_send.at[r - 1], mate(r))


def columns_scratch(n, span):
    mates = LANES // span
    groups = n // mates
    return [DMA, DMA, DMA((groups - 1,)), DMA, DMA((groups - 1,)), DMA((mates - 1,)), DMA((mates - 1,))]


def share_blocks(place, blocks, landed, sems, window=4):
    own_sem, send, recv, twin_send, twin_recv = sems
    n, part = place.n, blocks.shape[1] // 2
    rows = pl.ds(pl.multiple_of(place.half_row * part, part), part)

    def move(k):
        target = lax.rem(place.me + k, n)
        return remote(blocks.at[target, rows], landed.at[place.me, rows], send, recv.at[k - 1], (place.dp, target))

    own = pltpu.make_async_copy(blocks.at[place.me], landed.at[place.me], own_sem)
    own.start()
    for k in range(1, window):
        move(k).start()
    for k in range(1, n):
        yield
        if k + window - 1 < n:
            move(k + window - 1).start()
        move(k).wait_recv()
        ref = landed.at[lax.rem(place.me + n - k, n), rows]
        remote(ref, ref, twin_send, twin_recv, place.twin).start()
    yield
    own.wait()
    ref = landed.at[pl.ds(0, n - 1), pl.ds(0, part)]
    wait_landed(ref, twin_recv, place.twin)
    wait_sent(ref, twin_send, place.twin)
    wait_sent(ref, send, place.sibling)


def share_scratch(n):
    return [DMA, DMA, DMA((n - 1,)), DMA, DMA]


def outs_task(place, shards, full, sems):
    ring, (twin_send, twin_recv, sib_send, sib_recv) = sems[:4], sems[4:]
    mine = place.half_row
    full[mine, place.me] = jnp.where(mine == 0, shards[0][...], shards[1][...])
    order = []

    def twin(i):
        ref = full.at[mine, 2 * order[i] + place.core]
        return remote(ref, ref, twin_send, twin_recv.at[i], place.twin)

    def to_twin(chip):
        order.append(chip)
        twin(len(order) - 1).start()

    passed = 0
    for _ in gather(place, full.at[mine], ring, to_twin):
        yield
        if passed + 1 < len(order):
            twin(passed).wait_recv()
            ref = full.at[1 - mine, 2 * order[passed] + place.core]
            remote(ref, ref, sib_send, sib_recv, place.sibling).start()
            passed += 1
    while passed < place.chips:
        yield
        twin(passed).wait_recv()
        ref = full.at[1 - mine, 2 * order[passed] + place.core]
        remote(ref, ref, sib_send, sib_recv, place.sibling).start()
        passed += 1
    yield
    every = full.at[0, pl.ds(0, place.chips)]
    wait_landed(every, sib_recv, place.sibling)
    wait_sent(every, sib_send, place.sibling)
    wait_sent(every, twin_send, place.twin)


def outs_scratch(n):
    return [*gather_scratch(n), DMA, DMA((n // 2,)), DMA, DMA]


def heads_task(place, span, o_ref, own, pairs, heads, sems):
    mate_send, mate_recv, *ring = sems
    mates = LANES // span
    rows = heads.shape[1]
    group, lane = place.me // mates, lax.rem(place.me, mates)
    for start in range(0, own.shape[0], 256):
        own[start : start + 256, :] = own_part(place, o_ref[start : start + 256, :], span).astype(bf16)

    def part(index):
        return own.at[pl.ds(pl.multiple_of(index * rows, rows), rows), :]

    def swap(r):
        other = lax.rem(lane + r, mates)
        return remote(
            part(other), pairs.at[lane], mate_send.at[r - 1], mate_recv.at[r - 1], (place.dp, group * mates + other)
        )

    for r in range(1, mates):
        swap(r).start()
    pairs[lane] = part(lane)[...]
    yield
    for r in range(1, mates):
        swap(r).wait_recv()
    heads[place.me] = jnp.concatenate([pairs[i] for i in range(mates)], axis=1)
    yield from gather(place, heads, ring)
    for r in range(1, mates):
        swap(r).wait_send()


def heads_scratch(n, span, length):
    mates = LANES // span
    return [
        VMEM((length, span), bf16),
        VMEM((mates, length // mates, span), bf16),
        VMEM((n, length // mates, LANES), bf16),
        DMA((mates - 1,)),
        DMA((mates - 1,)),
        *gather_scratch(n),
    ]


def heads_at(heads, mates, lane, start, count):
    return jnp.concatenate([heads[at + lane, pl.ds(start, count), :] for at in range(0, heads.shape[0], mates)], axis=1)


def own_heads(place, heads, mates, count):
    blocks = heads.shape[1] // count
    start = pl.multiple_of(lax.rem(place.me, blocks) * count, count)
    return heads_at(heads, mates, place.me // blocks, start, count)


def roomy_at(n):
    return n <= 16


def open_stage(n, ndp, span, depth, count, width, slim):
    length = n * count
    roomy = roomy_at(n)
    mates = LANES // span

    def body(place, v, behind, first):
        v.x_all[place.me] = v.x[...]
        v.encoded[place.me] = v.enc[...]
        for i, ref in enumerate((v.wq, v.wk, v.wv, v.wcq, v.wck, v.wcv)):
            v.stack[i] = ref[...]
        segment = v.dec_seg[...].astype(f32)
        rows = [segment, jnp.where(v.dec_valid[...] == 1, segment, -1.0)]
        rows.append(jnp.where(v.enc_valid[...] == 1, v.enc_seg[...].astype(f32), -1.0))
        for ref in (v.gain_self, v.gain_cross, v.gain_feed):
            rows.append(jnp.concatenate([ref[...].astype(f32), jnp.zeros((1, LANES - depth), f32)], axis=1))
        rows.append(jnp.zeros((10, LANES), f32))
        v.mark[...] = jnp.concatenate(rows, axis=0).astype(bf16)
        v.marks_in[place.me] = v.mark[...]
        if first:
            greet(place.others() + peers(place, ndp))
        for other in place.others():
            remote(v.mark, v.marks_in.at[place.me], v.mark_send, v.mark_recv, other).start()
        side = lax.rem(place.me, mates) // (HEAD_DIM // span)

        def head(index):
            pair = v.buf[index]
            return jnp.where(side == 0, pair[:, :HEAD_DIM], pair[:, HEAD_DIM:])

        scale = HEAD_DIM ** (-0.5)
        gain, ready, waiting = [], [], []

        def begin(chip):
            if not ready:
                waiting.append(chip)
                return
            for b in (0, 1):
                v.normed_a[2 * chip + b] = normalise(v.x_all[2 * chip + b].astype(f32), gain[0]).astype(bf16)
            rows = rows_of(chip, count)
            qkv = mm(chip_rows(v.normed_a, chip), v.w_self[...])
            v.q1[rows, :] = (qkv[:, :HEAD_DIM].astype(bf16).astype(f32) * scale).astype(bf16)
            v.k1[rows, :] = qkv[:, HEAD_DIM : 2 * HEAD_DIM].astype(bf16)
            v.v1[rows, :] = qkv[:, 2 * HEAD_DIM :].astype(bf16)

        def cross(chip):
            if len(ready) < 2:
                waiting.append(chip)
                return
            rows = rows_of(chip, count)
            kv = mm(chip_rows(v.encoded, chip), v.w_ckv[...])
            v.k2[rows, :] = kv[:, :HEAD_DIM].astype(bf16)
            v.v2[rows, :] = kv[:, HEAD_DIM:].astype(bf16)

        def background():
            weights = columns_task(place, span, v.stack, v.buf, 4, 6, v.late)
            next(weights)
            for _ in gather(place, v.encoded, v.ring_enc, cross):
                yield
                if len(ready) < 2 and next(weights, "done") == "done":
                    v.w_ckv[...] = jnp.concatenate([head(4), head(5)], axis=1)
                    v.w_ckv_own[...] = jnp.concatenate([own_part(place, head(i), span) for i in (4, 5)], axis=1)
                    ready.append(True)
                    for chip in waiting:
                        cross(chip)
            v.saves.append(pltpu.make_async_copy(v.encoded, v._encoded, v.open_out.at[1]))
            v.saves[-1].start()

        def outs():
            yield from outs_task(place, (v.out_self, v.out_cross), v.outs_all, v.outs_in)
            v.saves.append(pltpu.make_async_copy(v.outs_all, v._outs_all, v.open_out.at[2]))
            v.saves[-1].start()

        weights = columns_task(place, span, v.stack, v.buf, 0, 4, v.early)
        next(weights)
        ring = gather(place, v.x_all, v.ring_x, begin)
        v.outs_task = outs()
        behind = one_by_one(behind, v.outs_task, background())
        for number, _ in enumerate(ring):
            if not ready and next(weights, "done") == "done":
                ref = v.marks_in.at[pl.ds(0, n - 1)]
                wait_landed(ref, v.mark_recv, place.sibling)
                wait_sent(ref, v.mark_send, place.sibling)
                v.marks[...] = v.marks_in[...]
                gain.append(gain_row(v.marks, 3, depth))
                v.w_self[...] = jnp.concatenate([head(0), head(1), head(2)], axis=1)
                v.w_self_own[...] = jnp.concatenate([own_part(place, head(i), span) for i in range(3)], axis=1)
                v.w_cq[...] = head(3)
                ready.append(True)
                for chip in waiting:
                    begin(chip)
                waiting.clear()
            elif ready and number % 2:
                next(behind, None)
        v.saves.append(pltpu.make_async_copy(v.normed_a, v._normed_one, v.open_out.at[0]))
        v.saves[-1].start()
        if not roomy:
            v.saves.append(pltpu.make_async_copy(v.x_all, v._x_all, v.open_out.at[3]))
            v.saves[-1].start()
        column, row = mark_columns(v.marks, 0), mark_row(v.marks, 1)
        beside(attend_forward(True, v.q1, v.k1, v.v1, column, row, v.o1, v.l1), behind)
        return behind

    head = shape(length, HEAD_DIM)
    gathered = shape(n, count, width)
    return Stage(
        body,
        ["x", "enc", "wq", "wk", "wv", "wcq", "wck", "wcv", "dec_seg", "dec_valid", "enc_seg", "enc_valid"]
        + ["gain_self", "gain_cross", "gain_feed", "out_self", "out_cross"],
        dict(
            **({} if roomy else dict(_x_all=gathered)),
            _outs_all=shape(2, n, depth, width), _normed_one=gathered, _encoded=gathered, q1=head, k1=head, v1=head, o1=shape(length, HEAD_DIM, kind=f32),
            l1=shape(1, length, kind=f32), k2=head, v2=head, w_self_own=shape(width, 3 * span),
            w_cq=shape(width, HEAD_DIM), w_ckv_own=shape(width, 2 * span), marks=shape(n, 16, LANES),
        ),
        dict(
            x_all=VMEM((n, count, width), bf16), normed_a=VMEM((n, count, width), bf16),
            encoded=VMEM((n, count, width), bf16), stack=VMEM((6, depth, width), bf16), buf=VMEM((6, width, LANES), bf16),
            w_self=VMEM((width, 3 * HEAD_DIM), bf16), w_ckv=VMEM((width, 2 * HEAD_DIM), bf16), mark=VMEM((16, LANES), bf16),
            marks_in=VMEM((n, 16, LANES), bf16), mark_send=DMA, mark_recv=DMA, open_out=DMA((4,)),
            outs_all=VMEM((2, n, depth, width), bf16), outs_in=outs_scratch(n),
            ring_x=gather_scratch(n), ring_enc=gather_scratch(n), early=columns_scratch(n, span),
            late=columns_scratch(n, span),
        ),
    )


def cross_stage(n, ndp, span, depth, count, width, slim):
    length = n * count
    roomy = roomy_at(n)
    mates = LANES // span

    def body(place, v, behind, first):
        kept = jnp.broadcast_to(v.dec_valid[...].astype(f32), (LANES, LANES)).T[:, :1]
        v.low_a[place.me] = (v.cotangent[...].astype(f32) * kept).astype(bf16)
        gain = gain_row(v.marks, 4, depth)
        if first:
            loads = [
                pltpu.make_async_copy(v._x_all, v.x_all, v.cross_load.at[0]),
                pltpu.make_async_copy(v._outs_all, v.outs_all, v.cross_load.at[1]),
            ]
            for load in loads:
                load.start()
            greet(place.others() + peers(place, ndp))
            for load in loads:
                load.wait()
        own, pairs, heads, *head_sems = v.heads_a

        blocks = n // 2 // mates

        def project(chip):
            step, rows = 2 * count, rows_of(chip, count)
            weight = v.outs_all[0].reshape(width, width)
            start = pl.multiple_of(lax.rem(chip, blocks) * step, step)
            value = mm(heads_at(heads, mates, chip // blocks, start, step), weight)
            value = value + chip_rows(v.x_all, chip).astype(f32)
            normed = normalise(value, gain).astype(bf16)
            value = value.astype(bf16)
            for b in (0, 1):
                v.x_all[2 * chip + b] = value[b * count : (b + 1) * count]
                v.normed_b[2 * chip + b] = normed[b * count : (b + 1) * count]
            query = mm(normed, v.w_cq[...]).astype(bf16)
            v.q2[rows, :] = (query.astype(f32) * HEAD_DIM ** (-0.5)).astype(bf16)

        def project_each():
            for chip in range(n // 2):
                project(jnp.int32(chip))
                yield

        def weights():
            for device in range(n):
                columns = slice(device * slim, (device + 1) * slim)
                both = [ref[:, columns].astype(f32) for ref in (v.gate, v.up)]
                v.targets[device] = jnp.concatenate(both, axis=1).astype(bf16)
            yield
            yield from share_blocks(place, v.targets, v.w_feed_in, v.feed_in)
            v.saves.append(pltpu.make_async_copy(v.w_feed_in, v._w_feed, v.cross_out.at[2]))
            v.saves[-1].start()

        def lows():
            yield from gather(place, v.low_a, v.ring_low)
            v.saves.append(pltpu.make_async_copy(v.low_a, v._low_all, v.cross_out.at[1]))
            v.saves[-1].start()

        behind = in_turn(behind, weights(), lows())
        beside(heads_task(place, span, v.o1, own, pairs, heads, head_sems), behind)
        if not first:
            drain(v.outs_task)
        v.resid_one[...] = mm(own_heads(place, heads, mates, count), v.outs_all[0].reshape(width, width))
        v.resid_one[...] += v.x[...].astype(f32)
        if first:
            pl.loop(0, n // 2)(project)
        else:
            beside(project_each(), behind, 3)
        for i, (source, target) in enumerate(((v.normed_b, v._normed_two), (v.x_all, v._resid_all))):
            v.saves.append(pltpu.make_async_copy(source, target, v.cross_out.at[3 * i]))
            v.saves[-1].start()
        column, row = mark_columns(v.marks, 0), mark_row(v.marks, 2)
        if first:
            beside(attend_forward(False, v.q2, v.k2, v.v2, column, row, v.o2, v.l2), behind, 3)
        else:
            drain(behind)
            drain(attend_forward(False, v.q2, v.k2, v.v2, column, row, v.o2, v.l2))
        return behind

    gathered = shape(n, count, width)
    return Stage(
        body,
        ["o1", "x", "marks", "w_cq", "k2", "v2", "cotangent", "dec_valid", "gate", "up"]
        + ([] if roomy else ["_x_all", "_outs_all"]),
        dict(
            resid_one=shape(count, width, kind=f32), _normed_two=gathered, _low_all=gathered, _resid_all=gathered, q2=shape(length, HEAD_DIM),
            o2=shape(length, HEAD_DIM, kind=f32), l2=shape(1, length, kind=f32), _w_feed=shape(n, depth, 2 * slim),
        ),
        dict(
            normed_b=VMEM((n, count, width), bf16), low_a=VMEM((n, count, width), bf16),
            targets=VMEM((n, depth, 2 * slim), bf16), w_feed_in=VMEM((n, depth, 2 * slim), bf16), cross_out=DMA((4,)),
            cross_load=DMA((2,)), x_all=VMEM((n, count, width), bf16), outs_all=VMEM((2, n, depth, width), bf16),
            ring_low=gather_scratch(n), heads_a=heads_scratch(n, span, length), feed_in=share_scratch(n),
        ),
    )


def norm_back(values, gain, grad):
    r = lax.rsqrt(jnp.mean(values * values, axis=-1, keepdims=True) + epsilon)
    scaled = grad * gain
    inner = jnp.mean(values * scaled, axis=-1, keepdims=True)
    return r * scaled - values * (r * r * r * inner), grad * values * r


def gelu_pair(v):
    c = 0.7978845608028654
    square = v * v
    t = jnp.tanh(c * v * (1.0 + 0.044715 * square))
    value = 0.5 * v * (1.0 + t)
    slope = 0.5 * (1.0 + t) + 0.5 * c * v * (1.0 - t * t) * (1.0 + 3.0 * 0.044715 * square)
    return value, slope


def feed_stage(n, ndp, span, depth, count, width, slim):
    length = n * count
    mates = LANES // span

    def body(place, v, behind, first):
        loads = [
            pltpu.make_async_copy(v._low_all, v.low_b, v.feed_load.at[0]),
            pltpu.make_async_copy(v._w_feed, v.w_feed, v.feed_load.at[1]),
            pltpu.make_async_copy(v._resid_all, v.normed_c, v.feed_load.at[2]),
            pltpu.make_async_copy(v._outs_all.at[1], v.out_cross_all, v.feed_load.at[3]),
        ]
        for load in loads:
            load.start()
        gain = gain_row(v.marks, 5, depth)
        if first:
            greet(place.others() + peers(place, ndp))

        own, pairs, heads, *head_sems = v.heads_c

        weight = v.out_cross_all
        blocks = n // 2 // mates
        made = []

        def feed(chip):
            made.append(chip)
            step, rows = 2 * count, rows_of(chip, count)
            start = pl.multiple_of(lax.rem(chip, blocks) * step, step)
            value = mm(heads_at(heads, mates, chip // blocks, start, step), weight[...].reshape(width, width))
            value = value + chip_rows(v.normed_c, chip).astype(f32)
            block = normalise(value, gain).astype(bf16)
            for b in (0, 1):
                v.normed_c[2 * chip + b] = block[b * count : (b + 1) * count]
            both = mm(block, v.w_feed[...].reshape(width, 2 * slim))
            gate, upward = both[:, :slim], both[:, slim:]
            value, slope = gelu_pair(gate)
            grad = mm_nt(chip_rows(v.low_b, chip), v.down[...])
            v.hidden[rows, :] = (value * upward).astype(bf16)
            both = jnp.concatenate([grad * upward * slope, grad * value], axis=1).astype(bf16)
            v.d_both[rows, :] = both
            return both

        def produce_back(chip):
            return mm_nt(feed(chip), v.w_feed[...].reshape(width, 2 * slim))

        def finish_back(k, value):
            rows = piece_rows(k, count)
            grad, part = norm_back(v.resid_two[rows, :], gain, value)
            v.grad_two[rows, :] = v.low_b[place.me, rows, :].astype(f32) + grad
            part = jnp.sum(part, axis=0, keepdims=True)
            v.tip_three[...] = part if k == 0 else v.tip_three[...] + part

        def weight_grads():
            step = 256
            while len(made) < n // 2:
                yield
            for start in range(0, width, step):
                columns = slice(start, start + step)
                left = v.normed_c[:, :, columns].reshape(length, step)
                v.feed_grad[columns, :] = mm_tn(left, v.d_both[...]).astype(bf16)
                yield
                left = v.low_b[:, :, columns].reshape(length, step)
                v.down_grad[:, columns] = mm_tn(v.hidden[...], left).astype(bf16)
                yield

        beside(heads_task(place, span, v.o2, own, pairs, heads, head_sems), behind)
        for load in loads:
            load.wait()
        v.resid_two[...] = mm(own_heads(place, heads, mates, count), weight[...].reshape(width, width)) + v.resid_one[...]
        grads = weight_grads()
        beside(scatter(place, v.sums_c, produce_back, finish_back), in_turn(behind, grads))
        drain(grads)
        return behind

    return Stage(
        body,
        ["o2", "resid_one", "marks", "_w_feed", "down", "_low_all", "_resid_all", "_outs_all"],
        dict(
            resid_two=shape(count, width, kind=f32), grad_two=shape(count, width, kind=f32),
            tip_three=shape(1, width, kind=f32), hidden=shape(length, slim), feed_grad=shape(width, 2 * slim),
            down_grad=shape(slim, width),
        ),
        dict(
            normed_c=VMEM((n, count, width), bf16), low_b=VMEM((n, count, width), bf16),
            w_feed=VMEM((n, depth, 2 * slim), bf16), d_both=VMEM((length, 2 * slim), bf16), feed_load=DMA((4,)),
            out_cross_all=VMEM((n, depth, width), bf16), heads_c=heads_scratch(n, span, length), sums_c=scatter_scratch(n, count, width),
        ),
    )


def own_grads(place, span, sources, target):
    step = 256
    for start in range(0, target.shape[0], step):
        rows = slice(start, start + step)
        parts = [own_part(place, source[rows, :].astype(bf16), span) for source in sources]
        target[rows, :] = jnp.concatenate(parts, axis=1)


def cross_back_stage(n, ndp, span, depth, count, width, slim):
    length = n * count

    def body(place, v, behind, first):
        v.low_c[place.me] = v.grad_two[...].astype(bf16)
        v.out_sum_c[...] = jnp.zeros_like(v.out_sum_c)
        if first:
            greet(place.others() + peers(place, ndp))

        def into(chip):
            block, rows = chip_rows(v.low_c, chip), rows_of(chip, count)
            v.d_attn_c[rows, :] = mm_nt(block, v.out_cross_head[...]).astype(bf16)
            v.out_sum_c[...] += mm_tn(own_part(place, v.o2[rows, :], span).astype(bf16), block)

        def produce(chip):
            return mm(v.hidden[rows_of(chip, count), :], v.down[...])

        def finish(k, value):
            rows = piece_rows(k, count)
            v.mixed[rows, :] = (v.resid_two[rows, :] + value).astype(bf16)

        def feed_rows(device):
            return v.feed_grad.at[pl.ds(pl.multiple_of(device * depth, depth), depth), :]

        feeds, *feed_sems = v.feed_back
        downs, *down_sems = v.down_back
        behind = in_turn(
            behind,
            settle_blocks(place, ndp, feed_rows, feeds, feed_sems),
            settle_rows(place, ndp, (v.down_grad,), downs, down_sems),
        )
        beside(gather(place, v.low_c, v.ring_d, into), behind)
        behind = in_turn(behind, scatter(place, v.sums_c, produce, finish))
        row, column = mark_row(v.marks, 0), mark_columns(v.marks, 2)
        attention = attend_backward(
            False, v.q2, v.k2, v.v2, v.d_attn_c, v.o2, v.l2, row, column, v.d_attn_c, v.dk_c, v.dv_c
        )
        beside(attention, behind, 3)
        drain(behind)
        v.saves.append(pltpu.make_async_copy(feeds, v._feeds, v.back_out.at[0]))
        v.saves.append(pltpu.make_async_copy(downs, v._downs, v.back_out.at[1]))
        for copy in v.saves[-2:]:
            copy.start()
        own_grads(place, span, (v.d_attn_c,), v.dq2)
        own_grads(place, span, (v.dk_c, v.dv_c), v.dkv2)
        v.out_two[...] = v.out_sum_c[...].astype(bf16)
        return iter(())

    return Stage(
        body,
        ["grad_two", "out_cross_head", "o2", "l2", "q2", "k2", "v2", "marks", "hidden", "down", "resid_two", "feed_grad"]
        + ["down_grad"],
        dict(
            dq2=shape(length, span), dkv2=shape(length, 2 * span), out_two=shape(span, width), mixed=shape(count, width),
            _feeds=shape(ndp, n, depth, 2 * slim), _downs=shape(ndp, slim, width),
        ),
        dict(
            low_c=VMEM((n, count, width), bf16), d_attn_c=VMEM((length, HEAD_DIM), bf16),
            dk_c=VMEM((length, HEAD_DIM), f32), dv_c=VMEM((length, HEAD_DIM), f32),
            out_sum_c=VMEM((span, width), f32), back_out=DMA((2,)), ring_d=gather_scratch(n),
            sums_c=scatter_scratch(n, count, width), feed_back=settle_blocks_scratch(n, ndp, (depth, 2 * slim), bf16),
            down_back=settle_rows_scratch(ndp, slim, width, 1),
        ),
    )


def self_back_stage(n, ndp, span, depth, count, width, slim):
    length = n * count
    roomy = roomy_at(n)

    def body(place, v, behind, first):
        lane = lax.rem(place.me, LANES // span)
        mine, wide, landed, *column_sems = v.columns_e
        outs, *out_sems = v.outs_e
        loads = [
            pltpu.make_async_copy(ref, v.saved, v.self_load.at[i]) for i, ref in enumerate((v._normed_two, v._encoded))
        ]
        loads[0].start()
        gain = gain_row(v.marks, 4, depth)
        v.out_sum_e[...] = jnp.zeros_like(v.out_sum_e)
        v.w_cq_own[...] = own_part(place, v.w_cq[...], span)
        if first:
            greet(place.others() + peers(place, ndp))

        def produce(chip):
            return mm_nt(v.dq2[rows_of(chip, count), :], v.w_cq_own[...])

        def finish(k, value):
            rows = piece_rows(k, count)
            grad, part = norm_back(v.resid_one[rows, :], gain, value)
            grad = v.grad_two[rows, :] + grad
            v.grad_one[rows, :] = grad
            v.low_e[place.me, rows, :] = grad.astype(bf16)
            part = jnp.sum(part, axis=0, keepdims=True)
            v.tip_two[...] = part if k == 0 else v.tip_two[...] + part

        def weight_grads():
            step = 256
            loads[0].wait()
            for start in range(0, width, step):
                columns = slice(start, start + step)
                left = v.saved[:, :, columns].reshape(length, step)
                mine[0, lane, columns, :] = mm_tn(left, v.dq2[...]).astype(bf16)
                yield
            loads[1].start()
            yield
            loads[1].wait()
            for start in range(0, width, step):
                columns = slice(start, start + step)
                left = v.saved[:, :, columns].reshape(length, step)
                value = mm_tn(left, v.dkv2[...]).astype(bf16)
                mine[1, lane, columns, :] = value[:, :span]
                mine[2, lane, columns, :] = value[:, span:]
                yield

        def into(chip):
            block, rows = chip_rows(v.low_e, chip), rows_of(chip, count)
            v.d_attn_e[rows, :] = mm_nt(block, v.out_self_head[...]).astype(bf16)
            v.out_sum_e[...] += mm_tn(own_part(place, v.o1[rows, :], span).astype(bf16), block)

        def produce_enc(chip):
            return mm_nt(v.dkv2[rows_of(chip, count), :], v.w_ckv_own[...])

        def finish_enc(k, value):
            v.enc_grad[piece_rows(k, count), :] = value

        def columns():
            yield from settle_columns(place, ndp, span, mine, wide, landed, column_sems)
            v.saves.append(pltpu.make_async_copy(landed, v._columns_two, v.self_load.at[2]))
            v.saves[-1].start()

        def rests():
            yield from settle_rows(place, ndp, (v.out_two,), outs, out_sems)
            v.saves.append(pltpu.make_async_copy(outs, v._outs_two, v.self_load.at[3]))
            v.saves[-1].start()

        grads = weight_grads()
        beside(scatter(place, v.sums_e, produce, finish), in_turn(behind, grads))
        drain(grads)
        encs = scatter(place, v.sums_f if roomy else v.sums_e, produce_enc, finish_enc)
        behind = in_turn(behind, columns(), rests(), *([encs] if roomy else []))
        beside(gather(place, v.low_e, v.ring_e, into), behind, 1, 3)
        if not roomy:
            behind = in_turn(behind, encs)
        row, column = mark_row(v.marks, 0), mark_columns(v.marks, 1)
        attention = attend_backward(
            True, v.q1, v.k1, v.v1, v.d_attn_e, v.o1, v.l1, row, column, v.d_attn_e, v.dk_e, v.dv_e
        )
        beside(attention, behind, 2)
        own_grads(place, span, (v.d_attn_e, v.dk_e, v.dv_e), v.grads_one)
        v.out_one[...] = v.out_sum_e[...].astype(bf16)
        return behind

    rows = shape(count, width, kind=f32)
    return Stage(
        body,
        ["dq2", "dkv2", "w_cq", "w_ckv_own", "resid_one", "grad_two", "marks", "out_self_head", "o1", "l1", "q1", "k1", "v1"]
        + ["out_two", "_normed_two", "_encoded"],
        dict(
            grads_one=shape(length, 3 * span), out_one=shape(span, width), grad_one=rows, enc_grad=rows,
            tip_two=shape(1, width, kind=f32), _columns_two=shape(ndp, 3, depth, width), _outs_two=shape(ndp, span, width),
        ),
        dict(
            saved=VMEM((n, count, width), bf16), low_e=VMEM((n, count, width), bf16),
            d_attn_e=VMEM((length, HEAD_DIM), bf16),
            dk_e=VMEM((length, HEAD_DIM), f32), dv_e=VMEM((length, HEAD_DIM), f32), out_sum_e=VMEM((span, width), f32),
            w_cq_own=VMEM((width, span), bf16), self_load=DMA((4,)), ring_e=gather_scratch(n),
            sums_e=scatter_scratch(n, count, width),
            columns_e=settle_columns_scratch(n, ndp, span, depth, width, 3), outs_e=settle_rows_scratch(ndp, span, width, 1),
            **(dict(sums_f=scatter_scratch(n, count, width)) if roomy else {}),
        ),
    )


def close_stage(n, ndp, span, depth, count, width, slim):
    length = n * count
    mates = LANES // span

    def body(place, v, behind, first):
        lane = lax.rem(place.me, mates)
        mine, wide, landed, *column_sems = v.columns_g
        outs, *out_sems = v.outs_g
        tips, *tip_sems = v.tips_g
        load = pltpu.make_async_copy(v._normed_one, v.saved, v.close_load.at[0])
        load.start()
        gain = gain_row(v.marks, 3, depth)
        v.tip_all[...] = jnp.zeros_like(v.tip_all)
        v.tip_all[1:2, :] = v.tip_two[...]
        v.tip_all[2:3, :] = v.tip_three[...]
        if first:
            greet(place.others() + peers(place, ndp))

        def produce(chip):
            return mm_nt(v.grads_one[rows_of(chip, count), :], v.w_self_own[...])

        def finish(k, value):
            rows = piece_rows(k, count)
            grad, part = norm_back(v.x[rows, :].astype(f32), gain, value)
            v.dec_grad[rows, :] = v.grad_one[rows, :] + grad
            v.tip_all[0:1, :] += jnp.sum(part, axis=0, keepdims=True)

        def columns():
            load.wait()
            step = 256
            for start in range(0, width, step):
                columns = slice(start, start + step)
                value = mm_tn(v.saved[:, :, columns].reshape(length, step), v.grads_one[...]).astype(bf16)
                for i in range(3):
                    mine[i, lane, columns, :] = value[:, i * span : (i + 1) * span]
                yield
            yield from settle_columns(place, ndp, span, mine, wide, landed, column_sems)

        def tip(device):
            return v.tip_all.at[:, pl.ds(pl.multiple_of(device // mates * LANES, LANES), LANES)]

        behind = in_turn(columns(), settle_rows(place, ndp, (v.out_one,), outs, out_sems), behind)
        beside(scatter(place, v.sums_e, produce, finish), behind)
        drain(in_turn(settle_tips(place, ndp, tip, tips, tip_sems), behind))
        for i, (source, target) in enumerate(((landed, v._columns_one), (outs, v._outs_one), (tips, v._tips))):
            v.saves.append(pltpu.make_async_copy(source, target, v.close_load.at[i + 1]))
            v.saves[-1].start()
        return iter(())

    return Stage(
        body,
        ["grads_one", "w_self_own", "x", "grad_one", "marks", "out_one", "tip_two", "tip_three", "_normed_one"],
        dict(
            dec_grad=shape(count, width, kind=f32), _columns_one=shape(ndp, 3, depth, width),
            _outs_one=shape(ndp, span, width), _tips=shape(ndp * n, 8, LANES, kind=f32),
        ),
        dict(
            saved=VMEM((n, count, width), bf16), tip_all=VMEM((8, width), f32), close_load=DMA((4,)),
            sums_e=scatter_scratch(n, count, width), columns_g=settle_columns_scratch(n, ndp, span, depth, width, 3),
            outs_g=settle_rows_scratch(ndp, span, width, 1), tips_g=settle_tips_scratch(n, ndp),
        ),
    )


def over_dp(landed, *index):
    return sum(landed[(d, *index)].astype(f32) for d in range(landed.shape[0]))


def total_kernel(
    n, span,
    columns_one, columns_two, outs_one, outs_two, feeds, downs, tips,
    gains_out, q_out, k_out, v_out, out_one, cq_out, ck_out, cv_out, out_two, gate_out, up_out, down_out,
):
    for i, ref in enumerate((q_out, k_out, v_out)):
        ref[...] = over_dp(columns_one, i)
    for i, ref in enumerate((cq_out, ck_out, cv_out)):
        ref[...] = over_dp(columns_two, i)
    out_one[...] = over_dp(outs_one)
    out_two[...] = over_dp(outs_two)
    down_out[...] = over_dp(downs)
    slim = gate_out.shape[1] // n
    for i in range(n):
        piece = over_dp(feeds, i)
        gate_out[:, i * slim : (i + 1) * slim] = piece[:, :slim]
        up_out[:, i * slim : (i + 1) * slim] = piece[:, slim:]
    total = over_dp(tips)
    mates = LANES // span
    lane = lax.rem(lax.axis_index("blk"), mates)
    part = total[:, :span]
    for i in range(1, mates):
        part = jnp.where(lane == i, total[:, i * span : (i + 1) * span], part)
    gains_out[...] = part


def total_grads(n, span, columns_one, columns_two, outs_one, outs_two, feeds, downs, tips):
    depth, width = columns_one.shape[2:]
    slim = downs.shape[1]

    square, out = shape(depth, width, kind=f32), shape(span, width, kind=f32)
    return pl.pallas_call(
        functools.partial(total_kernel, n, span),
        out_shape=(
            shape(8, span, kind=f32), square, square, square, out, square, square, square, out,
            shape(depth, n * slim, kind=f32), shape(depth, n * slim, kind=f32), shape(slim, width, kind=f32),
        ),
        compiler_params=pltpu.CompilerParams(vmem_limit_bytes=40 * 1024 * 1024),
        name="total_grads",
    )(columns_one, columns_two, outs_one, outs_two, feeds, downs, tips)


def local(
    n,
    ndp,
    dec_in,
    enc_out,
    cotangent,
    dec_seg,
    dec_valid,
    enc_seg,
    enc_valid,
    self_gain,
    self_query,
    self_key,
    self_value,
    self_out,
    cross_gain,
    cross_query,
    cross_key,
    cross_value,
    cross_out,
    feed_gain,
    feed_gate,
    feed_up,
    feed_down,
):
    width = dec_in.shape[2]
    depth = self_query.shape[0]
    span = width // n
    share = HEAD_DIM // span

    def whole_head(weight):
        if share == 1:
            return weight
        groups = [[h * share + i for i in range(share)] for h in range(n // share)]
        return lax.all_gather(weight, "blk", axis=0, tiled=True, axis_index_groups=groups)

    count, slim = dec_in.shape[1], feed_gate.shape[1] // n
    arrays = dict(
        x=dec_in[0], enc=enc_out[0], cotangent=cotangent[0],
        dec_seg=dec_seg, dec_valid=dec_valid, enc_seg=enc_seg, enc_valid=enc_valid,
        gain_self=self_gain[None], gain_cross=cross_gain[None], gain_feed=feed_gain[None],
        wq=self_query, wk=self_key, wv=self_value, wcq=cross_query, wck=cross_key, wcv=cross_value,
        out_self=self_out, out_cross=cross_out, gate=feed_gate, up=feed_up, down=feed_down,
        out_self_head=whole_head(self_out), out_cross_head=whole_head(cross_out),
    )
    stages = [
        (name, make(n, ndp, span, depth, count, width, slim))
        for name, make in (
            ("open", open_stage), ("cross", cross_stage), ("feed", feed_stage),
            ("cross_back", cross_back_stage), ("self_back", self_back_stage), ("close", close_stage),
        )
    ]
    size = 2 if roomy_at(n) else 1
    results = {"mixed", "dec_grad", "enc_grad", "_columns_one", "_columns_two", "_outs_one", "_outs_two"}
    results |= {"_feeds", "_downs", "_tips"}
    for at in range(0, len(stages), size):
        later = {key for _, stage in stages[at + size :] for key in stage.inputs}
        group = stages[at : at + size]
        name = "_and_".join(key for key, _ in group)
        fused(name, at, n, ndp, [stage for _, stage in group], arrays, later | results)
    gains, q, k, v, o, cq, ck, cv, co, gate, up, down = total_grads(
        n, span, *(arrays[key] for key in ("_columns_one", "_columns_two", "_outs_one", "_outs_two", "_feeds", "_downs", "_tips"))
    )
    return (
        arrays["mixed"][None], arrays["dec_grad"][None], arrays["enc_grad"][None],
        gains[0], q, k, v, o,
        gains[1], cq, ck, cv, co,
        gains[2], gate, up, down,
    )


def solution(mesh):
    row, token = P("dp", "blk"), P("dp", "blk", None)
    gain, weight = P("blk"), P("blk", None)
    return jax.shard_map(
        functools.partial(local, mesh.shape["blk"], mesh.shape["dp"]),
        mesh=mesh,
        in_specs=(token,) * 3 + (row,) * 4 + ((gain,) + (weight,) * 4) * 2 + (gain,) + (weight,) * 3,
        out_specs=(token,) * 3 + ((gain,) + (weight,) * 4) * 2 + (gain,) + (weight,) * 3,
        check_vma=False,
    )
```

```python
import functools
import types

import jax
import jax.numpy as jnp
from jax import lax
from jax.experimental import pallas as pl
from jax.experimental.pallas import tpu as pltpu
from jax.sharding import PartitionSpec as P

HEADS = 16
HEAD_DIM = 64
LANES = 128
PIECES = 2
epsilon = 1e-06
negative = -1e30
MESH = pl.DeviceIdType.MESH
bf16 = jnp.bfloat16
f32 = jnp.float32
VMEM = pltpu.VMEM
DMA = pltpu.SemaphoreType.DMA


def contract(left, right, dims):
    return lax.dot_general(left, right, ((dims[:1], dims[1:]), ((), ())), preferred_element_type=f32)


def mm(left, right):
    return contract(left, right, (1, 0))


def mm_nt(left, right):
    return contract(left, right, (1, 1))


def mm_tn(left, right):
    return contract(left, right, (0, 0))


class Place:
    def __init__(self, n):
        self.n, self.chips = n, n // 2
        self.half = self.chips // 2
        self.dp, self.me = lax.axis_index("dp"), lax.axis_index("blk")
        self.core = lax.rem(self.me, 2)
        chip = self.me // 2
        y, z = lax.rem(chip, 2), chip // 2
        self.pos = z + y * (self.chips - 1 - 2 * z)
        self.sibling = (self.dp, self.me + 1 - 2 * self.core)
        self.half_row = lax.rem(self.dp, 2)
        self.twin = (self.dp + 1 - 2 * self.half_row, self.me)
        self.sides = tuple((self.dp, 2 * self.chip(step) + self.core) for step in (1, -1))

    def chip(self, offset):
        position = lax.rem(self.pos + offset + 2 * self.chips, self.chips)
        side = position // (self.chips // 2)
        return 2 * (position + side * (self.chips - 1 - 2 * position)) + side

    def others(self):
        return [(self.dp, lax.rem(self.me + k, self.n)) for k in range(1, self.n)]

    def around(self):
        return [self.sibling, *self.sides]


def greet(partners):
    barrier = pltpu.get_barrier_semaphore()
    for partner in partners:
        pl.semaphore_signal(barrier, inc=1, device_id=partner, device_id_type=MESH)
    pl.semaphore_wait(barrier, len(partners))


def remote(src, dst, send, recv, device):
    return pltpu.make_async_remote_copy(
        src_ref=src, dst_ref=dst, send_sem=send, recv_sem=recv, device_id=device, device_id_type=MESH
    )


def wait_sent(ref, sem, device):
    remote(ref, ref, sem, sem, device).wait_send()


def wait_landed(ref, sem, device):
    remote(ref, ref, sem, sem, device).wait_recv()


def pieces_of(half, way, step):
    if step < half - 1:
        return tuple(range(PIECES))
    return tuple(range(PIECES // 2)) if way == 0 else tuple(range(PIECES // 2, PIECES))


def drain(task):
    for _ in task:
        pass


def beside(main, task, waits=1, steps=1):
    for count, _ in enumerate(main):
        if (count + 1) % steps == 0:
            for _ in range(waits):
                next(task, None)


def in_turn(*tasks):
    tasks = list(tasks)
    while tasks:
        for task in list(tasks):
            if next(task, "done") == "done":
                tasks.remove(task)
            else:
                yield


def one_by_one(*tasks):
    for task in tasks:
        yield from task


def gather_scratch(n):
    half = n // 4
    return [DMA, DMA((2, half, PIECES)), DMA, DMA((n // 2,))]


def gather(place, buf, sems, use=None):
    ring_send, ring_recv, sib_send, sib_recv = sems
    half, part = place.half, buf.shape[1] // PIECES

    def ring(way, step, k):
        ref = buf.at[2 * place.chip(-step if way == 0 else step) + place.core, pl.ds(k * part, part)]
        return remote(ref, ref, ring_send, ring_recv.at[way, step, k], place.sides[way])

    def across(offset):
        ref = buf.at[2 * place.chip(offset) + place.core]
        return remote(ref, ref, sib_send, sib_recv.at[offset + half - 1], place.sibling)

    def ready(offset):
        across(offset).wait_recv()
        if use is not None:
            use(place.chip(offset))

    for i in range(PIECES):
        for way in (0, 1):
            k = i if way == 0 else PIECES - 1 - i
            if k in pieces_of(half, way, 0):
                ring(way, 0, k).start()
    across(0).start()
    for step in range(half):
        for i in range(PIECES):
            for way in (0, 1):
                k = i if way == 0 else PIECES - 1 - i
                if k not in pieces_of(half, way, step):
                    continue
                yield
                ring(way, step, k).wait_recv()
                if step + 1 < half and k in pieces_of(half, way, step + 1):
                    ring(way, step + 1, k).start()
                if step + 1 < half and i == PIECES - 1:
                    across(-1 - step if way == 0 else step + 1).start()
        if step + 1 == half:
            across(half).start()
        for way in (0, 1) if step else (0,):
            ready(-step if way == 0 else step)
    yield
    ready(half)
    wait_sent(buf.at[pl.ds(0, place.chips - 1)], ring_send, place.sides[0])
    wait_sent(buf.at[pl.ds(0, place.chips)], sib_send, place.sibling)


def scatter_scratch(n, rows, columns):
    half = n // 4
    return [
        VMEM((n, rows, columns), bf16),
        VMEM((n // 2, rows, columns), bf16),
        VMEM((2, half, PIECES, rows // PIECES, columns), bf16),
        VMEM((2, half, PIECES, rows // PIECES, columns), bf16),
        DMA,
        DMA((2, half, PIECES)),
        DMA,
        DMA((n // 2,)),
    ]


def scatter(place, scratch, produce, finish):
    blocks, theirs, held, landed, ring_send, ring_recv, sib_send, sib_recv = scratch
    half, rows = place.half, blocks.shape[1]
    part = rows // PIECES

    def across(offset):
        chip = place.chip(offset)
        return remote(
            blocks.at[2 * chip + 1 - place.core], theirs.at[chip], sib_send, sib_recv.at[offset + half - 1], place.sibling
        )

    def make(offset):
        chip = place.chip(offset)
        value = produce(chip).astype(bf16)
        blocks[2 * chip] = value[:rows]
        blocks[2 * chip + 1] = value[rows:]
        across(offset).start()

    def ring(way, step, k):
        return remote(
            held.at[way, step, k], landed.at[way, step, k], ring_send, ring_recv.at[way, step, k], place.sides[way]
        )

    def mine(offset, k):
        chip, window = place.chip(offset), pl.ds(k * part, part)
        return blocks[2 * chip + place.core, window, :].astype(f32) + theirs[chip, window, :].astype(f32)

    first = [pieces_of(half, way, half - 1) for way in (0, 1)]
    make(half)
    for step in range(half):
        left = half - 1 - step
        for offset in (left, -left) if left else (0,):
            make(offset)
        yield
        across(half - step).wait_recv()
        if step:
            across(step - half).wait_recv()
        for i in range(PIECES):
            for way in (0, 1):
                k = i if way == 0 else PIECES - 1 - i
                if step == 0 and k not in first[way]:
                    continue
                offset = half if step == 0 else half - step if way == 0 else step - half
                value = mine(offset, k)
                if step >= 2 or (step == 1 and k in first[way]):
                    yield
                    ring(way, step - 1, k).wait_recv()
                    value = value + landed[way, step - 1, k].astype(f32)
                held[way, step, k] = value.astype(bf16)
                ring(way, step, k).start()
    yield
    across(0).wait_recv()
    for k in range(PIECES):
        value = mine(0, k)
        for way in (0, 1):
            yield
            ring(way, half - 1, k).wait_recv()
            value = value + landed[way, half - 1, k].astype(f32)
        finish(k, value)
    wait_sent(theirs.at[pl.ds(0, place.chips - 1)], ring_send, place.sides[0])
    wait_sent(theirs, sib_send, place.sibling)


def mark_row(marks, which):
    return jnp.concatenate([marks[i, which : which + 1, :] for i in range(marks.shape[0])], axis=1).astype(f32)


def mark_columns(marks, which):
    n = marks.shape[0]
    rows = jnp.concatenate([marks[i, which : which + 1, :].astype(f32) for i in range(n)], axis=0)
    rows = jnp.concatenate([rows, jnp.zeros((LANES - n, LANES), f32)], axis=0)
    return rows.T


def column_of(columns, first, count):
    blocks = count // LANES
    return jnp.concatenate([columns[:, first // LANES + i : first // LANES + i + 1] for i in range(blocks)], axis=0)


def gain_row(marks, which, depth):
    return jnp.concatenate(
        [marks[i, which : which + 1, :].astype(f32)[:, :depth] for i in range(marks.shape[0])], axis=1
    )


def normalise(values, gain):
    return values * lax.rsqrt(jnp.mean(values * values, axis=-1, keepdims=True) + epsilon) * gain


def tile_of(length):
    return 256 if length <= 2048 else 128


def attend_forward(causal, q_ref, k_ref, v_ref, query_column, key_row, o_ref, l_ref):
    length = q_ref.shape[0]
    tile = tile_of(length)

    def one(start, reach, column):
        rows = pl.ds(start, tile)
        scores = mm_nt(q_ref[rows, :], k_ref[:reach, :])
        keep = column == key_row[:, :reach]
        if causal:
            keep = keep & (
                lax.broadcasted_iota(jnp.int32, (tile, reach), 1)
                <= lax.broadcasted_iota(jnp.int32, (tile, reach), 0) + start
            )
        scores = jnp.where(keep, scores, negative)
        top = jnp.max(scores, axis=1, keepdims=True)
        weights = jnp.exp(scores - top)
        total = jnp.sum(weights, axis=1, keepdims=True)
        o_ref[rows, :] = mm(weights.astype(bf16), v_ref[:reach, :]) / total
        l_ref[:, rows] = jnp.broadcast_to(top + jnp.log(total), (tile, LANES)).T[:1, :]

    if tile == LANES and not causal:

        @pl.loop(0, length // tile)
        def _(i):
            lanes = lax.broadcasted_iota(jnp.int32, query_column.shape, 1)
            column = jnp.sum(jnp.where(lanes == i, query_column, 0.0), axis=1, keepdims=True)
            one(pl.multiple_of(i * tile, tile), length, column)

        return
    for start in range(0, length, tile):
        one(start, start + tile if causal else length, column_of(query_column, start, tile))
        yield


def attend_backward(
    causal, q_ref, k_ref, v_ref, g_ref, o_ref, l_ref, query_row, key_column, dq_ref, dk_sum, dv_sum
):
    length = q_ref.shape[0]
    tile = tile_of(length)
    dk_sum[...] = jnp.zeros_like(dk_sum)
    dv_sum[...] = jnp.zeros_like(dv_sum)
    for start in range(0, length, tile):
        reach = start + tile if causal else length
        rows = slice(start, start + tile)
        queries, grads = q_ref[rows, :], g_ref[rows, :]
        spread = jnp.sum(grads.astype(f32) * o_ref[rows, :], axis=1, keepdims=True)
        spread = jnp.broadcast_to(spread, (tile, LANES)).T[:1, :]
        dq = 0.0
        for begin in range(0, reach, 2048):
            part = slice(begin, min(reach, begin + 2048))
            keys = k_ref[part, :]
            count = keys.shape[0]
            scores = mm_nt(keys, queries)
            keep = column_of(key_column, begin, count) == query_row[:, rows]
            if causal:
                keep = keep & (
                    lax.broadcasted_iota(jnp.int32, (count, tile), 0) + begin
                    <= lax.broadcasted_iota(jnp.int32, (count, tile), 1) + start
                )
            probs = jnp.where(keep, jnp.exp(scores - l_ref[:, rows]), 0.0)
            dprobs = mm_nt(v_ref[part, :], grads)
            dscores = (probs * (dprobs - spread)).astype(bf16)
            dk_sum[part, :] += mm(dscores, queries)
            dv_sum[part, :] += mm(probs.astype(bf16), grads)
            dq = dq + mm_tn(dscores, keys)
        dq_ref[rows, :] = (dq * HEAD_DIM ** (-0.5)).astype(bf16)
        yield


class Stage:
    def __init__(self, body, inputs, outputs, scratch):
        self.body, self.inputs, self.outputs, self.scratch = body, inputs, outputs, scratch


def fused(name, collective_id, n, ndp, stages, arrays, wanted):
    outputs, scratch = {}, {}
    for stage in stages:
        outputs.update(stage.outputs)
        scratch.update(stage.scratch)
    inputs = [x for stage in stages for x in stage.inputs if x not in outputs]
    inputs = list(dict.fromkeys(inputs))
    for key in list(outputs):
        if key not in wanted:
            scratch[key] = VMEM(outputs[key].shape, outputs.pop(key).dtype)

    def specs(names):
        return tuple(pl.BlockSpec(memory_space=pl.ANY if x.startswith("_") else VMEM) for x in names)

    flat, slots = [], {}
    for key, value in scratch.items():
        many = isinstance(value, list)
        items = value if many else [value]
        slots[key] = (len(flat), len(items), many)
        flat += items

    def kernel(*refs):
        table = dict(zip(inputs + list(outputs), refs))
        rest = refs[len(inputs) + len(outputs) :]
        for key, (at, length, many) in slots.items():
            table[key] = rest[at : at + length] if many else rest[at]
        table["saves"] = []
        place = Place(n)
        view = types.SimpleNamespace(**table)
        behind = iter(())
        for number, stage in enumerate(stages):
            behind = stage.body(place, view, behind, number == 0)
        drain(behind)
        for copy in view.saves:
            copy.wait()

    results = pl.pallas_call(
        kernel,
        out_shape=tuple(outputs.values()),
        in_specs=specs(inputs),
        out_specs=specs(outputs),
        scratch_shapes=flat,
        compiler_params=pltpu.CompilerParams(
            collective_id=collective_id, has_side_effects=True, vmem_limit_bytes=(58 if n <= 16 else 62) * 1024 * 1024
        ),
        name=name,
    )(*[arrays[x] for x in inputs])
    arrays.update(zip(outputs, results))


def shape(*dims, kind=bf16):
    return jax.ShapeDtypeStruct(dims, kind)


def settle_columns(place, ndp, span, mine, wide, landed, sems):
    mate_send, mate_recv, own_sem, send, recv, dp_send, dp_recv = sems
    matrices, mates, width, _ = mine.shape
    groups = place.n // mates
    depth = landed.shape[2]
    group, lane = place.me // mates, lax.rem(place.me, mates)

    def swap(r):
        mate = group * mates + lax.rem(lane + r, mates)
        ref = mine.at[:, lane]
        return remote(ref, ref, mate_send.at[r - 1], mate_recv.at[r - 1], (place.dp, mate))

    def rows(device):
        return wide.at[:, pl.ds(pl.multiple_of(device * depth, depth), depth), :]

    def lanes(origin):
        return landed.at[place.dp, :, :, pl.ds(pl.multiple_of(origin * LANES, LANES), LANES)]

    def move(step):
        target = lax.rem(group + step, groups) * mates + lane
        return remote(rows(target), lanes(group), send, recv.at[step - 1], (place.dp, target))

    def peer(r):
        return (lax.rem(place.dp + r, ndp), place.me)

    def pass_on(ref, origin):
        for r in range(1, ndp):
            remote(ref, lanes(origin), dp_send.at[r - 1], dp_recv.at[r - 1], peer(r)).start()

    for r in range(1, mates):
        swap(r).start()
    yield
    for r in range(1, mates):
        swap(r).wait_recv()
    for m in range(matrices):
        wide[m] = jnp.concatenate([mine[m, i] for i in range(mates)], axis=1)
    for step in range(1, groups):
        move(step).start()
    own = pltpu.make_async_copy(rows(place.me), lanes(group), own_sem)
    own.start()
    pass_on(rows(place.me), group)
    for step in range(1, groups):
        yield
        move(step).wait_recv()
        origin = lax.rem(group + groups - step, groups)
        pass_on(lanes(origin), origin)
    yield
    own.wait()
    for r in range(1, mates):
        swap(r).wait_send()
    wait_sent(wide.at[:, pl.ds(0, (groups - 1) * depth), :], send, place.sibling)
    for r in range(1, ndp):
        wait_sent(landed.at[0], dp_send.at[r - 1], peer(r))
        wait_landed(landed.at[0], dp_recv.at[r - 1], peer(r))


def settle_columns_scratch(n, ndp, span, depth, width, matrices):
    mates = LANES // span
    groups = n // mates
    return [
        VMEM((matrices, mates, width, span), bf16),
        VMEM((matrices, width, LANES), bf16),
        VMEM((ndp, matrices, depth, width), bf16),
        DMA((mates - 1,)),
        DMA((mates - 1,)),
        DMA,
        DMA,
        DMA((groups - 1,)),
        DMA((ndp - 1,)),
        DMA((ndp - 1,)),
    ]


def settle_blocks(place, ndp, source, landed, sems):
    own_sem, send, recv, dp_send, dp_recv = sems
    n = place.n

    def move(k):
        target = lax.rem(place.me + k, n)
        return remote(source(target), landed.at[place.dp, place.me], send, recv.at[k - 1], (place.dp, target))

    def peer(r):
        return (lax.rem(place.dp + r, ndp), place.me)

    def pass_on(ref, origin):
        for r in range(1, ndp):
            remote(ref, landed.at[place.dp, origin], dp_send.at[r - 1], dp_recv.at[r - 1], peer(r)).start()

    window = 4
    for k in range(1, window):
        move(k).start()
    own = pltpu.make_async_copy(source(place.me), landed.at[place.dp, place.me], own_sem)
    own.start()
    pass_on(source(place.me), place.me)
    for k in range(1, n):
        yield
        if k + window - 1 < n:
            move(k + window - 1).start()
        move(k).wait_recv()
        origin = lax.rem(place.me + n - k, n)
        pass_on(landed.at[place.dp, origin], origin)
    yield
    own.wait()
    wait_sent(landed.at[0, pl.ds(0, n - 1)], send, place.sibling)
    for r in range(1, ndp):
        wait_sent(landed.at[0], dp_send.at[r - 1], peer(r))
        wait_landed(landed.at[0], dp_recv.at[r - 1], peer(r))


def settle_blocks_scratch(n, ndp, block, kind):
    return [VMEM((ndp, n) + block, kind), DMA, DMA, DMA((n - 1,)), DMA((ndp - 1,)), DMA((ndp - 1,))]


def settle_tips(place, ndp, source, landed, sems):
    own_sem, send, recv = sems
    n = place.n
    here = place.dp * n + place.me
    for r in range(ndp):
        for k in range(n):
            if r or k:
                target = (lax.rem(place.dp + r, ndp), lax.rem(place.me + k, n))
                remote(source(target[1]), landed.at[here], send, recv, target).start()
    own = pltpu.make_async_copy(source(place.me), landed.at[here], own_sem)
    own.start()
    yield
    own.wait()
    wait_landed(landed.at[pl.ds(0, ndp * n - 1)], recv, place.sibling)
    wait_sent(landed.at[pl.ds(0, ndp * n - 1)], send, place.sibling)


def settle_rows(place, ndp, parts, landed, sems):
    send, recv = sems
    copies, at = [], 0
    for i, part in enumerate(parts):
        window = pl.ds(at, part.shape[0])
        at += part.shape[0]
        for r in range(1, ndp):
            peer = lax.rem(place.dp + r, ndp)
            copy = remote(
                part, landed.at[place.dp, window], send.at[i, r - 1], recv.at[i, r - 1], (peer, place.me)
            )
            copy.start()
            copies.append(copy)
        landed[place.dp, window] = part[...]
    yield
    for copy in copies:
        copy.wait()


def settle_tips_scratch(n, ndp):
    return [VMEM((ndp * n, 8, LANES), f32), DMA, DMA, DMA]


def settle_rows_scratch(ndp, rows, width, parts):
    return [VMEM((ndp, rows, width), bf16), DMA((parts, ndp - 1)), DMA((parts, ndp - 1))]


def peers(place, ndp):
    return [(lax.rem(place.dp + r, ndp), place.me) for r in range(1, ndp)]


def own_part(place, values, span):
    share = HEAD_DIM // span
    part = values[:, :span]
    for i in range(1, share):
        part = jnp.where(lax.rem(place.me, share) == i, values[:, i * span : (i + 1) * span], part)
    return part


def rows_of(chip, count):
    return pl.ds(pl.multiple_of(chip * 2 * count, 2 * count), 2 * count)


def chip_rows(blocks, chip):
    _, count, width = blocks.shape
    return blocks[pl.ds(2 * chip, 2)].reshape(2 * count, width)


def piece_rows(k, count):
    part = count // PIECES
    return slice(k * part, (k + 1) * part)


def columns_task(place, span, stack, buf, first, last, sems):
    own_sem, send, recv, twin_send, twin_recv, pass_send, pass_recv = sems
    mates = LANES // span
    groups = place.n // mates
    depth = stack.shape[1]
    part = depth // 2
    group, lane = place.me // mates, lax.rem(place.me, mates)
    which = pl.ds(first, last - first)

    def lanes(target):
        return pl.ds(pl.multiple_of(target * LANES, LANES), LANES)

    def rows(device, begin, count):
        return buf.at[which, pl.ds(pl.multiple_of(device * depth + begin, part), count), :]

    def half(device, other):
        return rows(device, (1 - place.half_row if other else place.half_row) * part, part)

    def mate(r):
        return (place.dp, group * mates + lax.rem(lane + r, mates))

    def hand(source, target):
        for r in range(1, mates):
            remote(source, target, pass_send.at[r - 1], pass_recv.at[r - 1], mate(r)).start()

    def arrival(step):
        target = lax.rem(group + step, groups)
        source = stack.at[which, pl.ds(pl.multiple_of(place.half_row * part, part), part), lanes(target)]
        return remote(source, half(place.me, 0), send, recv.at[step - 1], (place.dp, target * mates + lane))

    def origin(step):
        return lax.rem(group + groups - step, groups) * mates + lane

    def twin(step):
        ref = half(origin(step), 0)
        return remote(ref, ref, twin_send, twin_recv.at[step - 1], place.twin)

    for step in range(1, groups):
        arrival(step).start()
    mine = stack.at[which, :, lanes(group)]
    own = pltpu.make_async_copy(mine, rows(place.me, 0, depth), own_sem)
    own.start()
    hand(mine, rows(place.me, 0, depth))
    for step in range(1, groups + 1):
        yield
        if step < groups:
            arrival(step).wait_recv()
            twin(step).start()
            ref = half(origin(step), 0)
            hand(ref, ref)
        if step > 1:
            twin(step - 1).wait_recv()
            ref = half(origin(step - 1), 1)
            hand(ref, ref)
    yield
    own.wait()
    sent = buf.at[which, pl.ds(0, (groups - 1) * part), :]
    wait_sent(sent, send, place.sibling)
    wait_sent(sent, twin_send, place.twin)
    for r in range(1, mates):
        passed = buf.at[which, pl.ds(0, groups * depth), :]
        wait_landed(passed, pass_recv.at[r - 1], mate(r))
        wait_sent(passed, pass_send.at[r - 1], mate(r))


def columns_scratch(n, span):
    mates = LANES // span
    groups = n // mates
    return [DMA, DMA, DMA((groups - 1,)), DMA, DMA((groups - 1,)), DMA((mates - 1,)), DMA((mates - 1,))]


def share_blocks(place, blocks, landed, sems, window=4):
    own_sem, send, recv, twin_send, twin_recv = sems
    n, part = place.n, blocks.shape[1] // 2
    rows = pl.ds(pl.multiple_of(place.half_row * part, part), part)

    def move(k):
        target = lax.rem(place.me + k, n)
        return remote(blocks.at[target, rows], landed.at[place.me, rows], send, recv.at[k - 1], (place.dp, target))

    own = pltpu.make_async_copy(blocks.at[place.me], landed.at[place.me], own_sem)
    own.start()
    for k in range(1, window):
        move(k).start()
    for k in range(1, n):
        yield
        if k + window - 1 < n:
            move(k + window - 1).start()
        move(k).wait_recv()
        ref = landed.at[lax.rem(place.me + n - k, n), rows]
        remote(ref, ref, twin_send, twin_recv, place.twin).start()
    yield
    own.wait()
    ref = landed.at[pl.ds(0, n - 1), pl.ds(0, part)]
    wait_landed(ref, twin_recv, place.twin)
    wait_sent(ref, twin_send, place.twin)
    wait_sent(ref, send, place.sibling)


def share_scratch(n):
    return [DMA, DMA, DMA((n - 1,)), DMA, DMA]


def outs_task(place, shards, full, sems):
    ring, (twin_send, twin_recv, sib_send, sib_recv) = sems[:4], sems[4:]
    mine = place.half_row
    full[mine, place.me] = jnp.where(mine == 0, shards[0][...], shards[1][...])
    order = []

    def twin(i):
        ref = full.at[mine, 2 * order[i] + place.core]
        return remote(ref, ref, twin_send, twin_recv.at[i], place.twin)

    def to_twin(chip):
        order.append(chip)
        twin(len(order) - 1).start()

    passed = 0
    for _ in gather(place, full.at[mine], ring, to_twin):
        yield
        if passed + 1 < len(order):
            twin(passed).wait_recv()
            ref = full.at[1 - mine, 2 * order[passed] + place.core]
            remote(ref, ref, sib_send, sib_recv, place.sibling).start()
            passed += 1
    while passed < place.chips:
        yield
        twin(passed).wait_recv()
        ref = full.at[1 - mine, 2 * order[passed] + place.core]
        remote(ref, ref, sib_send, sib_recv, place.sibling).start()
        passed += 1
    yield
    every = full.at[0, pl.ds(0, place.chips)]
    wait_landed(every, sib_recv, place.sibling)
    wait_sent(every, sib_send, place.sibling)
    wait_sent(every, twin_send, place.twin)


def outs_scratch(n):
    return [*gather_scratch(n), DMA, DMA((n // 2,)), DMA, DMA]


def heads_task(place, span, o_ref, own, pairs, heads, sems):
    mate_send, mate_recv, *ring = sems
    mates = LANES // span
    rows = heads.shape[1]
    group, lane = place.me // mates, lax.rem(place.me, mates)
    for start in range(0, own.shape[0], 256):
        own[start : start + 256, :] = own_part(place, o_ref[start : start + 256, :], span).astype(bf16)

    def part(index):
        return own.at[pl.ds(pl.multiple_of(index * rows, rows), rows), :]

    def swap(r):
        other = lax.rem(lane + r, mates)
        return remote(
            part(other), pairs.at[lane], mate_send.at[r - 1], mate_recv.at[r - 1], (place.dp, group * mates + other)
        )

    for r in range(1, mates):
        swap(r).start()
    pairs[lane] = part(lane)[...]
    yield
    for r in range(1, mates):
        swap(r).wait_recv()
    heads[place.me] = jnp.concatenate([pairs[i] for i in range(mates)], axis=1)
    yield from gather(place, heads, ring)
    for r in range(1, mates):
        swap(r).wait_send()


def heads_scratch(n, span, length):
    mates = LANES // span
    return [
        VMEM((length, span), bf16),
        VMEM((mates, length // mates, span), bf16),
        VMEM((n, length // mates, LANES), bf16),
        DMA((mates - 1,)),
        DMA((mates - 1,)),
        *gather_scratch(n),
    ]


def heads_at(heads, mates, lane, start, count):
    return jnp.concatenate([heads[at + lane, pl.ds(start, count), :] for at in range(0, heads.shape[0], mates)], axis=1)


def own_heads(place, heads, mates, count):
    blocks = heads.shape[1] // count
    start = pl.multiple_of(lax.rem(place.me, blocks) * count, count)
    return heads_at(heads, mates, place.me // blocks, start, count)


def join_columns(place, span, mine, wide, theirs, landed, sems):
    mate_send, mate_recv, swap_send, swap_recv, own_sem, send, recv, twin_send, twin_recv = sems
    matrices, mates, _, _ = mine.shape
    groups = place.n // mates
    group, lane = place.me // mates, lax.rem(place.me, mates)
    half = place.half_row

    def swap(r):
        mate = group * mates + lax.rem(lane + r, mates)
        ref = mine.at[:, lane]
        return remote(ref, ref, mate_send.at[r - 1], mate_recv.at[r - 1], (place.dp, mate))

    def lanes(origin):
        return landed.at[:, half, :, pl.ds(pl.multiple_of(origin * LANES, LANES), LANES)]

    def move(step):
        target = lax.rem(group + step, groups) * mates + lane
        return remote(theirs.at[:, target], lanes(group), send, recv.at[step - 1], (place.dp, target))

    def pass_on(ref, origin):
        remote(ref, lanes(origin), twin_send, twin_recv, place.twin).start()

    for r in range(1, mates):
        swap(r).start()
    yield
    for r in range(1, mates):
        swap(r).wait_recv()
    for m in range(matrices):
        wide[m] = jnp.concatenate([mine[m, i] for i in range(mates)], axis=1).reshape(wide.shape[1:])
    across = remote(wide.at[:, :, 1 - half], theirs, swap_send, swap_recv, place.twin)
    across.start()
    yield
    yield
    yield
    across.wait_recv()
    for m in range(matrices):
        theirs[m] = (theirs[m].astype(f32) + wide[m, :, half].astype(f32)).astype(bf16)
    for step in range(1, groups):
        move(step).start()
    own = pltpu.make_async_copy(theirs.at[:, place.me], lanes(group), own_sem)
    own.start()
    pass_on(theirs.at[:, place.me], group)
    for step in range(1, groups):
        yield
        move(step).wait_recv()
        origin = lax.rem(group + groups - step, groups)
        pass_on(lanes(origin), origin)
    yield
    own.wait()
    across.wait_send()
    for r in range(1, mates):
        swap(r).wait_send()
    wait_sent(theirs.at[:, pl.ds(0, groups - 1)], send, place.sibling)
    wait_sent(landed.at[:, 0], twin_send, place.twin)
    wait_landed(landed.at[:, 0], twin_recv, place.twin)


def join_columns_scratch(n, span, depth, width, matrices):
    mates = LANES // span
    groups = n // mates
    return [
        VMEM((matrices, mates, width, span), bf16),
        VMEM((matrices, n, 2, depth // 2, LANES), bf16),
        VMEM((matrices, n, depth // 2, LANES), bf16),
        VMEM((matrices, 2, depth // 2, width), bf16),
        DMA((mates - 1,)),
        DMA((mates - 1,)),
        DMA, DMA, DMA, DMA,
        DMA((groups - 1,)),
        DMA, DMA,
    ]


def join_blocks(place, blocks, theirs, landed, sems, window=4):
    swap_send, swap_recv, own_sem, send, recv, twin_send, twin_recv = sems
    n, half = place.n, place.half_row

    def move(k):
        target = lax.rem(place.me + k, n)
        return remote(theirs.at[target], landed.at[place.me, half], send, recv.at[k - 1], (place.dp, target))

    def pass_on(ref, origin):
        remote(ref, landed.at[origin, half], twin_send, twin_recv, place.twin).start()

    across = remote(blocks.at[:, 1 - half], theirs, swap_send, swap_recv, place.twin)
    across.start()
    for _ in range(5):
        yield
    across.wait_recv()
    for device in range(n):
        theirs[device] = (theirs[device].astype(f32) + blocks[device, half].astype(f32)).astype(bf16)
    for k in range(1, window):
        move(k).start()
    own = pltpu.make_async_copy(theirs.at[place.me], landed.at[place.me, half], own_sem)
    own.start()
    pass_on(theirs.at[place.me], place.me)
    for k in range(1, n):
        yield
        if k + window - 1 < n:
            move(k + window - 1).start()
        move(k).wait_recv()
        origin = lax.rem(place.me + n - k, n)
        pass_on(landed.at[origin, half], origin)
    yield
    own.wait()
    across.wait_send()
    wait_sent(theirs.at[pl.ds(0, n - 1)], send, place.sibling)
    wait_sent(landed.at[:, 0], twin_send, place.twin)
    wait_landed(landed.at[:, 0], twin_recv, place.twin)


def join_blocks_scratch(n, part, columns):
    return [
        VMEM((n, part, columns), bf16), VMEM((n, 2, part, columns), bf16),
        DMA, DMA, DMA, DMA, DMA((n - 1,)), DMA, DMA,
    ]


def columns_home(n, ndp, span, depth, width, matrices):
    if ndp == 2:
        return join_columns_scratch(n, span, depth, width, matrices), shape(1, matrices, 2, depth // 2, width)
    return settle_columns_scratch(n, ndp, span, depth, width, matrices), shape(ndp, matrices, depth, width)


def columns_to_owners(place, ndp, span, scratch, out, sem, saves):
    if ndp == 2:
        mine, wide, theirs, landed, *sems = scratch
        yield from join_columns(place, span, mine, wide, theirs, landed, sems)
        saves.append(pltpu.make_async_copy(landed, out.at[0], sem))
    else:
        mine, wide, landed, *sems = scratch
        yield from settle_columns(place, ndp, span, mine, wide, landed, sems)
        saves.append(pltpu.make_async_copy(landed, out, sem))
    saves[-1].start()


def blocks_home(n, ndp, depth, columns):
    if ndp == 2:
        return join_blocks_scratch(n, depth // 2, columns), shape(1, n, 2, depth // 2, columns)
    return settle_blocks_scratch(n, ndp, (2, depth // 2, columns), bf16), shape(ndp, n, 2, depth // 2, columns)


def blocks_to_owners(place, ndp, blocks, scratch, out, sem, saves):
    if ndp == 2:
        theirs, landed, *sems = scratch
        yield from join_blocks(place, blocks, theirs, landed, sems)
        saves.append(pltpu.make_async_copy(landed, out.at[0], sem))
    else:
        landed, *sems = scratch
        yield from settle_blocks(place, ndp, lambda device: blocks.at[device], landed, sems)
        saves.append(pltpu.make_async_copy(landed, out, sem))
    saves[-1].start()


def roomy_at(n):
    return n <= 16


def open_stage(n, ndp, span, depth, count, width, slim):
    length = n * count
    roomy = roomy_at(n)
    mates = LANES // span

    def body(place, v, behind, first):
        v.x_all[place.me] = v.x[...]
        v.encoded[place.me] = v.enc[...]
        for i, ref in enumerate((v.wq, v.wk, v.wv, v.wcq, v.wck, v.wcv)):
            v.stack[i] = ref[...]
        segment = v.dec_seg[...].astype(f32)
        rows = [segment, jnp.where(v.dec_valid[...] == 1, segment, -1.0)]
        rows.append(jnp.where(v.enc_valid[...] == 1, v.enc_seg[...].astype(f32), -1.0))
        for ref in (v.gain_self, v.gain_cross, v.gain_feed):
            rows.append(jnp.concatenate([ref[...].astype(f32), jnp.zeros((1, LANES - depth), f32)], axis=1))
        rows.append(jnp.zeros((10, LANES), f32))
        v.mark[...] = jnp.concatenate(rows, axis=0).astype(bf16)
        v.marks_in[place.me] = v.mark[...]
        if first:
            greet(place.others() + peers(place, ndp))
        for other in place.others():
            remote(v.mark, v.marks_in.at[place.me], v.mark_send, v.mark_recv, other).start()
        side = lax.rem(place.me, mates) // (HEAD_DIM // span)

        def head(index):
            pair = v.buf[index]
            return jnp.where(side == 0, pair[:, :HEAD_DIM], pair[:, HEAD_DIM:])

        scale = HEAD_DIM ** (-0.5)
        gain, ready, waiting = [], [], []

        def begin(chip):
            if not ready:
                waiting.append(chip)
                return
            for b in (0, 1):
                v.normed_a[2 * chip + b] = normalise(v.x_all[2 * chip + b].astype(f32), gain[0]).astype(bf16)
            rows = rows_of(chip, count)
            qkv = mm(chip_rows(v.normed_a, chip), v.w_self[...])
            v.q1[rows, :] = (qkv[:, :HEAD_DIM].astype(bf16).astype(f32) * scale).astype(bf16)
            v.k1[rows, :] = qkv[:, HEAD_DIM : 2 * HEAD_DIM].astype(bf16)
            v.v1[rows, :] = qkv[:, 2 * HEAD_DIM :].astype(bf16)

        def cross(chip):
            if len(ready) < 2:
                waiting.append(chip)
                return
            rows = rows_of(chip, count)
            kv = mm(chip_rows(v.encoded, chip), v.w_ckv[...])
            v.k2[rows, :] = kv[:, :HEAD_DIM].astype(bf16)
            v.v2[rows, :] = kv[:, HEAD_DIM:].astype(bf16)

        def background():
            weights = columns_task(place, span, v.stack, v.buf, 4, 6, v.late)
            next(weights)
            for _ in gather(place, v.encoded, v.ring_enc, cross):
                yield
                if len(ready) < 2 and next(weights, "done") == "done":
                    v.w_ckv[...] = jnp.concatenate([head(4), head(5)], axis=1)
                    v.w_ckv_own[...] = jnp.concatenate([own_part(place, head(i), span) for i in (4, 5)], axis=1)
                    ready.append(True)
                    for chip in waiting:
                        cross(chip)
            v.saves.append(pltpu.make_async_copy(v.encoded, v._encoded, v.open_out.at[1]))
            v.saves[-1].start()

        def outs():
            yield from outs_task(place, (v.out_self, v.out_cross), v.outs_all, v.outs_in)
            v.saves.append(pltpu.make_async_copy(v.outs_all, v._outs_all, v.open_out.at[2]))
            v.saves[-1].start()

        weights = columns_task(place, span, v.stack, v.buf, 0, 4, v.early)
        next(weights)
        ring = gather(place, v.x_all, v.ring_x, begin)
        v.outs_task = outs()
        behind = one_by_one(behind, v.outs_task, background())
        for number, _ in enumerate(ring):
            if not ready and next(weights, "done") == "done":
                ref = v.marks_in.at[pl.ds(0, n - 1)]
                wait_landed(ref, v.mark_recv, place.sibling)
                wait_sent(ref, v.mark_send, place.sibling)
                v.marks[...] = v.marks_in[...]
                gain.append(gain_row(v.marks, 3, depth))
                v.w_self[...] = jnp.concatenate([head(0), head(1), head(2)], axis=1)
                v.w_self_own[...] = jnp.concatenate([own_part(place, head(i), span) for i in range(3)], axis=1)
                v.w_cq[...] = head(3)
                ready.append(True)
                for chip in waiting:
                    begin(chip)
                waiting.clear()
            elif ready and number % 2:
                next(behind, None)
        v.saves.append(pltpu.make_async_copy(v.normed_a, v._normed_one, v.open_out.at[0]))
        v.saves[-1].start()
        if not roomy:
            v.saves.append(pltpu.make_async_copy(v.x_all, v._x_all, v.open_out.at[3]))
            v.saves[-1].start()
        column, row = mark_columns(v.marks, 0), mark_row(v.marks, 1)
        beside(attend_forward(True, v.q1, v.k1, v.v1, column, row, v.o1, v.l1), behind)
        return behind

    head = shape(length, HEAD_DIM)
    gathered = shape(n, count, width)
    return Stage(
        body,
        ["x", "enc", "wq", "wk", "wv", "wcq", "wck", "wcv", "dec_seg", "dec_valid", "enc_seg", "enc_valid"]
        + ["gain_self", "gain_cross", "gain_feed", "out_self", "out_cross"],
        dict(
            **({} if roomy else dict(_x_all=gathered)),
            _outs_all=shape(2, n, depth, width), _normed_one=gathered, _encoded=gathered, q1=head, k1=head, v1=head, o1=shape(length, HEAD_DIM, kind=f32),
            l1=shape(1, length, kind=f32), k2=head, v2=head, w_self_own=shape(width, 3 * span),
            w_cq=shape(width, HEAD_DIM), w_ckv_own=shape(width, 2 * span), marks=shape(n, 16, LANES),
        ),
        dict(
            x_all=VMEM((n, count, width), bf16), normed_a=VMEM((n, count, width), bf16),
            encoded=VMEM((n, count, width), bf16), stack=VMEM((6, depth, width), bf16), buf=VMEM((6, width, LANES), bf16),
            w_self=VMEM((width, 3 * HEAD_DIM), bf16), w_ckv=VMEM((width, 2 * HEAD_DIM), bf16), mark=VMEM((16, LANES), bf16),
            marks_in=VMEM((n, 16, LANES), bf16), mark_send=DMA, mark_recv=DMA, open_out=DMA((4,)),
            outs_all=VMEM((2, n, depth, width), bf16), outs_in=outs_scratch(n),
            ring_x=gather_scratch(n), ring_enc=gather_scratch(n), early=columns_scratch(n, span),
            late=columns_scratch(n, span),
        ),
    )


def cross_stage(n, ndp, span, depth, count, width, slim):
    length = n * count
    roomy = roomy_at(n)
    mates = LANES // span

    def body(place, v, behind, first):
        kept = jnp.broadcast_to(v.dec_valid[...].astype(f32), (LANES, LANES)).T[:, :1]
        v.low_a[place.me] = (v.cotangent[...].astype(f32) * kept).astype(bf16)
        gain = gain_row(v.marks, 4, depth)
        if first:
            loads = [
                pltpu.make_async_copy(v._x_all, v.x_all, v.cross_load.at[0]),
                pltpu.make_async_copy(v._outs_all, v.outs_all, v.cross_load.at[1]),
            ]
            for load in loads:
                load.start()
            greet(place.others() + peers(place, ndp))
            for load in loads:
                load.wait()
        own, pairs, heads, *head_sems = v.heads_a

        blocks = n // 2 // mates

        def project(chip):
            step, rows = 2 * count, rows_of(chip, count)
            weight = v.outs_all[0].reshape(width, width)
            start = pl.multiple_of(lax.rem(chip, blocks) * step, step)
            value = mm(heads_at(heads, mates, chip // blocks, start, step), weight)
            value = value + chip_rows(v.x_all, chip).astype(f32)
            normed = normalise(value, gain).astype(bf16)
            value = value.astype(bf16)
            for b in (0, 1):
                v.x_all[2 * chip + b] = value[b * count : (b + 1) * count]
                v.normed_b[2 * chip + b] = normed[b * count : (b + 1) * count]
            query = mm(normed, v.w_cq[...]).astype(bf16)
            v.q2[rows, :] = (query.astype(f32) * HEAD_DIM ** (-0.5)).astype(bf16)

        def project_each():
            for chip in range(n // 2):
                project(jnp.int32(chip))
                yield

        def weights():
            for device in range(n):
                columns = slice(device * slim, (device + 1) * slim)
                both = [ref[:, columns].astype(f32) for ref in (v.gate, v.up)]
                v.targets[device] = jnp.concatenate(both, axis=1).astype(bf16)
            yield
            yield from share_blocks(place, v.targets, v.w_feed_in, v.feed_in)
            v.saves.append(pltpu.make_async_copy(v.w_feed_in, v._w_feed, v.cross_out.at[2]))
            v.saves[-1].start()

        def lows():
            yield from gather(place, v.low_a, v.ring_low)
            v.saves.append(pltpu.make_async_copy(v.low_a, v._low_all, v.cross_out.at[1]))
            v.saves[-1].start()

        behind = in_turn(behind, weights(), lows())
        beside(heads_task(place, span, v.o1, own, pairs, heads, head_sems), behind)
        if not first:
            drain(v.outs_task)
        v.resid_one[...] = mm(own_heads(place, heads, mates, count), v.outs_all[0].reshape(width, width))
        v.resid_one[...] += v.x[...].astype(f32)
        if first:
            pl.loop(0, n // 2)(project)
        else:
            beside(project_each(), behind, 3)
        for i, (source, target) in enumerate(((v.normed_b, v._normed_two), (v.x_all, v._resid_all))):
            v.saves.append(pltpu.make_async_copy(source, target, v.cross_out.at[3 * i]))
            v.saves[-1].start()
        column, row = mark_columns(v.marks, 0), mark_row(v.marks, 2)
        if first:
            beside(attend_forward(False, v.q2, v.k2, v.v2, column, row, v.o2, v.l2), behind, 3)
        else:
            drain(behind)
            drain(attend_forward(False, v.q2, v.k2, v.v2, column, row, v.o2, v.l2))
        return behind

    gathered = shape(n, count, width)
    return Stage(
        body,
        ["o1", "x", "marks", "w_cq", "k2", "v2", "cotangent", "dec_valid", "gate", "up"]
        + ([] if roomy else ["_x_all", "_outs_all"]),
        dict(
            resid_one=shape(count, width, kind=f32), _normed_two=gathered, _low_all=gathered, _resid_all=gathered, q2=shape(length, HEAD_DIM),
            o2=shape(length, HEAD_DIM, kind=f32), l2=shape(1, length, kind=f32), _w_feed=shape(n, depth, 2 * slim),
        ),
        dict(
            normed_b=VMEM((n, count, width), bf16), low_a=VMEM((n, count, width), bf16),
            targets=VMEM((n, depth, 2 * slim), bf16), w_feed_in=VMEM((n, depth, 2 * slim), bf16), cross_out=DMA((4,)),
            cross_load=DMA((2,)), x_all=VMEM((n, count, width), bf16), outs_all=VMEM((2, n, depth, width), bf16),
            ring_low=gather_scratch(n), heads_a=heads_scratch(n, span, length), feed_in=share_scratch(n),
        ),
    )


def norm_back(values, gain, grad):
    r = lax.rsqrt(jnp.mean(values * values, axis=-1, keepdims=True) + epsilon)
    scaled = grad * gain
    inner = jnp.mean(values * scaled, axis=-1, keepdims=True)
    return r * scaled - values * (r * r * r * inner), grad * values * r


def gelu_pair(v):
    c = 0.7978845608028654
    square = v * v
    t = jnp.tanh(c * v * (1.0 + 0.044715 * square))
    value = 0.5 * v * (1.0 + t)
    slope = 0.5 * (1.0 + t) + 0.5 * c * v * (1.0 - t * t) * (1.0 + 3.0 * 0.044715 * square)
    return value, slope


def feed_stage(n, ndp, span, depth, count, width, slim):
    length = n * count
    mates = LANES // span

    def body(place, v, behind, first):
        loads = [
            pltpu.make_async_copy(v._low_all, v.low_b, v.feed_load.at[0]),
            pltpu.make_async_copy(v._w_feed, v.w_feed, v.feed_load.at[1]),
            pltpu.make_async_copy(v._resid_all, v.normed_c, v.feed_load.at[2]),
            pltpu.make_async_copy(v._outs_all.at[1], v.out_cross_all, v.feed_load.at[3]),
        ]
        for load in loads:
            load.start()
        gain = gain_row(v.marks, 5, depth)
        if first:
            greet(place.others() + peers(place, ndp))

        own, pairs, heads, *head_sems = v.heads_c

        weight = v.out_cross_all
        blocks = n // 2 // mates
        made = []

        def feed(chip):
            made.append(chip)
            step, rows = 2 * count, rows_of(chip, count)
            start = pl.multiple_of(lax.rem(chip, blocks) * step, step)
            value = mm(heads_at(heads, mates, chip // blocks, start, step), weight[...].reshape(width, width))
            value = value + chip_rows(v.normed_c, chip).astype(f32)
            block = normalise(value, gain).astype(bf16)
            for b in (0, 1):
                v.normed_c[2 * chip + b] = block[b * count : (b + 1) * count]
            both = mm(block, v.w_feed[...].reshape(width, 2 * slim))
            gate, upward = both[:, :slim], both[:, slim:]
            value, slope = gelu_pair(gate)
            grad = mm_nt(chip_rows(v.low_b, chip), v.down[...])
            v.hidden[rows, :] = (value * upward).astype(bf16)
            both = jnp.concatenate([grad * upward * slope, grad * value], axis=1).astype(bf16)
            v.d_both[rows, :] = both
            return both

        def produce_back(chip):
            return mm_nt(feed(chip), v.w_feed[...].reshape(width, 2 * slim))

        def finish_back(k, value):
            rows = piece_rows(k, count)
            grad, part = norm_back(v.resid_two[rows, :], gain, value)
            v.grad_two[rows, :] = v.low_b[place.me, rows, :].astype(f32) + grad
            part = jnp.sum(part, axis=0, keepdims=True)
            v.tip_three[...] = part if k == 0 else v.tip_three[...] + part

        def weight_grads():
            step = 256
            while len(made) < n // 2:
                yield
            for start in range(0, width, step):
                columns = slice(start, start + step)
                left = v.normed_c[:, :, columns].reshape(length, step)
                value = mm_tn(left, v.d_both[...]).astype(bf16)
                v.feed_grad[start // depth : (start + step) // depth] = value.reshape(step // depth, 2, depth // 2, 2 * slim)
                yield
                left = v.low_b[:, :, columns].reshape(length, step)
                v.down_grad[:, columns] = mm_tn(v.hidden[...], left).astype(bf16)
                yield

        beside(heads_task(place, span, v.o2, own, pairs, heads, head_sems), behind)
        for load in loads:
            load.wait()
        v.resid_two[...] = mm(own_heads(place, heads, mates, count), weight[...].reshape(width, width)) + v.resid_one[...]
        grads = weight_grads()
        beside(scatter(place, v.sums_c, produce_back, finish_back), in_turn(behind, grads))
        drain(grads)
        return behind

    return Stage(
        body,
        ["o2", "resid_one", "marks", "_w_feed", "down", "_low_all", "_resid_all", "_outs_all"],
        dict(
            resid_two=shape(count, width, kind=f32), grad_two=shape(count, width, kind=f32),
            tip_three=shape(1, width, kind=f32), hidden=shape(length, slim), feed_grad=shape(n, 2, depth // 2, 2 * slim),
            down_grad=shape(slim, width),
        ),
        dict(
            normed_c=VMEM((n, count, width), bf16), low_b=VMEM((n, count, width), bf16),
            w_feed=VMEM((n, depth, 2 * slim), bf16), d_both=VMEM((length, 2 * slim), bf16), feed_load=DMA((4,)),
            out_cross_all=VMEM((n, depth, width), bf16), heads_c=heads_scratch(n, span, length), sums_c=scatter_scratch(n, count, width),
        ),
    )


def own_grads(place, span, sources, target):
    step = 256
    for start in range(0, target.shape[0], step):
        rows = slice(start, start + step)
        parts = [own_part(place, source[rows, :].astype(bf16), span) for source in sources]
        target[rows, :] = jnp.concatenate(parts, axis=1)


def cross_back_stage(n, ndp, span, depth, count, width, slim):
    length = n * count

    def body(place, v, behind, first):
        v.low_c[place.me] = v.grad_two[...].astype(bf16)
        v.out_sum_c[...] = jnp.zeros_like(v.out_sum_c)
        if first:
            greet(place.others() + peers(place, ndp))

        def into(chip):
            block, rows = chip_rows(v.low_c, chip), rows_of(chip, count)
            v.d_attn_c[rows, :] = mm_nt(block, v.out_cross_head[...]).astype(bf16)
            v.out_sum_c[...] += mm_tn(own_part(place, v.o2[rows, :], span).astype(bf16), block)

        def produce(chip):
            return mm(v.hidden[rows_of(chip, count), :], v.down[...])

        def finish(k, value):
            rows = piece_rows(k, count)
            v.mixed[rows, :] = (v.resid_two[rows, :] + value).astype(bf16)

        downs, *down_sems = v.down_back
        behind = in_turn(
            behind,
            blocks_to_owners(place, ndp, v.feed_grad, v.feed_back, v._feeds, v.back_out.at[0], v.saves),
            settle_rows(place, ndp, (v.down_grad,), downs, down_sems),
        )
        beside(gather(place, v.low_c, v.ring_d, into), behind)
        behind = in_turn(behind, scatter(place, v.sums_c, produce, finish))
        row, column = mark_row(v.marks, 0), mark_columns(v.marks, 2)
        attention = attend_backward(
            False, v.q2, v.k2, v.v2, v.d_attn_c, v.o2, v.l2, row, column, v.d_attn_c, v.dk_c, v.dv_c
        )
        beside(attention, behind, 3)
        drain(behind)
        v.saves.append(pltpu.make_async_copy(downs, v._downs, v.back_out.at[1]))
        v.saves[-1].start()
        own_grads(place, span, (v.d_attn_c,), v.dq2)
        own_grads(place, span, (v.dk_c, v.dv_c), v.dkv2)
        v.out_two[...] = v.out_sum_c[...].astype(bf16)
        return iter(())

    return Stage(
        body,
        ["grad_two", "out_cross_head", "o2", "l2", "q2", "k2", "v2", "marks", "hidden", "down", "resid_two", "feed_grad"]
        + ["down_grad"],
        dict(
            dq2=shape(length, span), dkv2=shape(length, 2 * span), out_two=shape(span, width), mixed=shape(count, width),
            _feeds=blocks_home(n, ndp, depth, 2 * slim)[1], _downs=shape(ndp, slim, width),
        ),
        dict(
            low_c=VMEM((n, count, width), bf16), d_attn_c=VMEM((length, HEAD_DIM), bf16),
            dk_c=VMEM((length, HEAD_DIM), f32), dv_c=VMEM((length, HEAD_DIM), f32),
            out_sum_c=VMEM((span, width), f32), back_out=DMA((2,)), ring_d=gather_scratch(n),
            sums_c=scatter_scratch(n, count, width), feed_back=blocks_home(n, ndp, depth, 2 * slim)[0],
            down_back=settle_rows_scratch(ndp, slim, width, 1),
        ),
    )


def self_back_stage(n, ndp, span, depth, count, width, slim):
    length = n * count
    roomy = roomy_at(n)

    def body(place, v, behind, first):
        lane = lax.rem(place.me, LANES // span)
        mine = v.columns_e[0]
        outs, *out_sems = v.outs_e
        loads = [
            pltpu.make_async_copy(ref, v.saved, v.self_load.at[i]) for i, ref in enumerate((v._normed_two, v._encoded))
        ]
        loads[0].start()
        gain = gain_row(v.marks, 4, depth)
        v.out_sum_e[...] = jnp.zeros_like(v.out_sum_e)
        v.w_cq_own[...] = own_part(place, v.w_cq[...], span)
        if first:
            greet(place.others() + peers(place, ndp))

        def produce(chip):
            return mm_nt(v.dq2[rows_of(chip, count), :], v.w_cq_own[...])

        def finish(k, value):
            rows = piece_rows(k, count)
            grad, part = norm_back(v.resid_one[rows, :], gain, value)
            grad = v.grad_two[rows, :] + grad
            v.grad_one[rows, :] = grad
            v.low_e[place.me, rows, :] = grad.astype(bf16)
            part = jnp.sum(part, axis=0, keepdims=True)
            v.tip_two[...] = part if k == 0 else v.tip_two[...] + part

        def weight_grads():
            step = 256
            loads[0].wait()
            for start in range(0, width, step):
                columns = slice(start, start + step)
                left = v.saved[:, :, columns].reshape(length, step)
                mine[0, lane, columns, :] = mm_tn(left, v.dq2[...]).astype(bf16)
                yield
            loads[1].start()
            yield
            loads[1].wait()
            for start in range(0, width, step):
                columns = slice(start, start + step)
                left = v.saved[:, :, columns].reshape(length, step)
                value = mm_tn(left, v.dkv2[...]).astype(bf16)
                mine[1, lane, columns, :] = value[:, :span]
                mine[2, lane, columns, :] = value[:, span:]
                yield

        def into(chip):
            block, rows = chip_rows(v.low_e, chip), rows_of(chip, count)
            v.d_attn_e[rows, :] = mm_nt(block, v.out_self_head[...]).astype(bf16)
            v.out_sum_e[...] += mm_tn(own_part(place, v.o1[rows, :], span).astype(bf16), block)

        def produce_enc(chip):
            return mm_nt(v.dkv2[rows_of(chip, count), :], v.w_ckv_own[...])

        def finish_enc(k, value):
            v.enc_grad[piece_rows(k, count), :] = value

        def rests():
            yield from settle_rows(place, ndp, (v.out_two,), outs, out_sems)
            v.saves.append(pltpu.make_async_copy(outs, v._outs_two, v.self_load.at[3]))
            v.saves[-1].start()

        grads = weight_grads()
        beside(scatter(place, v.sums_e, produce, finish), in_turn(behind, grads))
        drain(grads)
        encs = scatter(place, v.sums_f if roomy else v.sums_e, produce_enc, finish_enc)
        columns = columns_to_owners(place, ndp, span, v.columns_e, v._columns_two, v.self_load.at[2], v.saves)
        behind = in_turn(behind, columns, rests(), *([encs] if roomy else []))
        beside(gather(place, v.low_e, v.ring_e, into), behind, 1, 3)
        if not roomy:
            behind = in_turn(behind, encs)
        row, column = mark_row(v.marks, 0), mark_columns(v.marks, 1)
        attention = attend_backward(
            True, v.q1, v.k1, v.v1, v.d_attn_e, v.o1, v.l1, row, column, v.d_attn_e, v.dk_e, v.dv_e
        )
        beside(attention, behind, 2)
        own_grads(place, span, (v.d_attn_e, v.dk_e, v.dv_e), v.grads_one)
        v.out_one[...] = v.out_sum_e[...].astype(bf16)
        return behind

    rows = shape(count, width, kind=f32)
    return Stage(
        body,
        ["dq2", "dkv2", "w_cq", "w_ckv_own", "resid_one", "grad_two", "marks", "out_self_head", "o1", "l1", "q1", "k1", "v1"]
        + ["out_two", "_normed_two", "_encoded"],
        dict(
            grads_one=shape(length, 3 * span), out_one=shape(span, width), grad_one=rows, enc_grad=rows,
            tip_two=shape(1, width, kind=f32), _columns_two=columns_home(n, ndp, span, depth, width, 3)[1], _outs_two=shape(ndp, span, width),
        ),
        dict(
            saved=VMEM((n, count, width), bf16), low_e=VMEM((n, count, width), bf16),
            d_attn_e=VMEM((length, HEAD_DIM), bf16),
            dk_e=VMEM((length, HEAD_DIM), f32), dv_e=VMEM((length, HEAD_DIM), f32), out_sum_e=VMEM((span, width), f32),
            w_cq_own=VMEM((width, span), bf16), self_load=DMA((4,)), ring_e=gather_scratch(n),
            sums_e=scatter_scratch(n, count, width),
            columns_e=columns_home(n, ndp, span, depth, width, 3)[0], outs_e=settle_rows_scratch(ndp, span, width, 1),
            **(dict(sums_f=scatter_scratch(n, count, width)) if roomy else {}),
        ),
    )


def close_stage(n, ndp, span, depth, count, width, slim):
    length = n * count
    mates = LANES // span

    def body(place, v, behind, first):
        lane = lax.rem(place.me, mates)
        mine = v.columns_g[0]
        outs, *out_sems = v.outs_g
        tips, *tip_sems = v.tips_g
        load = pltpu.make_async_copy(v._normed_one, v.saved, v.close_load.at[0])
        load.start()
        gain = gain_row(v.marks, 3, depth)
        v.tip_all[...] = jnp.zeros_like(v.tip_all)
        v.tip_all[1:2, :] = v.tip_two[...]
        v.tip_all[2:3, :] = v.tip_three[...]
        if first:
            greet(place.others() + peers(place, ndp))

        def produce(chip):
            return mm_nt(v.grads_one[rows_of(chip, count), :], v.w_self_own[...])

        def finish(k, value):
            rows = piece_rows(k, count)
            grad, part = norm_back(v.x[rows, :].astype(f32), gain, value)
            v.dec_grad[rows, :] = v.grad_one[rows, :] + grad
            v.tip_all[0:1, :] += jnp.sum(part, axis=0, keepdims=True)

        def columns():
            load.wait()
            step = 256
            for start in range(0, width, step):
                columns = slice(start, start + step)
                value = mm_tn(v.saved[:, :, columns].reshape(length, step), v.grads_one[...]).astype(bf16)
                for i in range(3):
                    mine[i, lane, columns, :] = value[:, i * span : (i + 1) * span]
                yield
            yield from columns_to_owners(place, ndp, span, v.columns_g, v._columns_one, v.close_load.at[1], v.saves)

        def tip(device):
            return v.tip_all.at[:, pl.ds(pl.multiple_of(device // mates * LANES, LANES), LANES)]

        behind = in_turn(columns(), settle_rows(place, ndp, (v.out_one,), outs, out_sems), behind)
        beside(scatter(place, v.sums_e, produce, finish), behind)
        drain(in_turn(settle_tips(place, ndp, tip, tips, tip_sems), behind))
        for i, (source, target) in enumerate(((outs, v._outs_one), (tips, v._tips))):
            v.saves.append(pltpu.make_async_copy(source, target, v.close_load.at[i + 2]))
            v.saves[-1].start()
        return iter(())

    return Stage(
        body,
        ["grads_one", "w_self_own", "x", "grad_one", "marks", "out_one", "tip_two", "tip_three", "_normed_one"],
        dict(
            dec_grad=shape(count, width, kind=f32), _columns_one=columns_home(n, ndp, span, depth, width, 3)[1],
            _outs_one=shape(ndp, span, width), _tips=shape(ndp * n, 8, LANES, kind=f32),
        ),
        dict(
            saved=VMEM((n, count, width), bf16), tip_all=VMEM((8, width), f32), close_load=DMA((4,)),
            sums_e=scatter_scratch(n, count, width), columns_g=columns_home(n, ndp, span, depth, width, 3)[0],
            outs_g=settle_rows_scratch(ndp, span, width, 1), tips_g=settle_tips_scratch(n, ndp),
        ),
    )


def over_dp(landed, *index):
    return sum(landed[(d, *index)].astype(f32) for d in range(landed.shape[0]))


def total_kernel(
    n, span,
    *refs,
):
    sources, targets, rest = refs[:7], refs[7:19], refs[19:]
    gains_out, q_out, k_out, v_out, out_one, cq_out, ck_out, cv_out, out_two, gate_out, up_out, down_out = targets
    columns_one, columns_two, outs_one, outs_two, feeds, downs, tips = rest[:7]
    loads = [pltpu.make_async_copy(a, b, rest[7].at[i]) for i, (a, b) in enumerate(zip(sources, rest))]
    for load in loads:
        load.start()
    for load in loads:
        load.wait()
    for i, ref in enumerate((q_out, k_out, v_out)):
        ref[...] = over_dp(columns_one, i).reshape(ref.shape)
    for i, ref in enumerate((cq_out, ck_out, cv_out)):
        ref[...] = over_dp(columns_two, i).reshape(ref.shape)
    out_one[...] = over_dp(outs_one)
    out_two[...] = over_dp(outs_two)
    down_out[...] = over_dp(downs)
    slim = gate_out.shape[1] // n
    for i in range(n):
        piece = over_dp(feeds, i).reshape(gate_out.shape[0], 2 * slim)
        gate_out[:, i * slim : (i + 1) * slim] = piece[:, :slim]
        up_out[:, i * slim : (i + 1) * slim] = piece[:, slim:]
    total = over_dp(tips)
    mates = LANES // span
    lane = lax.rem(lax.axis_index("blk"), mates)
    part = total[:, :span]
    for i in range(1, mates):
        part = jnp.where(lane == i, total[:, i * span : (i + 1) * span], part)
    gains_out[...] = part


def total_grads(n, span, columns_one, columns_two, outs_one, outs_two, feeds, downs, tips):
    width = columns_one.shape[-1]
    depth = columns_one.size // columns_one.shape[0] // 3 // width
    slim = downs.shape[1]
    arrays = (columns_one, columns_two, outs_one, outs_two, feeds, downs, tips)

    square, out = shape(depth, width, kind=f32), shape(span, width, kind=f32)
    return pl.pallas_call(
        functools.partial(total_kernel, n, span),
        out_shape=(
            shape(8, span, kind=f32), square, square, square, out, square, square, square, out,
            shape(depth, n * slim, kind=f32), shape(depth, n * slim, kind=f32), shape(slim, width, kind=f32),
        ),
        in_specs=[pl.BlockSpec(memory_space=pl.ANY)] * 7,
        scratch_shapes=[VMEM(x.shape, x.dtype) for x in arrays] + [DMA((7,))],
        compiler_params=pltpu.CompilerParams(vmem_limit_bytes=56 * 1024 * 1024),
        name="total_grads",
    )(*arrays)


def local(
    n,
    ndp,
    dec_in,
    enc_out,
    cotangent,
    dec_seg,
    dec_valid,
    enc_seg,
    enc_valid,
    self_gain,
    self_query,
    self_key,
    self_value,
    self_out,
    cross_gain,
    cross_query,
    cross_key,
    cross_value,
    cross_out,
    feed_gain,
    feed_gate,
    feed_up,
    feed_down,
):
    width = dec_in.shape[2]
    depth = self_query.shape[0]
    span = width // n
    share = HEAD_DIM // span

    def whole_head(weight):
        if share == 1:
            return weight
        groups = [[h * share + i for i in range(share)] for h in range(n // share)]
        return lax.all_gather(weight, "blk", axis=0, tiled=True, axis_index_groups=groups)

    count, slim = dec_in.shape[1], feed_gate.shape[1] // n
    arrays = dict(
        x=dec_in[0], enc=enc_out[0], cotangent=cotangent[0],
        dec_seg=dec_seg, dec_valid=dec_valid, enc_seg=enc_seg, enc_valid=enc_valid,
        gain_self=self_gain[None], gain_cross=cross_gain[None], gain_feed=feed_gain[None],
        wq=self_query, wk=self_key, wv=self_value, wcq=cross_query, wck=cross_key, wcv=cross_value,
        out_self=self_out, out_cross=cross_out, gate=feed_gate, up=feed_up, down=feed_down,
        out_self_head=whole_head(self_out), out_cross_head=whole_head(cross_out),
    )
    stages = [
        (name, make(n, ndp, span, depth, count, width, slim))
        for name, make in (
            ("open", open_stage), ("cross", cross_stage), ("feed", feed_stage),
            ("cross_back", cross_back_stage), ("self_back", self_back_stage), ("close", close_stage),
        )
    ]
    size = 2 if roomy_at(n) else 1
    results = {"mixed", "dec_grad", "enc_grad", "_columns_one", "_columns_two", "_outs_one", "_outs_two"}
    results |= {"_feeds", "_downs", "_tips"}
    for at in range(0, len(stages), size):
        later = {key for _, stage in stages[at + size :] for key in stage.inputs}
        group = stages[at : at + size]
        name = "_and_".join(key for key, _ in group)
        fused(name, at, n, ndp, [stage for _, stage in group], arrays, later | results)
    gains, q, k, v, o, cq, ck, cv, co, gate, up, down = total_grads(
        n, span, *(arrays[key] for key in ("_columns_one", "_columns_two", "_outs_one", "_outs_two", "_feeds", "_downs", "_tips"))
    )
    return (
        arrays["mixed"][None], arrays["dec_grad"][None], arrays["enc_grad"][None],
        gains[0], q, k, v, o,
        gains[1], cq, ck, cv, co,
        gains[2], gate, up, down,
    )


def solution(mesh):
    row, token = P("dp", "blk"), P("dp", "blk", None)
    gain, weight = P("blk"), P("blk", None)
    return jax.shard_map(
        functools.partial(local, mesh.shape["blk"], mesh.shape["dp"]),
        mesh=mesh,
        in_specs=(token,) * 3 + (row,) * 4 + ((gain,) + (weight,) * 4) * 2 + (gain,) + (weight,) * 3,
        out_specs=(token,) * 3 + ((gain,) + (weight,) * 4) * 2 + (gain,) + (weight,) * 3,
        check_vma=False,
    )
```

```python
import functools
import types

import jax
import jax.numpy as jnp
from jax import lax
from jax.experimental import pallas as pl
from jax.experimental.pallas import tpu as pltpu
from jax.sharding import PartitionSpec as P

HEADS = 16
HEAD_DIM = 64
LANES = 128
PIECES = 2
epsilon = 1e-06
negative = -1e30
MESH = pl.DeviceIdType.MESH
bf16 = jnp.bfloat16
f32 = jnp.float32
VMEM = pltpu.VMEM
DMA = pltpu.SemaphoreType.DMA


def contract(left, right, dims):
    return lax.dot_general(left, right, ((dims[:1], dims[1:]), ((), ())), preferred_element_type=f32)


def mm(left, right):
    return contract(left, right, (1, 0))


def mm_nt(left, right):
    return contract(left, right, (1, 1))


def mm_tn(left, right):
    return contract(left, right, (0, 0))


class Place:
    def __init__(self, n):
        self.n, self.chips = n, n // 2
        self.half = self.chips // 2
        self.dp, self.me = lax.axis_index("dp"), lax.axis_index("blk")
        self.core = lax.rem(self.me, 2)
        chip = self.me // 2
        y, z = lax.rem(chip, 2), chip // 2
        self.pos = z + y * (self.chips - 1 - 2 * z)
        self.sibling = (self.dp, self.me + 1 - 2 * self.core)
        self.half_row = lax.rem(self.dp, 2)
        self.twin = (self.dp + 1 - 2 * self.half_row, self.me)
        self.sides = tuple((self.dp, 2 * self.chip(step) + self.core) for step in (1, -1))

    def chip(self, offset):
        position = lax.rem(self.pos + offset + 2 * self.chips, self.chips)
        side = position // (self.chips // 2)
        return 2 * (position + side * (self.chips - 1 - 2 * position)) + side

    def others(self):
        return [(self.dp, lax.rem(self.me + k, self.n)) for k in range(1, self.n)]

    def around(self):
        return [self.sibling, *self.sides]


def greet(partners):
    barrier = pltpu.get_barrier_semaphore()
    for partner in partners:
        pl.semaphore_signal(barrier, inc=1, device_id=partner, device_id_type=MESH)
    pl.semaphore_wait(barrier, len(partners))


def remote(src, dst, send, recv, device):
    return pltpu.make_async_remote_copy(
        src_ref=src, dst_ref=dst, send_sem=send, recv_sem=recv, device_id=device, device_id_type=MESH
    )


def wait_sent(ref, sem, device):
    remote(ref, ref, sem, sem, device).wait_send()


def wait_landed(ref, sem, device):
    remote(ref, ref, sem, sem, device).wait_recv()


def pieces_of(half, way, step):
    if step < half - 1:
        return tuple(range(PIECES))
    return tuple(range(PIECES // 2)) if way == 0 else tuple(range(PIECES // 2, PIECES))


def drain(task):
    for _ in task:
        pass


def beside(main, task, waits=1, steps=1):
    for count, _ in enumerate(main):
        if (count + 1) % steps == 0:
            for _ in range(waits):
                next(task, None)


def in_turn(*tasks):
    tasks = list(tasks)
    while tasks:
        for task in list(tasks):
            if next(task, "done") == "done":
                tasks.remove(task)
            else:
                yield


def one_by_one(*tasks):
    for task in tasks:
        yield from task


def gather_scratch(n):
    half = n // 4
    return [DMA, DMA((2, half, PIECES)), DMA, DMA((n // 2,))]


def gather(place, buf, sems, use=None):
    ring_send, ring_recv, sib_send, sib_recv = sems
    half, part = place.half, buf.shape[1] // PIECES

    def ring(way, step, k):
        ref = buf.at[2 * place.chip(-step if way == 0 else step) + place.core, pl.ds(k * part, part)]
        return remote(ref, ref, ring_send, ring_recv.at[way, step, k], place.sides[way])

    def across(offset):
        ref = buf.at[2 * place.chip(offset) + place.core]
        return remote(ref, ref, sib_send, sib_recv.at[offset + half - 1], place.sibling)

    def ready(offset):
        across(offset).wait_recv()
        if use is not None:
            use(place.chip(offset))

    for i in range(PIECES):
        for way in (0, 1):
            k = i if way == 0 else PIECES - 1 - i
            if k in pieces_of(half, way, 0):
                ring(way, 0, k).start()
    across(0).start()
    for step in range(half):
        for i in range(PIECES):
            for way in (0, 1):
                k = i if way == 0 else PIECES - 1 - i
                if k not in pieces_of(half, way, step):
                    continue
                yield
                ring(way, step, k).wait_recv()
                if step + 1 < half and k in pieces_of(half, way, step + 1):
                    ring(way, step + 1, k).start()
                if step + 1 < half and i == PIECES - 1:
                    across(-1 - step if way == 0 else step + 1).start()
        if step + 1 == half:
            across(half).start()
        for way in (0, 1) if step else (0,):
            ready(-step if way == 0 else step)
    yield
    ready(half)
    wait_sent(buf.at[pl.ds(0, place.chips - 1)], ring_send, place.sides[0])
    wait_sent(buf.at[pl.ds(0, place.chips)], sib_send, place.sibling)


def scatter_scratch(n, rows, columns):
    half = n // 4
    return [
        VMEM((n, rows, columns), bf16),
        VMEM((n // 2, rows, columns), bf16),
        VMEM((2, half, PIECES, rows // PIECES, columns), bf16),
        VMEM((2, half, PIECES, rows // PIECES, columns), bf16),
        DMA,
        DMA((2, half, PIECES)),
        DMA,
        DMA((n // 2,)),
    ]


def scatter(place, scratch, produce, finish):
    blocks, theirs, held, landed, ring_send, ring_recv, sib_send, sib_recv = scratch
    half, rows = place.half, blocks.shape[1]
    part = rows // PIECES

    def across(offset):
        chip = place.chip(offset)
        return remote(
            blocks.at[2 * chip + 1 - place.core], theirs.at[chip], sib_send, sib_recv.at[offset + half - 1], place.sibling
        )

    def make(offset):
        chip = place.chip(offset)
        value = produce(chip).astype(bf16)
        blocks[2 * chip] = value[:rows]
        blocks[2 * chip + 1] = value[rows:]
        across(offset).start()

    def ring(way, step, k):
        return remote(
            held.at[way, step, k], landed.at[way, step, k], ring_send, ring_recv.at[way, step, k], place.sides[way]
        )

    def mine(offset, k):
        chip, window = place.chip(offset), pl.ds(k * part, part)
        return blocks[2 * chip + place.core, window, :].astype(f32) + theirs[chip, window, :].astype(f32)

    first = [pieces_of(half, way, half - 1) for way in (0, 1)]
    make(half)
    for step in range(half):
        left = half - 1 - step
        for offset in (left, -left) if left else (0,):
            make(offset)
        yield
        across(half - step).wait_recv()
        if step:
            across(step - half).wait_recv()
        for i in range(PIECES):
            for way in (0, 1):
                k = i if way == 0 else PIECES - 1 - i
                if step == 0 and k not in first[way]:
                    continue
                offset = half if step == 0 else half - step if way == 0 else step - half
                value = mine(offset, k)
                if step >= 2 or (step == 1 and k in first[way]):
                    yield
                    ring(way, step - 1, k).wait_recv()
                    value = value + landed[way, step - 1, k].astype(f32)
                held[way, step, k] = value.astype(bf16)
                ring(way, step, k).start()
    yield
    across(0).wait_recv()
    for k in range(PIECES):
        value = mine(0, k)
        for way in (0, 1):
            yield
            ring(way, half - 1, k).wait_recv()
            value = value + landed[way, half - 1, k].astype(f32)
        finish(k, value)
    wait_sent(theirs.at[pl.ds(0, place.chips - 1)], ring_send, place.sides[0])
    wait_sent(theirs, sib_send, place.sibling)


def mark_row(marks, which):
    return jnp.concatenate([marks[i, which : which + 1, :] for i in range(marks.shape[0])], axis=1).astype(f32)


def mark_columns(marks, which):
    n = marks.shape[0]
    rows = jnp.concatenate([marks[i, which : which + 1, :].astype(f32) for i in range(n)], axis=0)
    rows = jnp.concatenate([rows, jnp.zeros((LANES - n, LANES), f32)], axis=0)
    return rows.T


def column_of(columns, first, count):
    blocks = count // LANES
    return jnp.concatenate([columns[:, first // LANES + i : first // LANES + i + 1] for i in range(blocks)], axis=0)


def gain_row(marks, which, depth):
    return jnp.concatenate(
        [marks[i, which : which + 1, :].astype(f32)[:, :depth] for i in range(marks.shape[0])], axis=1
    )


def normalise(values, gain):
    return values * lax.rsqrt(jnp.mean(values * values, axis=-1, keepdims=True) + epsilon) * gain


def tile_of(length):
    return 256 if length <= 2048 else 128


def attend_forward(causal, q_ref, k_ref, v_ref, query_column, key_row, o_ref, l_ref):
    length = q_ref.shape[0]
    tile = tile_of(length)

    def one(start, reach, column):
        rows = pl.ds(start, tile)
        scores = mm_nt(q_ref[rows, :], k_ref[:reach, :])
        keep = column == key_row[:, :reach]
        if causal:
            keep = keep & (
                lax.broadcasted_iota(jnp.int32, (tile, reach), 1)
                <= lax.broadcasted_iota(jnp.int32, (tile, reach), 0) + start
            )
        scores = jnp.where(keep, scores, negative)
        top = jnp.max(scores, axis=1, keepdims=True)
        weights = jnp.exp(scores - top)
        total = jnp.sum(weights, axis=1, keepdims=True)
        o_ref[rows, :] = mm(weights.astype(bf16), v_ref[:reach, :]) / total
        l_ref[:, rows] = jnp.broadcast_to(top + jnp.log(total), (tile, LANES)).T[:1, :]

    if tile == LANES and not causal:

        @pl.loop(0, length // tile)
        def _(i):
            lanes = lax.broadcasted_iota(jnp.int32, query_column.shape, 1)
            column = jnp.sum(jnp.where(lanes == i, query_column, 0.0), axis=1, keepdims=True)
            one(pl.multiple_of(i * tile, tile), length, column)

        return
    for start in range(0, length, tile):
        one(start, start + tile if causal else length, column_of(query_column, start, tile))
        yield


def attend_backward(
    causal, q_ref, k_ref, v_ref, g_ref, o_ref, l_ref, query_row, key_column, dq_ref, dk_sum, dv_sum
):
    length = q_ref.shape[0]
    tile = tile_of(length)
    dk_sum[...] = jnp.zeros_like(dk_sum)
    dv_sum[...] = jnp.zeros_like(dv_sum)
    for start in range(0, length, tile):
        reach = start + tile if causal else length
        rows = slice(start, start + tile)
        queries, grads = q_ref[rows, :], g_ref[rows, :]
        spread = jnp.sum(grads.astype(f32) * o_ref[rows, :], axis=1, keepdims=True)
        spread = jnp.broadcast_to(spread, (tile, LANES)).T[:1, :]
        dq = 0.0
        for begin in range(0, reach, 2048):
            part = slice(begin, min(reach, begin + 2048))
            keys = k_ref[part, :]
            count = keys.shape[0]
            scores = mm_nt(keys, queries)
            keep = column_of(key_column, begin, count) == query_row[:, rows]
            if causal:
                keep = keep & (
                    lax.broadcasted_iota(jnp.int32, (count, tile), 0) + begin
                    <= lax.broadcasted_iota(jnp.int32, (count, tile), 1) + start
                )
            probs = jnp.where(keep, jnp.exp(scores - l_ref[:, rows]), 0.0)
            dprobs = mm_nt(v_ref[part, :], grads)
            dscores = (probs * (dprobs - spread)).astype(bf16)
            dk_sum[part, :] += mm(dscores, queries)
            dv_sum[part, :] += mm(probs.astype(bf16), grads)
            dq = dq + mm_tn(dscores, keys)
        dq_ref[rows, :] = (dq * HEAD_DIM ** (-0.5)).astype(bf16)
        yield


class Stage:
    def __init__(self, body, inputs, outputs, scratch):
        self.body, self.inputs, self.outputs, self.scratch = body, inputs, outputs, scratch


def fused(name, collective_id, n, ndp, stages, arrays, wanted):
    outputs, scratch = {}, {}
    for stage in stages:
        outputs.update(stage.outputs)
        scratch.update(stage.scratch)
    inputs = [x for stage in stages for x in stage.inputs if x not in outputs]
    inputs = list(dict.fromkeys(inputs))
    for key in list(outputs):
        if key not in wanted:
            scratch[key] = VMEM(outputs[key].shape, outputs.pop(key).dtype)

    def specs(names):
        return tuple(pl.BlockSpec(memory_space=pl.ANY if x.startswith("_") else VMEM) for x in names)

    flat, slots = [], {}
    for key, value in scratch.items():
        many = isinstance(value, list)
        items = value if many else [value]
        slots[key] = (len(flat), len(items), many)
        flat += items

    def kernel(*refs):
        table = dict(zip(inputs + list(outputs), refs))
        rest = refs[len(inputs) + len(outputs) :]
        for key, (at, length, many) in slots.items():
            table[key] = rest[at : at + length] if many else rest[at]
        table["saves"] = []
        place = Place(n)
        view = types.SimpleNamespace(**table)
        behind = iter(())
        for number, stage in enumerate(stages):
            behind = stage.body(place, view, behind, number == 0)
        drain(behind)
        for copy in view.saves:
            copy.wait()

    results = pl.pallas_call(
        kernel,
        out_shape=tuple(outputs.values()),
        in_specs=specs(inputs),
        out_specs=specs(outputs),
        scratch_shapes=flat,
        compiler_params=pltpu.CompilerParams(
            collective_id=collective_id, has_side_effects=True, vmem_limit_bytes=(58 if n <= 16 else 62) * 1024 * 1024
        ),
        name=name,
    )(*[arrays[x] for x in inputs])
    arrays.update(zip(outputs, results))


def shape(*dims, kind=bf16):
    return jax.ShapeDtypeStruct(dims, kind)


def settle_columns(place, ndp, span, mine, wide, landed, sems):
    mate_send, mate_recv, own_sem, send, recv, dp_send, dp_recv = sems
    matrices, mates, width, _ = mine.shape
    groups = place.n // mates
    depth = landed.shape[2]
    group, lane = place.me // mates, lax.rem(place.me, mates)

    def swap(r):
        mate = group * mates + lax.rem(lane + r, mates)
        ref = mine.at[:, lane]
        return remote(ref, ref, mate_send.at[r - 1], mate_recv.at[r - 1], (place.dp, mate))

    def rows(device):
        return wide.at[:, pl.ds(pl.multiple_of(device * depth, depth), depth), :]

    def lanes(origin):
        return landed.at[place.dp, :, :, pl.ds(pl.multiple_of(origin * LANES, LANES), LANES)]

    def move(step):
        target = lax.rem(group + step, groups) * mates + lane
        return remote(rows(target), lanes(group), send, recv.at[step - 1], (place.dp, target))

    def peer(r):
        return (lax.rem(place.dp + r, ndp), place.me)

    def pass_on(ref, origin):
        for r in range(1, ndp):
            remote(ref, lanes(origin), dp_send.at[r - 1], dp_recv.at[r - 1], peer(r)).start()

    for r in range(1, mates):
        swap(r).start()
    yield
    for r in range(1, mates):
        swap(r).wait_recv()
    for m in range(matrices):
        wide[m] = jnp.concatenate([mine[m, i] for i in range(mates)], axis=1)
    for step in range(1, groups):
        move(step).start()
    own = pltpu.make_async_copy(rows(place.me), lanes(group), own_sem)
    own.start()
    pass_on(rows(place.me), group)
    for step in range(1, groups):
        yield
        move(step).wait_recv()
        origin = lax.rem(group + groups - step, groups)
        pass_on(lanes(origin), origin)
    yield
    own.wait()
    for r in range(1, mates):
        swap(r).wait_send()
    wait_sent(wide.at[:, pl.ds(0, (groups - 1) * depth), :], send, place.sibling)
    for r in range(1, ndp):
        wait_sent(landed.at[0], dp_send.at[r - 1], peer(r))
        wait_landed(landed.at[0], dp_recv.at[r - 1], peer(r))


def settle_columns_scratch(n, ndp, span, depth, width, matrices):
    mates = LANES // span
    groups = n // mates
    return [
        VMEM((matrices, mates, width, span), bf16),
        VMEM((matrices, width, LANES), bf16),
        VMEM((ndp, matrices, depth, width), bf16),
        DMA((mates - 1,)),
        DMA((mates - 1,)),
        DMA,
        DMA,
        DMA((groups - 1,)),
        DMA((ndp - 1,)),
        DMA((ndp - 1,)),
    ]


def settle_blocks(place, ndp, source, landed, sems):
    own_sem, send, recv, dp_send, dp_recv = sems
    n = place.n

    def move(k):
        target = lax.rem(place.me + k, n)
        return remote(source(target), landed.at[place.dp, place.me], send, recv.at[k - 1], (place.dp, target))

    def peer(r):
        return (lax.rem(place.dp + r, ndp), place.me)

    def pass_on(ref, origin):
        for r in range(1, ndp):
            remote(ref, landed.at[place.dp, origin], dp_send.at[r - 1], dp_recv.at[r - 1], peer(r)).start()

    window = 4
    for k in range(1, window):
        move(k).start()
    own = pltpu.make_async_copy(source(place.me), landed.at[place.dp, place.me], own_sem)
    own.start()
    pass_on(source(place.me), place.me)
    for k in range(1, n):
        yield
        if k + window - 1 < n:
            move(k + window - 1).start()
        move(k).wait_recv()
        origin = lax.rem(place.me + n - k, n)
        pass_on(landed.at[place.dp, origin], origin)
    yield
    own.wait()
    wait_sent(landed.at[0, pl.ds(0, n - 1)], send, place.sibling)
    for r in range(1, ndp):
        wait_sent(landed.at[0], dp_send.at[r - 1], peer(r))
        wait_landed(landed.at[0], dp_recv.at[r - 1], peer(r))


def settle_blocks_scratch(n, ndp, block, kind):
    return [VMEM((ndp, n) + block, kind), DMA, DMA, DMA((n - 1,)), DMA((ndp - 1,)), DMA((ndp - 1,))]


def settle_tips(place, ndp, source, landed, sems):
    own_sem, send, recv = sems
    n = place.n
    here = place.dp * n + place.me
    for r in range(ndp):
        for k in range(n):
            if r or k:
                target = (lax.rem(place.dp + r, ndp), lax.rem(place.me + k, n))
                remote(source(target[1]), landed.at[here], send, recv, target).start()
    own = pltpu.make_async_copy(source(place.me), landed.at[here], own_sem)
    own.start()
    yield
    own.wait()
    wait_landed(landed.at[pl.ds(0, ndp * n - 1)], recv, place.sibling)
    wait_sent(landed.at[pl.ds(0, ndp * n - 1)], send, place.sibling)


def settle_rows(place, ndp, parts, landed, sems):
    send, recv = sems
    copies, at = [], 0
    for i, part in enumerate(parts):
        window = pl.ds(at, part.shape[0])
        at += part.shape[0]
        for r in range(1, ndp):
            peer = lax.rem(place.dp + r, ndp)
            copy = remote(
                part, landed.at[place.dp, window], send.at[i, r - 1], recv.at[i, r - 1], (peer, place.me)
            )
            copy.start()
            copies.append(copy)
        landed[place.dp, window] = part[...]
    yield
    for copy in copies:
        copy.wait()


def settle_tips_scratch(n, ndp):
    return [VMEM((ndp * n, 8, LANES), f32), DMA, DMA, DMA]


def settle_rows_scratch(ndp, rows, width, parts):
    return [VMEM((ndp, rows, width), bf16), DMA((parts, ndp - 1)), DMA((parts, ndp - 1))]


def peers(place, ndp):
    return [(lax.rem(place.dp + r, ndp), place.me) for r in range(1, ndp)]


def own_part(place, values, span):
    share = HEAD_DIM // span
    part = values[:, :span]
    for i in range(1, share):
        part = jnp.where(lax.rem(place.me, share) == i, values[:, i * span : (i + 1) * span], part)
    return part


def rows_of(chip, count):
    return pl.ds(pl.multiple_of(chip * 2 * count, 2 * count), 2 * count)


def chip_rows(blocks, chip):
    _, count, width = blocks.shape
    return blocks[pl.ds(2 * chip, 2)].reshape(2 * count, width)


def piece_rows(k, count):
    part = count // PIECES
    return slice(k * part, (k + 1) * part)


def columns_task(place, span, stack, buf, first, last, sems):
    own_sem, send, recv, twin_send, twin_recv, pass_send, pass_recv = sems
    mates = LANES // span
    groups = place.n // mates
    depth = stack.shape[1]
    part = depth // 2
    group, lane = place.me // mates, lax.rem(place.me, mates)
    which = pl.ds(first, last - first)

    def lanes(target):
        return pl.ds(pl.multiple_of(target * LANES, LANES), LANES)

    def rows(device, begin, count):
        return buf.at[which, pl.ds(pl.multiple_of(device * depth + begin, part), count), :]

    def half(device, other):
        return rows(device, (1 - place.half_row if other else place.half_row) * part, part)

    def mate(r):
        return (place.dp, group * mates + lax.rem(lane + r, mates))

    def hand(source, target):
        for r in range(1, mates):
            remote(source, target, pass_send.at[r - 1], pass_recv.at[r - 1], mate(r)).start()

    def arrival(step):
        target = lax.rem(group + step, groups)
        source = stack.at[which, pl.ds(pl.multiple_of(place.half_row * part, part), part), lanes(target)]
        return remote(source, half(place.me, 0), send, recv.at[step - 1], (place.dp, target * mates + lane))

    def origin(step):
        return lax.rem(group + groups - step, groups) * mates + lane

    def twin(step):
        ref = half(origin(step), 0)
        return remote(ref, ref, twin_send, twin_recv.at[step - 1], place.twin)

    for step in range(1, groups):
        arrival(step).start()
    mine = stack.at[which, :, lanes(group)]
    own = pltpu.make_async_copy(mine, rows(place.me, 0, depth), own_sem)
    own.start()
    hand(mine, rows(place.me, 0, depth))
    for step in range(1, groups + 1):
        yield
        if step < groups:
            arrival(step).wait_recv()
            twin(step).start()
            ref = half(origin(step), 0)
            hand(ref, ref)
        if step > 1:
            twin(step - 1).wait_recv()
            ref = half(origin(step - 1), 1)
            hand(ref, ref)
    yield
    own.wait()
    sent = buf.at[which, pl.ds(0, (groups - 1) * part), :]
    wait_sent(sent, send, place.sibling)
    wait_sent(sent, twin_send, place.twin)
    for r in range(1, mates):
        passed = buf.at[which, pl.ds(0, groups * depth), :]
        wait_landed(passed, pass_recv.at[r - 1], mate(r))
        wait_sent(passed, pass_send.at[r - 1], mate(r))


def columns_scratch(n, span):
    mates = LANES // span
    groups = n // mates
    return [DMA, DMA, DMA((groups - 1,)), DMA, DMA((groups - 1,)), DMA((mates - 1,)), DMA((mates - 1,))]


def share_blocks(place, blocks, landed, sems, window=4):
    own_sem, send, recv, twin_send, twin_recv = sems
    n, part = place.n, blocks.shape[1] // 2
    rows = pl.ds(pl.multiple_of(place.half_row * part, part), part)

    def move(k):
        target = lax.rem(place.me + k, n)
        return remote(blocks.at[target, rows], landed.at[place.me, rows], send, recv.at[k - 1], (place.dp, target))

    own = pltpu.make_async_copy(blocks.at[place.me], landed.at[place.me], own_sem)
    own.start()
    for k in range(1, window):
        move(k).start()
    for k in range(1, n):
        yield
        if k + window - 1 < n:
            move(k + window - 1).start()
        move(k).wait_recv()
        ref = landed.at[lax.rem(place.me + n - k, n), rows]
        remote(ref, ref, twin_send, twin_recv, place.twin).start()
    yield
    own.wait()
    ref = landed.at[pl.ds(0, n - 1), pl.ds(0, part)]
    wait_landed(ref, twin_recv, place.twin)
    wait_sent(ref, twin_send, place.twin)
    wait_sent(ref, send, place.sibling)


def share_scratch(n):
    return [DMA, DMA, DMA((n - 1,)), DMA, DMA]


def outs_task(place, shards, full, sems):
    ring, (twin_send, twin_recv, sib_send, sib_recv) = sems[:4], sems[4:]
    mine = place.half_row
    full[mine, place.me] = jnp.where(mine == 0, shards[0][...], shards[1][...])
    order = []

    def twin(i):
        ref = full.at[mine, 2 * order[i] + place.core]
        return remote(ref, ref, twin_send, twin_recv.at[i], place.twin)

    def to_twin(chip):
        order.append(chip)
        twin(len(order) - 1).start()

    passed = 0
    for _ in gather(place, full.at[mine], ring, to_twin):
        yield
        if passed + 1 < len(order):
            twin(passed).wait_recv()
            ref = full.at[1 - mine, 2 * order[passed] + place.core]
            remote(ref, ref, sib_send, sib_recv, place.sibling).start()
            passed += 1
    while passed < place.chips:
        yield
        twin(passed).wait_recv()
        ref = full.at[1 - mine, 2 * order[passed] + place.core]
        remote(ref, ref, sib_send, sib_recv, place.sibling).start()
        passed += 1
    yield
    every = full.at[0, pl.ds(0, place.chips)]
    wait_landed(every, sib_recv, place.sibling)
    wait_sent(every, sib_send, place.sibling)
    wait_sent(every, twin_send, place.twin)


def outs_scratch(n):
    return [*gather_scratch(n), DMA, DMA((n // 2,)), DMA, DMA]


def heads_task(place, span, o_ref, own, pairs, heads, sems):
    mate_send, mate_recv, *ring = sems
    mates = LANES // span
    rows = heads.shape[1]
    group, lane = place.me // mates, lax.rem(place.me, mates)
    for start in range(0, own.shape[0], 256):
        own[start : start + 256, :] = own_part(place, o_ref[start : start + 256, :], span).astype(bf16)

    def part(index):
        return own.at[pl.ds(pl.multiple_of(index * rows, rows), rows), :]

    def swap(r):
        other = lax.rem(lane + r, mates)
        return remote(
            part(other), pairs.at[lane], mate_send.at[r - 1], mate_recv.at[r - 1], (place.dp, group * mates + other)
        )

    for r in range(1, mates):
        swap(r).start()
    pairs[lane] = part(lane)[...]
    yield
    for r in range(1, mates):
        swap(r).wait_recv()
    heads[place.me] = jnp.concatenate([pairs[i] for i in range(mates)], axis=1)
    yield from gather(place, heads, ring)
    for r in range(1, mates):
        swap(r).wait_send()


def heads_scratch(n, span, length):
    mates = LANES // span
    return [
        VMEM((length, span), bf16),
        VMEM((mates, length // mates, span), bf16),
        VMEM((n, length // mates, LANES), bf16),
        DMA((mates - 1,)),
        DMA((mates - 1,)),
        *gather_scratch(n),
    ]


def heads_at(heads, mates, lane, start, count):
    return jnp.concatenate([heads[at + lane, pl.ds(start, count), :] for at in range(0, heads.shape[0], mates)], axis=1)


def own_heads(place, heads, mates, count):
    blocks = heads.shape[1] // count
    start = pl.multiple_of(lax.rem(place.me, blocks) * count, count)
    return heads_at(heads, mates, place.me // blocks, start, count)


def join_columns(place, span, mine, wide, theirs, landed, sems):
    mate_send, mate_recv, swap_send, swap_recv, own_sem, send, recv, twin_send, twin_recv = sems
    matrices, mates, _, _ = mine.shape
    groups = place.n // mates
    group, lane = place.me // mates, lax.rem(place.me, mates)
    half = place.half_row

    def swap(r):
        mate = group * mates + lax.rem(lane + r, mates)
        ref = mine.at[:, lane]
        return remote(ref, ref, mate_send.at[r - 1], mate_recv.at[r - 1], (place.dp, mate))

    def lanes(origin):
        return landed.at[:, half, :, pl.ds(pl.multiple_of(origin * LANES, LANES), LANES)]

    def move(step):
        target = lax.rem(group + step, groups) * mates + lane
        return remote(theirs.at[:, target], lanes(group), send, recv.at[step - 1], (place.dp, target))

    def pass_on(ref, origin):
        remote(ref, lanes(origin), twin_send, twin_recv, place.twin).start()

    for r in range(1, mates):
        swap(r).start()
    yield
    for r in range(1, mates):
        swap(r).wait_recv()
    for m in range(matrices):
        wide[m] = jnp.concatenate([mine[m, i] for i in range(mates)], axis=1).reshape(wide.shape[1:])
    across = remote(wide.at[:, :, 1 - half], theirs, swap_send, swap_recv, place.twin)
    across.start()
    yield
    yield
    yield
    across.wait_recv()
    for m in range(matrices):
        theirs[m] = (theirs[m].astype(f32) + wide[m, :, half].astype(f32)).astype(bf16)
    for step in range(1, groups):
        move(step).start()
    own = pltpu.make_async_copy(theirs.at[:, place.me], lanes(group), own_sem)
    own.start()
    pass_on(theirs.at[:, place.me], group)
    for step in range(1, groups):
        yield
        move(step).wait_recv()
        origin = lax.rem(group + groups - step, groups)
        pass_on(lanes(origin), origin)
    yield
    own.wait()
    across.wait_send()
    for r in range(1, mates):
        swap(r).wait_send()
    wait_sent(theirs.at[:, pl.ds(0, groups - 1)], send, place.sibling)
    wait_sent(landed.at[:, 0], twin_send, place.twin)
    wait_landed(landed.at[:, 0], twin_recv, place.twin)


def join_columns_scratch(n, span, depth, width, matrices):
    mates = LANES // span
    groups = n // mates
    return [
        VMEM((matrices, mates, width, span), bf16),
        VMEM((matrices, n, 2, depth // 2, LANES), bf16),
        VMEM((matrices, n, depth // 2, LANES), bf16),
        VMEM((matrices, 2, depth // 2, width), bf16),
        DMA((mates - 1,)),
        DMA((mates - 1,)),
        DMA, DMA, DMA, DMA,
        DMA((groups - 1,)),
        DMA, DMA,
    ]


def join_blocks(place, blocks, theirs, landed, sems, window=4):
    swap_send, swap_recv, own_sem, send, recv, twin_send, twin_recv = sems
    n, half = place.n, place.half_row

    def move(k):
        target = lax.rem(place.me + k, n)
        return remote(theirs.at[target], landed.at[place.me, half], send, recv.at[k - 1], (place.dp, target))

    def pass_on(ref, origin):
        remote(ref, landed.at[origin, half], twin_send, twin_recv, place.twin).start()

    across = remote(blocks.at[:, 1 - half], theirs, swap_send, swap_recv, place.twin)
    across.start()
    for _ in range(5):
        yield
    across.wait_recv()
    for device in range(n):
        theirs[device] = (theirs[device].astype(f32) + blocks[device, half].astype(f32)).astype(bf16)
    for k in range(1, window):
        move(k).start()
    own = pltpu.make_async_copy(theirs.at[place.me], landed.at[place.me, half], own_sem)
    own.start()
    pass_on(theirs.at[place.me], place.me)
    for k in range(1, n):
        yield
        if k + window - 1 < n:
            move(k + window - 1).start()
        move(k).wait_recv()
        origin = lax.rem(place.me + n - k, n)
        pass_on(landed.at[origin, half], origin)
    yield
    own.wait()
    across.wait_send()
    wait_sent(theirs.at[pl.ds(0, n - 1)], send, place.sibling)
    wait_sent(landed.at[:, 0], twin_send, place.twin)
    wait_landed(landed.at[:, 0], twin_recv, place.twin)


def join_blocks_scratch(n, part, columns):
    return [
        VMEM((n, part, columns), bf16), VMEM((n, 2, part, columns), bf16),
        DMA, DMA, DMA, DMA, DMA((n - 1,)), DMA, DMA,
    ]


def columns_home(n, ndp, span, depth, width, matrices):
    if ndp == 2:
        return join_columns_scratch(n, span, depth, width, matrices), shape(1, matrices, 2, depth // 2, width)
    return settle_columns_scratch(n, ndp, span, depth, width, matrices), shape(ndp, matrices, depth, width)


def columns_to_owners(place, ndp, span, scratch, out, sem, saves):
    if ndp == 2:
        mine, wide, theirs, landed, *sems = scratch
        yield from join_columns(place, span, mine, wide, theirs, landed, sems)
        saves.append(pltpu.make_async_copy(landed, out.at[0], sem))
    else:
        mine, wide, landed, *sems = scratch
        yield from settle_columns(place, ndp, span, mine, wide, landed, sems)
        saves.append(pltpu.make_async_copy(landed, out, sem))
    saves[-1].start()


def blocks_home(n, ndp, depth, columns):
    if ndp == 2:
        return join_blocks_scratch(n, depth // 2, columns), shape(1, n, 2, depth // 2, columns)
    return settle_blocks_scratch(n, ndp, (2, depth // 2, columns), bf16), shape(ndp, n, 2, depth // 2, columns)


def blocks_to_owners(place, ndp, blocks, scratch, out, sem, saves):
    if ndp == 2:
        theirs, landed, *sems = scratch
        yield from join_blocks(place, blocks, theirs, landed, sems)
        saves.append(pltpu.make_async_copy(landed, out.at[0], sem))
    else:
        landed, *sems = scratch
        yield from settle_blocks(place, ndp, lambda device: blocks.at[device], landed, sems)
        saves.append(pltpu.make_async_copy(landed, out, sem))
    saves[-1].start()


def roomy_at(n):
    return n <= 16


def open_stage(n, ndp, span, depth, count, width, slim):
    length = n * count
    roomy = roomy_at(n)
    mates = LANES // span

    def body(place, v, behind, first):
        v.x_all[place.me] = v.x[...]
        v.encoded[place.me] = v.enc[...]
        for i, ref in enumerate((v.wq, v.wk, v.wv, v.wcq, v.wck, v.wcv)):
            v.stack[i] = ref[...]
        segment = v.dec_seg[...].astype(f32)
        rows = [segment, jnp.where(v.dec_valid[...] == 1, segment, -1.0)]
        rows.append(jnp.where(v.enc_valid[...] == 1, v.enc_seg[...].astype(f32), -1.0))
        for ref in (v.gain_self, v.gain_cross, v.gain_feed):
            rows.append(jnp.concatenate([ref[...].astype(f32), jnp.zeros((1, LANES - depth), f32)], axis=1))
        rows.append(jnp.zeros((10, LANES), f32))
        v.mark[...] = jnp.concatenate(rows, axis=0).astype(bf16)
        v.marks_in[place.me] = v.mark[...]
        if first:
            greet(place.others() + peers(place, ndp))
        for other in place.others():
            remote(v.mark, v.marks_in.at[place.me], v.mark_send, v.mark_recv, other).start()
        side = lax.rem(place.me, mates) // (HEAD_DIM // span)

        def head(index):
            pair = v.buf[index]
            return jnp.where(side == 0, pair[:, :HEAD_DIM], pair[:, HEAD_DIM:])

        scale = HEAD_DIM ** (-0.5)
        gain, ready, waiting = [], [], []

        def begin(chip):
            if not ready:
                waiting.append(chip)
                return
            for b in (0, 1):
                v.normed_a[2 * chip + b] = normalise(v.x_all[2 * chip + b].astype(f32), gain[0]).astype(bf16)
            rows = rows_of(chip, count)
            qkv = mm(chip_rows(v.normed_a, chip), v.w_self[...])
            v.q1[rows, :] = (qkv[:, :HEAD_DIM].astype(bf16).astype(f32) * scale).astype(bf16)
            v.k1[rows, :] = qkv[:, HEAD_DIM : 2 * HEAD_DIM].astype(bf16)
            v.v1[rows, :] = qkv[:, 2 * HEAD_DIM :].astype(bf16)

        def cross(chip):
            if len(ready) < 2:
                waiting.append(chip)
                return
            rows = rows_of(chip, count)
            kv = mm(chip_rows(v.encoded, chip), v.w_ckv[...])
            v.k2[rows, :] = kv[:, :HEAD_DIM].astype(bf16)
            v.v2[rows, :] = kv[:, HEAD_DIM:].astype(bf16)

        def background():
            weights = columns_task(place, span, v.stack, v.buf, 4, 6, v.late)
            next(weights)
            for _ in gather(place, v.encoded, v.ring_enc, cross):
                yield
                if len(ready) < 2 and next(weights, "done") == "done":
                    v.w_ckv[...] = jnp.concatenate([head(4), head(5)], axis=1)
                    v.w_ckv_own[...] = jnp.concatenate([own_part(place, head(i), span) for i in (4, 5)], axis=1)
                    ready.append(True)
                    for chip in waiting:
                        cross(chip)
            v.saves.append(pltpu.make_async_copy(v.encoded, v._encoded, v.open_out.at[1]))
            v.saves[-1].start()

        def outs():
            yield from outs_task(place, (v.out_self, v.out_cross), v.outs_all, v.outs_in)
            v.saves.append(pltpu.make_async_copy(v.outs_all, v._outs_all, v.open_out.at[2]))
            v.saves[-1].start()

        weights = columns_task(place, span, v.stack, v.buf, 0, 4, v.early)
        next(weights)
        ring = gather(place, v.x_all, v.ring_x, begin)
        v.outs_task = outs()
        behind = one_by_one(behind, v.outs_task, background())
        for number, _ in enumerate(ring):
            if not ready and next(weights, "done") == "done":
                ref = v.marks_in.at[pl.ds(0, n - 1)]
                wait_landed(ref, v.mark_recv, place.sibling)
                wait_sent(ref, v.mark_send, place.sibling)
                v.marks[...] = v.marks_in[...]
                gain.append(gain_row(v.marks, 3, depth))
                v.w_self[...] = jnp.concatenate([head(0), head(1), head(2)], axis=1)
                v.w_self_own[...] = jnp.concatenate([own_part(place, head(i), span) for i in range(3)], axis=1)
                v.w_cq[...] = head(3)
                ready.append(True)
                for chip in waiting:
                    begin(chip)
                waiting.clear()
            elif ready and number % 2:
                next(behind, None)
        v.saves.append(pltpu.make_async_copy(v.normed_a, v._normed_one, v.open_out.at[0]))
        v.saves[-1].start()
        if not roomy:
            v.saves.append(pltpu.make_async_copy(v.x_all, v._x_all, v.open_out.at[3]))
            v.saves[-1].start()
        column, row = mark_columns(v.marks, 0), mark_row(v.marks, 1)
        beside(attend_forward(True, v.q1, v.k1, v.v1, column, row, v.o1, v.l1), behind)
        return behind

    head = shape(length, HEAD_DIM)
    gathered = shape(n, count, width)
    return Stage(
        body,
        ["x", "enc", "wq", "wk", "wv", "wcq", "wck", "wcv", "dec_seg", "dec_valid", "enc_seg", "enc_valid"]
        + ["gain_self", "gain_cross", "gain_feed", "out_self", "out_cross"],
        dict(
            **({} if roomy else dict(_x_all=gathered)),
            _outs_all=shape(2, n, depth, width), _normed_one=gathered, _encoded=gathered, q1=head, k1=head, v1=head, o1=shape(length, HEAD_DIM, kind=f32),
            l1=shape(1, length, kind=f32), k2=head, v2=head, w_self_own=shape(width, 3 * span),
            w_cq=shape(width, HEAD_DIM), w_ckv_own=shape(width, 2 * span), marks=shape(n, 16, LANES),
        ),
        dict(
            x_all=VMEM((n, count, width), bf16), normed_a=VMEM((n, count, width), bf16),
            encoded=VMEM((n, count, width), bf16), stack=VMEM((6, depth, width), bf16), buf=VMEM((6, width, LANES), bf16),
            w_self=VMEM((width, 3 * HEAD_DIM), bf16), w_ckv=VMEM((width, 2 * HEAD_DIM), bf16), mark=VMEM((16, LANES), bf16),
            marks_in=VMEM((n, 16, LANES), bf16), mark_send=DMA, mark_recv=DMA, open_out=DMA((4,)),
            outs_all=VMEM((2, n, depth, width), bf16), outs_in=outs_scratch(n),
            ring_x=gather_scratch(n), ring_enc=gather_scratch(n), early=columns_scratch(n, span),
            late=columns_scratch(n, span),
        ),
    )


def cross_stage(n, ndp, span, depth, count, width, slim):
    length = n * count
    roomy = roomy_at(n)
    mates = LANES // span

    def body(place, v, behind, first):
        kept = jnp.broadcast_to(v.dec_valid[...].astype(f32), (LANES, LANES)).T[:, :1]
        v.low_a[place.me] = (v.cotangent[...].astype(f32) * kept).astype(bf16)
        gain = gain_row(v.marks, 4, depth)
        if first:
            loads = [
                pltpu.make_async_copy(v._x_all, v.x_all, v.cross_load.at[0]),
                pltpu.make_async_copy(v._outs_all, v.outs_all, v.cross_load.at[1]),
            ]
            for load in loads:
                load.start()
            greet(place.others() + peers(place, ndp))
            for load in loads:
                load.wait()
        own, pairs, heads, *head_sems = v.heads_a

        blocks = n // 2 // mates

        def project(chip):
            step, rows = 2 * count, rows_of(chip, count)
            weight = v.outs_all[0].reshape(width, width)
            start = pl.multiple_of(lax.rem(chip, blocks) * step, step)
            value = mm(heads_at(heads, mates, chip // blocks, start, step), weight)
            value = value + chip_rows(v.x_all, chip).astype(f32)
            normed = normalise(value, gain).astype(bf16)
            value = value.astype(bf16)
            for b in (0, 1):
                v.x_all[2 * chip + b] = value[b * count : (b + 1) * count]
                v.normed_b[2 * chip + b] = normed[b * count : (b + 1) * count]
            query = mm(normed, v.w_cq[...]).astype(bf16)
            v.q2[rows, :] = (query.astype(f32) * HEAD_DIM ** (-0.5)).astype(bf16)

        def project_each():
            for chip in range(n // 2):
                project(jnp.int32(chip))
                yield

        def weights():
            for device in range(n):
                columns = slice(device * slim, (device + 1) * slim)
                both = [ref[:, columns].astype(f32) for ref in (v.gate, v.up)]
                v.targets[device] = jnp.concatenate(both, axis=1).astype(bf16)
            yield
            yield from share_blocks(place, v.targets, v.w_feed_in, v.feed_in)
            v.saves.append(pltpu.make_async_copy(v.w_feed_in, v._w_feed, v.cross_out.at[2]))
            v.saves[-1].start()

        def lows():
            yield from gather(place, v.low_a, v.ring_low)
            v.saves.append(pltpu.make_async_copy(v.low_a, v._low_all, v.cross_out.at[1]))
            v.saves[-1].start()

        behind = in_turn(behind, weights(), lows())
        beside(heads_task(place, span, v.o1, own, pairs, heads, head_sems), behind)
        if not first:
            drain(v.outs_task)
        v.resid_one[...] = mm(own_heads(place, heads, mates, count), v.outs_all[0].reshape(width, width))
        v.resid_one[...] += v.x[...].astype(f32)
        if first:
            pl.loop(0, n // 2)(project)
        else:
            beside(project_each(), behind, 3)
        for i, (source, target) in enumerate(((v.normed_b, v._normed_two), (v.x_all, v._resid_all))):
            v.saves.append(pltpu.make_async_copy(source, target, v.cross_out.at[3 * i]))
            v.saves[-1].start()
        column, row = mark_columns(v.marks, 0), mark_row(v.marks, 2)
        if first:
            beside(attend_forward(False, v.q2, v.k2, v.v2, column, row, v.o2, v.l2), behind, 3)
        else:
            drain(behind)
            drain(attend_forward(False, v.q2, v.k2, v.v2, column, row, v.o2, v.l2))
        return behind

    gathered = shape(n, count, width)
    return Stage(
        body,
        ["o1", "x", "marks", "w_cq", "k2", "v2", "cotangent", "dec_valid", "gate", "up"]
        + ([] if roomy else ["_x_all", "_outs_all"]),
        dict(
            resid_one=shape(count, width, kind=f32), _normed_two=gathered, _low_all=gathered, _resid_all=gathered, q2=shape(length, HEAD_DIM),
            o2=shape(length, HEAD_DIM, kind=f32), l2=shape(1, length, kind=f32), _w_feed=shape(n, depth, 2 * slim),
        ),
        dict(
            normed_b=VMEM((n, count, width), bf16), low_a=VMEM((n, count, width), bf16),
            targets=VMEM((n, depth, 2 * slim), bf16), w_feed_in=VMEM((n, depth, 2 * slim), bf16), cross_out=DMA((4,)),
            cross_load=DMA((2,)), x_all=VMEM((n, count, width), bf16), outs_all=VMEM((2, n, depth, width), bf16),
            ring_low=gather_scratch(n), heads_a=heads_scratch(n, span, length), feed_in=share_scratch(n),
        ),
    )


def norm_back(values, gain, grad):
    r = lax.rsqrt(jnp.mean(values * values, axis=-1, keepdims=True) + epsilon)
    scaled = grad * gain
    inner = jnp.mean(values * scaled, axis=-1, keepdims=True)
    return r * scaled - values * (r * r * r * inner), grad * values * r


def gelu_pair(v):
    c = 0.7978845608028654
    square = v * v
    t = jnp.tanh(c * v * (1.0 + 0.044715 * square))
    value = 0.5 * v * (1.0 + t)
    slope = 0.5 * (1.0 + t) + 0.5 * c * v * (1.0 - t * t) * (1.0 + 3.0 * 0.044715 * square)
    return value, slope


def feed_stage(n, ndp, span, depth, count, width, slim):
    length = n * count
    mates = LANES // span

    def body(place, v, behind, first):
        loads = [
            pltpu.make_async_copy(v._low_all, v.low_b, v.feed_load.at[0]),
            pltpu.make_async_copy(v._w_feed, v.w_feed, v.feed_load.at[1]),
            pltpu.make_async_copy(v._resid_all, v.normed_c, v.feed_load.at[2]),
            pltpu.make_async_copy(v._outs_all.at[1], v.out_cross_all, v.feed_load.at[3]),
        ]
        for load in loads:
            load.start()
        gain = gain_row(v.marks, 5, depth)
        if first:
            greet(place.others() + peers(place, ndp))

        own, pairs, heads, *head_sems = v.heads_c

        weight = v.out_cross_all
        blocks = n // 2 // mates
        made = []

        def feed(chip):
            made.append(chip)
            step, rows = 2 * count, rows_of(chip, count)
            start = pl.multiple_of(lax.rem(chip, blocks) * step, step)
            value = mm(heads_at(heads, mates, chip // blocks, start, step), weight[...].reshape(width, width))
            value = value + chip_rows(v.normed_c, chip).astype(f32)
            block = normalise(value, gain).astype(bf16)
            for b in (0, 1):
                v.normed_c[2 * chip + b] = block[b * count : (b + 1) * count]
            both = mm(block, v.w_feed[...].reshape(width, 2 * slim))
            gate, upward = both[:, :slim], both[:, slim:]
            value, slope = gelu_pair(gate)
            grad = mm_nt(chip_rows(v.low_b, chip), v.down[...])
            v.hidden[rows, :] = (value * upward).astype(bf16)
            both = jnp.concatenate([grad * upward * slope, grad * value], axis=1).astype(bf16)
            v.d_both[rows, :] = both
            return both

        def produce_back(chip):
            return mm_nt(feed(chip), v.w_feed[...].reshape(width, 2 * slim))

        def finish_back(k, value):
            rows = piece_rows(k, count)
            grad, part = norm_back(v.resid_two[rows, :], gain, value)
            v.grad_two[rows, :] = v.low_b[place.me, rows, :].astype(f32) + grad
            part = jnp.sum(part, axis=0, keepdims=True)
            v.tip_three[...] = part if k == 0 else v.tip_three[...] + part

        def weight_grads():
            step = 256
            while len(made) < n // 2:
                yield
            for start in range(0, width, step):
                columns = slice(start, start + step)
                left = v.normed_c[:, :, columns].reshape(length, step)
                value = mm_tn(left, v.d_both[...]).astype(bf16)
                v.feed_grad[start // depth : (start + step) // depth] = value.reshape(step // depth, 2, depth // 2, 2 * slim)
                yield
                left = v.low_b[:, :, columns].reshape(length, step)
                v.down_grad[:, columns] = mm_tn(v.hidden[...], left).astype(bf16)
                yield

        beside(heads_task(place, span, v.o2, own, pairs, heads, head_sems), behind)
        for load in loads:
            load.wait()
        v.resid_two[...] = mm(own_heads(place, heads, mates, count), weight[...].reshape(width, width)) + v.resid_one[...]
        grads = weight_grads()
        beside(scatter(place, v.sums_c, produce_back, finish_back), in_turn(behind, grads))
        drain(grads)
        return behind

    return Stage(
        body,
        ["o2", "resid_one", "marks", "_w_feed", "down", "_low_all", "_resid_all", "_outs_all"],
        dict(
            resid_two=shape(count, width, kind=f32), grad_two=shape(count, width, kind=f32),
            tip_three=shape(1, width, kind=f32), hidden=shape(length, slim), feed_grad=shape(n, 2, depth // 2, 2 * slim),
            down_grad=shape(slim, width),
        ),
        dict(
            normed_c=VMEM((n, count, width), bf16), low_b=VMEM((n, count, width), bf16),
            w_feed=VMEM((n, depth, 2 * slim), bf16), d_both=VMEM((length, 2 * slim), bf16), feed_load=DMA((4,)),
            out_cross_all=VMEM((n, depth, width), bf16), heads_c=heads_scratch(n, span, length), sums_c=scatter_scratch(n, count, width),
        ),
    )


def own_grads(place, span, sources, target):
    step = 256
    for start in range(0, target.shape[0], step):
        rows = slice(start, start + step)
        parts = [own_part(place, source[rows, :].astype(bf16), span) for source in sources]
        target[rows, :] = jnp.concatenate(parts, axis=1)


def cross_back_stage(n, ndp, span, depth, count, width, slim):
    length = n * count

    def body(place, v, behind, first):
        v.low_c[place.me] = v.grad_two[...].astype(bf16)
        v.out_sum_c[...] = jnp.zeros_like(v.out_sum_c)
        if first:
            greet(place.others() + peers(place, ndp))

        def into(chip):
            block, rows = chip_rows(v.low_c, chip), rows_of(chip, count)
            v.d_attn_c[rows, :] = mm_nt(block, v.out_cross_head[...]).astype(bf16)
            v.out_sum_c[...] += mm_tn(own_part(place, v.o2[rows, :], span).astype(bf16), block)

        def produce(chip):
            return mm(v.hidden[rows_of(chip, count), :], v.down[...])

        def finish(k, value):
            rows = piece_rows(k, count)
            v.mixed[rows, :] = (v.resid_two[rows, :] + value).astype(bf16)

        downs, *down_sems = v.down_back
        behind = in_turn(
            behind,
            blocks_to_owners(place, ndp, v.feed_grad, v.feed_back, v._feeds, v.back_out.at[0], v.saves),
            settle_rows(place, ndp, (v.down_grad,), downs, down_sems),
        )
        beside(gather(place, v.low_c, v.ring_d, into), behind, 1, 2)
        behind = in_turn(behind, scatter(place, v.sums_c, produce, finish))
        row, column = mark_row(v.marks, 0), mark_columns(v.marks, 2)
        attention = attend_backward(
            False, v.q2, v.k2, v.v2, v.d_attn_c, v.o2, v.l2, row, column, v.d_attn_c, v.dk_c, v.dv_c
        )
        beside(attention, behind, 3)
        drain(behind)
        v.saves.append(pltpu.make_async_copy(downs, v._downs, v.back_out.at[1]))
        v.saves[-1].start()
        own_grads(place, span, (v.d_attn_c,), v.dq2)
        own_grads(place, span, (v.dk_c, v.dv_c), v.dkv2)
        v.out_two[...] = v.out_sum_c[...].astype(bf16)
        return iter(())

    return Stage(
        body,
        ["grad_two", "out_cross_head", "o2", "l2", "q2", "k2", "v2", "marks", "hidden", "down", "resid_two", "feed_grad"]
        + ["down_grad"],
        dict(
            dq2=shape(length, span), dkv2=shape(length, 2 * span), out_two=shape(span, width), mixed=shape(count, width),
            _feeds=blocks_home(n, ndp, depth, 2 * slim)[1], _downs=shape(ndp, slim, width),
        ),
        dict(
            low_c=VMEM((n, count, width), bf16), d_attn_c=VMEM((length, HEAD_DIM), bf16),
            dk_c=VMEM((length, HEAD_DIM), f32), dv_c=VMEM((length, HEAD_DIM), f32),
            out_sum_c=VMEM((span, width), f32), back_out=DMA((2,)), ring_d=gather_scratch(n),
            sums_c=scatter_scratch(n, count, width), feed_back=blocks_home(n, ndp, depth, 2 * slim)[0],
            down_back=settle_rows_scratch(ndp, slim, width, 1),
        ),
    )


def self_back_stage(n, ndp, span, depth, count, width, slim):
    length = n * count
    roomy = roomy_at(n)

    def body(place, v, behind, first):
        lane = lax.rem(place.me, LANES // span)
        mine = v.columns_e[0]
        outs, *out_sems = v.outs_e
        loads = [
            pltpu.make_async_copy(ref, v.saved, v.self_load.at[i]) for i, ref in enumerate((v._normed_two, v._encoded))
        ]
        loads[0].start()
        gain = gain_row(v.marks, 4, depth)
        v.out_sum_e[...] = jnp.zeros_like(v.out_sum_e)
        v.w_cq_own[...] = own_part(place, v.w_cq[...], span)
        if first:
            greet(place.others() + peers(place, ndp))

        def produce(chip):
            return mm_nt(v.dq2[rows_of(chip, count), :], v.w_cq_own[...])

        def finish(k, value):
            rows = piece_rows(k, count)
            grad, part = norm_back(v.resid_one[rows, :], gain, value)
            grad = v.grad_two[rows, :] + grad
            v.grad_one[rows, :] = grad
            v.low_e[place.me, rows, :] = grad.astype(bf16)
            part = jnp.sum(part, axis=0, keepdims=True)
            v.tip_two[...] = part if k == 0 else v.tip_two[...] + part

        def weight_grads():
            step = 256
            loads[0].wait()
            for start in range(0, width, step):
                columns = slice(start, start + step)
                left = v.saved[:, :, columns].reshape(length, step)
                mine[0, lane, columns, :] = mm_tn(left, v.dq2[...]).astype(bf16)
                yield
            loads[1].start()
            yield
            loads[1].wait()
            for start in range(0, width, step):
                columns = slice(start, start + step)
                left = v.saved[:, :, columns].reshape(length, step)
                value = mm_tn(left, v.dkv2[...]).astype(bf16)
                mine[1, lane, columns, :] = value[:, :span]
                mine[2, lane, columns, :] = value[:, span:]
                yield

        def into(chip):
            block, rows = chip_rows(v.low_e, chip), rows_of(chip, count)
            v.d_attn_e[rows, :] = mm_nt(block, v.out_self_head[...]).astype(bf16)
            v.out_sum_e[...] += mm_tn(own_part(place, v.o1[rows, :], span).astype(bf16), block)

        def produce_enc(chip):
            return mm_nt(v.dkv2[rows_of(chip, count), :], v.w_ckv_own[...])

        def finish_enc(k, value):
            v.enc_grad[piece_rows(k, count), :] = value

        def rests():
            yield from settle_rows(place, ndp, (v.out_two,), outs, out_sems)
            v.saves.append(pltpu.make_async_copy(outs, v._outs_two, v.self_load.at[3]))
            v.saves[-1].start()

        grads = weight_grads()
        beside(scatter(place, v.sums_e, produce, finish), in_turn(behind, grads))
        drain(grads)
        encs = scatter(place, v.sums_f if roomy else v.sums_e, produce_enc, finish_enc)
        columns = columns_to_owners(place, ndp, span, v.columns_e, v._columns_two, v.self_load.at[2], v.saves)
        behind = in_turn(behind, columns, rests(), *([encs] if roomy else []))
        beside(gather(place, v.low_e, v.ring_e, into), behind, 1, 3)
        if not roomy:
            behind = in_turn(behind, encs)
        row, column = mark_row(v.marks, 0), mark_columns(v.marks, 1)
        attention = attend_backward(
            True, v.q1, v.k1, v.v1, v.d_attn_e, v.o1, v.l1, row, column, v.d_attn_e, v.dk_e, v.dv_e
        )
        beside(attention, behind, 2)
        own_grads(place, span, (v.d_attn_e, v.dk_e, v.dv_e), v.grads_one)
        v.out_one[...] = v.out_sum_e[...].astype(bf16)
        return behind

    rows = shape(count, width, kind=f32)
    return Stage(
        body,
        ["dq2", "dkv2", "w_cq", "w_ckv_own", "resid_one", "grad_two", "marks", "out_self_head", "o1", "l1", "q1", "k1", "v1"]
        + ["out_two", "_normed_two", "_encoded"],
        dict(
            grads_one=shape(length, 3 * span), out_one=shape(span, width), grad_one=rows, enc_grad=rows,
            tip_two=shape(1, width, kind=f32), _columns_two=columns_home(n, ndp, span, depth, width, 3)[1], _outs_two=shape(ndp, span, width),
        ),
        dict(
            saved=VMEM((n, count, width), bf16), low_e=VMEM((n, count, width), bf16),
            d_attn_e=VMEM((length, HEAD_DIM), bf16),
            dk_e=VMEM((length, HEAD_DIM), f32), dv_e=VMEM((length, HEAD_DIM), f32), out_sum_e=VMEM((span, width), f32),
            w_cq_own=VMEM((width, span), bf16), self_load=DMA((4,)), ring_e=gather_scratch(n),
            sums_e=scatter_scratch(n, count, width),
            columns_e=columns_home(n, ndp, span, depth, width, 3)[0], outs_e=settle_rows_scratch(ndp, span, width, 1),
            **(dict(sums_f=scatter_scratch(n, count, width)) if roomy else {}),
        ),
    )


def close_stage(n, ndp, span, depth, count, width, slim):
    length = n * count
    mates = LANES // span

    def body(place, v, behind, first):
        lane = lax.rem(place.me, mates)
        mine = v.columns_g[0]
        outs, *out_sems = v.outs_g
        tips, *tip_sems = v.tips_g
        load = pltpu.make_async_copy(v._normed_one, v.saved, v.close_load.at[0])
        load.start()
        gain = gain_row(v.marks, 3, depth)
        v.tip_all[...] = jnp.zeros_like(v.tip_all)
        v.tip_all[1:2, :] = v.tip_two[...]
        v.tip_all[2:3, :] = v.tip_three[...]
        if first:
            greet(place.others() + peers(place, ndp))

        def produce(chip):
            return mm_nt(v.grads_one[rows_of(chip, count), :], v.w_self_own[...])

        def finish(k, value):
            rows = piece_rows(k, count)
            grad, part = norm_back(v.x[rows, :].astype(f32), gain, value)
            v.dec_grad[rows, :] = v.grad_one[rows, :] + grad
            v.tip_all[0:1, :] += jnp.sum(part, axis=0, keepdims=True)

        def columns():
            load.wait()
            step = 256
            for start in range(0, width, step):
                columns = slice(start, start + step)
                value = mm_tn(v.saved[:, :, columns].reshape(length, step), v.grads_one[...]).astype(bf16)
                for i in range(3):
                    mine[i, lane, columns, :] = value[:, i * span : (i + 1) * span]
                yield
            yield from columns_to_owners(place, ndp, span, v.columns_g, v._columns_one, v.close_load.at[1], v.saves)

        def tip(device):
            return v.tip_all.at[:, pl.ds(pl.multiple_of(device // mates * LANES, LANES), LANES)]

        behind = in_turn(columns(), settle_rows(place, ndp, (v.out_one,), outs, out_sems), behind)
        beside(scatter(place, v.sums_e, produce, finish), behind)
        drain(in_turn(settle_tips(place, ndp, tip, tips, tip_sems), behind))
        for i, (source, target) in enumerate(((outs, v._outs_one), (tips, v._tips))):
            v.saves.append(pltpu.make_async_copy(source, target, v.close_load.at[i + 2]))
            v.saves[-1].start()
        return iter(())

    return Stage(
        body,
        ["grads_one", "w_self_own", "x", "grad_one", "marks", "out_one", "tip_two", "tip_three", "_normed_one"],
        dict(
            dec_grad=shape(count, width, kind=f32), _columns_one=columns_home(n, ndp, span, depth, width, 3)[1],
            _outs_one=shape(ndp, span, width), _tips=shape(ndp * n, 8, LANES, kind=f32),
        ),
        dict(
            saved=VMEM((n, count, width), bf16), tip_all=VMEM((8, width), f32), close_load=DMA((4,)),
            sums_e=scatter_scratch(n, count, width), columns_g=columns_home(n, ndp, span, depth, width, 3)[0],
            outs_g=settle_rows_scratch(ndp, span, width, 1), tips_g=settle_tips_scratch(n, ndp),
        ),
    )


def over_dp(landed, *index):
    return sum(landed[(d, *index)].astype(f32) for d in range(landed.shape[0]))


def total_kernel(
    n, span,
    *refs,
):
    sources, targets, rest = refs[:7], refs[7:19], refs[19:]
    gains_out, q_out, k_out, v_out, out_one, cq_out, ck_out, cv_out, out_two, gate_out, up_out, down_out = targets
    columns_one, columns_two, outs_one, outs_two, feeds, downs, tips = rest[:7]
    loads = [pltpu.make_async_copy(a, b, rest[7].at[i]) for i, (a, b) in enumerate(zip(sources, rest))]
    for load in loads:
        load.start()
    for load in loads:
        load.wait()
    for i, ref in enumerate((q_out, k_out, v_out)):
        ref[...] = over_dp(columns_one, i).reshape(ref.shape)
    for i, ref in enumerate((cq_out, ck_out, cv_out)):
        ref[...] = over_dp(columns_two, i).reshape(ref.shape)
    out_one[...] = over_dp(outs_one)
    out_two[...] = over_dp(outs_two)
    down_out[...] = over_dp(downs)
    slim = gate_out.shape[1] // n
    for i in range(n):
        piece = over_dp(feeds, i).reshape(gate_out.shape[0], 2 * slim)
        gate_out[:, i * slim : (i + 1) * slim] = piece[:, :slim]
        up_out[:, i * slim : (i + 1) * slim] = piece[:, slim:]
    total = over_dp(tips)
    mates = LANES // span
    lane = lax.rem(lax.axis_index("blk"), mates)
    part = total[:, :span]
    for i in range(1, mates):
        part = jnp.where(lane == i, total[:, i * span : (i + 1) * span], part)
    gains_out[...] = part


def total_grads(n, span, columns_one, columns_two, outs_one, outs_two, feeds, downs, tips):
    width = columns_one.shape[-1]
    depth = columns_one.size // columns_one.shape[0] // 3 // width
    slim = downs.shape[1]
    arrays = (columns_one, columns_two, outs_one, outs_two, feeds, downs, tips)

    square, out = shape(depth, width, kind=f32), shape(span, width, kind=f32)
    return pl.pallas_call(
        functools.partial(total_kernel, n, span),
        out_shape=(
            shape(8, span, kind=f32), square, square, square, out, square, square, square, out,
            shape(depth, n * slim, kind=f32), shape(depth, n * slim, kind=f32), shape(slim, width, kind=f32),
        ),
        in_specs=[pl.BlockSpec(memory_space=pl.ANY)] * 7,
        scratch_shapes=[VMEM(x.shape, x.dtype) for x in arrays] + [DMA((7,))],
        compiler_params=pltpu.CompilerParams(vmem_limit_bytes=56 * 1024 * 1024),
        name="total_grads",
    )(*arrays)


def local(
    n,
    ndp,
    dec_in,
    enc_out,
    cotangent,
    dec_seg,
    dec_valid,
    enc_seg,
    enc_valid,
    self_gain,
    self_query,
    self_key,
    self_value,
    self_out,
    cross_gain,
    cross_query,
    cross_key,
    cross_value,
    cross_out,
    feed_gain,
    feed_gate,
    feed_up,
    feed_down,
):
    width = dec_in.shape[2]
    depth = self_query.shape[0]
    span = width // n
    share = HEAD_DIM // span

    def whole_head(weight):
        if share == 1:
            return weight
        groups = [[h * share + i for i in range(share)] for h in range(n // share)]
        return lax.all_gather(weight, "blk", axis=0, tiled=True, axis_index_groups=groups)

    count, slim = dec_in.shape[1], feed_gate.shape[1] // n
    arrays = dict(
        x=dec_in[0], enc=enc_out[0], cotangent=cotangent[0],
        dec_seg=dec_seg, dec_valid=dec_valid, enc_seg=enc_seg, enc_valid=enc_valid,
        gain_self=self_gain[None], gain_cross=cross_gain[None], gain_feed=feed_gain[None],
        wq=self_query, wk=self_key, wv=self_value, wcq=cross_query, wck=cross_key, wcv=cross_value,
        out_self=self_out, out_cross=cross_out, gate=feed_gate, up=feed_up, down=feed_down,
        out_self_head=whole_head(self_out), out_cross_head=whole_head(cross_out),
    )
    stages = [
        (name, make(n, ndp, span, depth, count, width, slim))
        for name, make in (
            ("open", open_stage), ("cross", cross_stage), ("feed", feed_stage),
            ("cross_back", cross_back_stage), ("self_back", self_back_stage), ("close", close_stage),
        )
    ]
    size = 2 if roomy_at(n) else 1
    results = {"mixed", "dec_grad", "enc_grad", "_columns_one", "_columns_two", "_outs_one", "_outs_two"}
    results |= {"_feeds", "_downs", "_tips"}
    for at in range(0, len(stages), size):
        later = {key for _, stage in stages[at + size :] for key in stage.inputs}
        group = stages[at : at + size]
        name = "_and_".join(key for key, _ in group)
        fused(name, at, n, ndp, [stage for _, stage in group], arrays, later | results)
    gains, q, k, v, o, cq, ck, cv, co, gate, up, down = total_grads(
        n, span, *(arrays[key] for key in ("_columns_one", "_columns_two", "_outs_one", "_outs_two", "_feeds", "_downs", "_tips"))
    )
    return (
        arrays["mixed"][None], arrays["dec_grad"][None], arrays["enc_grad"][None],
        gains[0], q, k, v, o,
        gains[1], cq, ck, cv, co,
        gains[2], gate, up, down,
    )


def solution(mesh):
    row, token = P("dp", "blk"), P("dp", "blk", None)
    gain, weight = P("blk"), P("blk", None)
    return jax.shard_map(
        functools.partial(local, mesh.shape["blk"], mesh.shape["dp"]),
        mesh=mesh,
        in_specs=(token,) * 3 + (row,) * 4 + ((gain,) + (weight,) * 4) * 2 + (gain,) + (weight,) * 3,
        out_specs=(token,) * 3 + ((gain,) + (weight,) * 4) * 2 + (gain,) + (weight,) * 3,
        check_vma=False,
    )
```
